128 devices in a mesh: row: 16 (over x, y), col: 8 (over z, core).
Axes of the slice: x: 4, y: 4, z: 4, core: 2. Of those that a mesh axis runs over, the one named last changes fastest.
Arguments:
- source1: float32 [2, 64, 48, 128], P(None, 'row', 'col'), may hold values from -6 to 6
- source2: float32 [2, 64, 48, 128], P(None, 'row', 'col'), may hold values from -6 to 6
- coupling: float32 [2, 64, 48], P(None, 'row', 'col'), may hold values from -1.5 to 1.5
- factor1: float32 [2, 3072, 3072], P(None, 'row', 'col'), may hold values from -0.0546875 to 0.0546875
- factor2: float32 [2, 3072, 3072], P(None, 'row', 'col'), may hold values from -0.0546875 to 0.0546875
- diag_inv: float32 [2, 768, 3072], P(None, None, 'row'), may hold values from -0.15625 to 0.15625
- front_order: int32 [3072], replicated, may hold values from 0 to 3071, each once
Outputs:
- solution1: float32 [2, 64, 48, 128], P(None, 'row', 'col')
- forward2: float32 [2, 3072, 128], P(None, 'row')
The draws below stay inside these ranges and needn't reach their ends.
Inputs may be any that keep to these rules, and one draw needn't show every extreme that they name: `front_order`: a permutation of the patch's 3072 cells.
All inputs are finite; a program needn't handle non-finite values.
Results may differ from the reference program's by a relative error of at most 0.00012.
Values sent between devices are 32-bit elements; how exact they have to be, the bound alone decides.
No kernel may reach another device: no remote copies, remote signals or barrier semaphores. Data moves between devices by JAX's collectives and lax.ppermute only.
A program may use at most 64 MiB of HBM per device.

```python
import jax
import jax.numpy as jnp
from jax import lax

RHS = 128
BLOCKS = 4
NY = 64
NX = 48
NF = 3072
NB = 768
PIECE = 96
N_COL = 8


def shard_levels(key, shape, split, smallest, largest):
    loudness, own = 1.0, jax.random.fold_in(key, 6)
    for axis_at, shards_of in split:
        steps = jnp.exp(jax.random.uniform(jax.random.fold_in(own, axis_at), (shards_of,), jnp.float32, smallest / len(split), largest / len(split)))
        loudness = loudness * jnp.repeat(steps, shape[axis_at] // shards_of).reshape([-1 if axis == axis_at else 1 for axis in range(len(shape))])
    return loudness


def normal_values(rng, dims, scale, bound, shards=(), kind=jnp.bfloat16):
    gain = shard_levels(rng, dims, shards, -0.22, 0.18) if shards else 1.0
    drawn = jax.random.normal(rng, dims, jnp.float32) * scale * gain
    return jnp.minimum(jnp.maximum(drawn, -bound), bound).astype(kind)


def setup_inputs(seed: int = 0) -> dict:
    key_of = jax.random.split(jax.random.key(seed), 8)
    source1 = normal_values(key_of[0], (2, NY, NX, RHS), 1.0, 6.0, ((1, 16), (2, 8)), jnp.float32)
    source2 = normal_values(key_of[1], (2, NY, NX, RHS), 1.0, 6.0, ((1, 16), (2, 8)), jnp.float32)
    coupling = jnp.clip(jax.random.uniform(key_of[2], (2, NY, NX), jnp.float32, -1.5, 1.5) * shard_levels(key_of[2], (2, NY, NX), ((1, 16), (2, 8)), -0.4, 0.0), -1.5, 1.5)
    factor1 = normal_values(key_of[3], (2, NF, NF), (4 * NF) ** -0.5, 0.0546875, ((1, 16), (2, 8)), jnp.float32)
    factor2 = normal_values(key_of[4], (2, NF, NF), (4 * NF) ** -0.5, 0.0546875, ((1, 16), (2, 8)), jnp.float32)
    diag_inv = normal_values(key_of[5], (2, NB, NF), (2 * NB) ** -0.5, 0.15625, ((2, 16),), jnp.float32)
    front_order = jax.random.permutation(key_of[6], NF).astype(jnp.int32)
    return dict(source1=source1, source2=source2, coupling=coupling, factor1=factor1, factor2=factor2, diag_inv=diag_inv, front_order=front_order)


def complex_product(matrix, vector):
    highest = lax.Precision.HIGHEST
    real_part = jnp.dot(matrix[0], vector[0], precision=highest, preferred_element_type=jnp.float32) - jnp.dot(matrix[1], vector[1], precision=highest, preferred_element_type=jnp.float32)
    imag_part = jnp.dot(matrix[0], vector[1], precision=highest, preferred_element_type=jnp.float32) + jnp.dot(matrix[1], vector[0], precision=highest, preferred_element_type=jnp.float32)
    return jnp.stack([real_part, imag_part])


def front_matrix(factor):
    stored = factor.reshape(2, NF, N_COL, BLOCKS, PIECE)
    return jnp.transpose(stored, (0, 1, 3, 2, 4)).reshape(2, NF, NF)


def to_front(plane, front_order):
    flat_plane = plane.reshape(2, NY * NX, RHS)
    return flat_plane[:, front_order, :]


def forward_solve(matrix, rhs_front):
    vector = jnp.zeros_like(rhs_front)
    for current in range(BLOCKS):
        start = current * NB
        summed = complex_product(matrix[:, start:start + NB, :], vector)
        vector = vector.at[:, start:start + NB, :].set(rhs_front[:, start:start + NB, :] - summed)
    return vector


def backward_solve(matrix, inverse, rhs_front):
    vector = jnp.zeros_like(rhs_front)
    for current in range(BLOCKS - 1, -1, -1):
        start = current * NB
        summed = complex_product(matrix[:, start:start + NB, :], vector)
        solved = complex_product(inverse[:, :, start:start + NB], rhs_front[:, start:start + NB, :] - summed)
        vector = vector.at[:, start:start + NB, :].set(solved)
    return vector


def reference(source1, source2, coupling, factor1, factor2, diag_inv, front_order):
    b_first = to_front(source1, front_order)
    matrix_one = front_matrix(factor1)
    y_first = forward_solve(matrix_one, b_first)
    x_first = backward_solve(matrix_one, diag_inv, y_first)
    slots = jnp.zeros((NF,), jnp.int32).at[front_order].set(jnp.arange(NF, dtype=jnp.int32))
    solution1 = x_first[:, slots, :].reshape(2, NY, NX, RHS)
    link_real = coupling[0][:, :, None]
    link_imag = coupling[1][:, :, None]
    next_real = source2[0] - (link_real * solution1[0] - link_imag * solution1[1])
    next_imag = source2[1] - (link_real * solution1[1] + link_imag * solution1[0])
    next_rhs = jnp.stack([next_real, next_imag])
    b_second = to_front(next_rhs, front_order)
    forward2 = forward_solve(front_matrix(factor2), b_second)
    return solution1, forward2
```

```python
import functools

import jax
import jax.numpy as jnp
from jax import lax
from jax.experimental import pallas as pl
from jax.experimental.pallas import tpu as pltpu
from jax.sharding import PartitionSpec as P

GROUP = 4
CHUNK = 16
ROWS = 2 * CHUNK
SLAB = 192
BLOCK = 768
PIECE = 96
CELLS = 24
VMEM = 40 * 1024 * 1024

SDS = jax.ShapeDtypeStruct
f32 = jnp.float32


def split(value):
    high = value.astype(jnp.bfloat16)
    return high, (value - high.astype(f32)).astype(jnp.bfloat16)


def complex_dot(vector, weight):
    half = weight.shape[1] // 2
    weight_high, weight_low = split(weight)
    high, low = split(vector)
    both = jnp.dot(
        jnp.concatenate([high, low], axis=0), weight_high, preferred_element_type=f32
    )
    total = both[:ROWS] + both[ROWS:] + jnp.dot(high, weight_low, preferred_element_type=f32)
    real = total[:CHUNK, :half] - total[CHUNK:, half:]
    imag = total[:CHUNK, half:] + total[CHUNK:, :half]
    return jnp.concatenate([real, imag], axis=0)


def block_weight(ref, at=0):
    return ref[:, at].reshape(BLOCK, 2 * SLAB)


def slabs_dot(refs, weight_ref, q, keep=None):
    total = None
    for d, ref in enumerate(refs):
        source = lax.rem(q - d + GROUP, GROUP)
        slab = ref[...]
        if keep is not None:
            keep[source] = slab
        weight = weight_ref[pl.ds(2 * source, 2), 0].reshape(SLAB, 2 * SLAB)
        part = complex_dot(slab, weight)
        total = part if total is None else total + part
    return total


def add_refs(refs):
    total = refs[0][...]
    for ref in refs[1:]:
        total = total + ref[...]
    return total


def call(body, out_shape, inputs, blocks=None, scratch=()):
    blocks = blocks or {}
    specs = []
    for at, value in enumerate(inputs):
        if at in blocks:
            specs.append(blocks[at])
        elif value.dtype == jnp.int32:
            specs.append(pl.BlockSpec(memory_space=pltpu.SMEM))
        else:
            specs.append(pl.BlockSpec(value.shape, lambda i, n=value.ndim: (0,) * n))
    outs = tuple(
        pl.BlockSpec(shape.shape, lambda i, n=len(shape.shape): (0,) * n) for shape in out_shape
    )
    return pl.pallas_call(
        body,
        grid=(1,),
        in_specs=specs,
        out_specs=outs,
        out_shape=tuple(out_shape),
        scratch_shapes=scratch,
        compiler_params=pltpu.CompilerParams(vmem_limit_bytes=VMEM),
    )(*inputs)


def factor_block(block):
    return pl.BlockSpec((8, 1, PIECE, 2 * SLAB), lambda i: (0, block, 0, 0))


def pack_kernel(first_ref, second_ref, link_ref, out_ref):
    lane = lax.broadcasted_iota(jnp.int32, (6, 128), 1)
    for y in range(4):
        parts = [first_ref[0, y], first_ref[1, y], second_ref[0, y], second_ref[1, y]]
        links = jnp.where(lane < 96, link_ref[0, y], link_ref[1, y])
        for c in range(8):
            row = links
            for at, part in enumerate(parts):
                shift = (16 * at - 16 * c) % 128
                moved = pltpu.roll(part, shift, 1) if shift else part
                row = jnp.where((lane >= 16 * at) & (lane < 16 * at + 16), moved, row)
            out_ref[c, 6 * y : 6 * y + 6, :] = row


def front_kernel(where_ref, cells_ref, rhs_ref, link_ref, rows_ref):
    def some(step, carry):
        for u in range(16):
            at = step * 16 + u
            rows_ref[pl.ds(at, 1), :] = cells_ref[pl.ds(where_ref[at], 1), :]
        return carry

    lax.fori_loop(0, 64, some, 0)
    for part in range(8):
        turned = rows_ref[128 * part : 128 * part + 128, :].T
        rhs_ref[:, 128 * part : 128 * part + 128] = turned[:64]
        link_ref[0:8, 128 * part : 128 * part + 128] = turned[64:72]
        link_ref[8:16, 128 * part : 128 * part + 128] = turned[96:104]


def start_kernel(place_ref, rhs_ref, weight_ref, acc_ref):
    product = complex_dot(rhs_ref[0:ROWS, 0:BLOCK], block_weight(weight_ref))
    slab = rhs_ref[0:ROWS, BLOCK : BLOCK + SLAB]
    acc_ref[...] = jnp.where(place_ref[0] > 0, slab - product, slab)


def forward_one_kernel(place_ref, acc_ref, y0, y1, y2, y3, weight_ref, out_ref, keep_ref):
    q = place_ref[1]
    out_ref[...] = acc_ref[...] - slabs_dot([y0, y1, y2, y3], weight_ref, q, keep_ref)


def sent_dot(sent_ref, weight_ref):
    total = None
    for s in range(GROUP):
        weight = weight_ref[2 * s : 2 * s + 2, 0].reshape(SLAB, 2 * SLAB)
        part = complex_dot(sent_ref[s], weight)
        total = part if total is None else total + part
    return total


def forward_two_kernel(
    place_ref, acc_ref, y0, y1, y2, y3, sent_ref, weight2_ref, weight1_ref, inverse_ref, out_ref, part_ref
):
    q = place_ref[1]
    solved = (
        acc_ref[...]
        - slabs_dot([y0, y1, y2, y3], weight2_ref, q)
        - sent_dot(sent_ref, weight1_ref)
    )
    out_ref[...] = solved
    part_ref[...] = complex_dot(solved, inverse_ref[...])


def back_three_kernel(acc_ref, p0, p1, p2, p3, weight_ref, inverse_ref, x_ref, out_ref, part_ref):
    x = add_refs([p0, p1, p2, p3])
    x_ref[...] = x
    acc = acc_ref[...] - complex_dot(x, block_weight(weight_ref))
    out_ref[...] = acc
    part_ref[...] = complex_dot(acc, inverse_ref[...])


def back_two_kernel(
    acc_ref, p0, p1, p2, p3, x3_ref, weight2_ref, weight3_ref, inverse_ref, x_ref, out_ref, part_ref
):
    x = add_refs([p0, p1, p2, p3])
    x_ref[0] = x
    x_ref[1] = x3_ref[...]
    acc = (
        acc_ref[...]
        - complex_dot(x3_ref[...], block_weight(weight3_ref))
        - complex_dot(x, block_weight(weight2_ref))
    )
    out_ref[...] = acc
    part_ref[...] = complex_dot(acc, inverse_ref[...])


def back_one_kernel(
    acc_ref, p0, p1, p2, p3, later_ref, weight1_ref, weight2_ref, weight3_ref, inverse_ref, x_ref, part_ref
):
    x = add_refs([p0, p1, p2, p3])
    x_ref[0] = x
    x_ref[1] = later_ref[0]
    acc = (
        acc_ref[...]
        - complex_dot(later_ref[1], block_weight(weight3_ref))
        - complex_dot(later_ref[0], block_weight(weight2_ref))
        - complex_dot(x, block_weight(weight1_ref))
    )
    part_ref[...] = complex_dot(acc, inverse_ref[...])


def coupled(rhs, link_real, link_imag, x):
    real = rhs[:CHUNK] - (link_real * x[:CHUNK] - link_imag * x[CHUNK:])
    imag = rhs[CHUNK:] - (link_real * x[CHUNK:] + link_imag * x[:CHUNK])
    return jnp.concatenate([real, imag], axis=0)


def second_block(rhs_ref, link_ref, x):
    return coupled(
        rhs_ref[ROWS : 2 * ROWS, 0:BLOCK], link_ref[0:1, 0:BLOCK], link_ref[8:9, 0:BLOCK], x
    )


def second_slab(rhs_ref, link_ref, x, q):
    own = x[:, 0:SLAB]
    for s in range(1, GROUP):
        own = jnp.where(q == s, x[:, SLAB * s : SLAB * s + SLAB], own)
    end = BLOCK + SLAB
    return coupled(
        rhs_ref[ROWS : 2 * ROWS, BLOCK:end], link_ref[0:1, BLOCK:end], link_ref[8:9, BLOCK:end], own
    )


def couple_kernel(
    place_ref, rhs_ref, link_ref, p0, p1, p2, p3, x1_ref, x2_ref, x3_ref, weight_ref, x0_ref, slab_ref, out_ref
):
    plane, q = place_ref[0], place_ref[1]
    x0 = add_refs([p0, p1, p2, p3])
    x0_ref[0] = x0
    x0_ref[1] = x1_ref[...]
    own = jnp.where(plane == 1, x1_ref[...], jnp.where(plane == 2, x2_ref[...], x3_ref[...]))
    slab = second_slab(rhs_ref, link_ref, own, q)
    slab_ref[...] = slab
    out_ref[...] = slab - complex_dot(second_block(rhs_ref, link_ref, x0), block_weight(weight_ref))


def second_one_kernel(
    place_ref,
    rhs_ref,
    link_ref,
    slab_ref,
    x0_ref,
    f0,
    f1,
    f2,
    f3,
    weight0_ref,
    weight1_ref,
    out_ref,
    keep_ref,
):
    plane, q = place_ref[0], place_ref[1]
    x0 = x0_ref[...]
    first = second_slab(rhs_ref, link_ref, x0, q)
    product = complex_dot(second_block(rhs_ref, link_ref, x0), block_weight(weight0_ref))
    later = slab_ref[...] - product - slabs_dot([f0, f1, f2, f3], weight1_ref, q, keep_ref)
    out_ref[...] = jnp.where(plane == 0, first, later)


def cells_kernel(where_ref, x0_ref, x1_ref, x2_ref, x3_ref, out_ref, front_ref, rows_ref):
    for k, ref in enumerate((x0_ref, x1_ref, x2_ref, x3_ref)):
        for part in range(6):
            at = BLOCK * k + 128 * part
            piece = ref[:, 128 * part : 128 * part + 128]
            wide = jnp.concatenate([piece, jnp.zeros((128 - ROWS, 128), f32)], axis=0)
            front_ref[at : at + 128, :] = wide.T
    rows_ref[...] = jnp.zeros_like(rows_ref)
    for c in range(8):
        for u in range(CELLS):
            rows_ref[64 + u : 65 + u, :] = front_ref[pl.ds(where_ref[CELLS * c + u], 1), :]
        out_ref[c] = rows_ref[...].T[:ROWS]


def second_two_kernel(
    place_ref, acc_ref, f0, f1, f2, f3, sent_ref, cells_ref, weight2_ref, weight1_ref, out_ref
):
    q = place_ref[1]
    solved = (
        acc_ref[...]
        - slabs_dot([f0, f1, f2, f3], weight2_ref, q)
        - sent_dot(sent_ref, weight1_ref)
    )
    lane = lax.broadcasted_iota(jnp.int32, (ROWS, 128), 1)
    tail = jnp.concatenate([solved[:, 128:], jnp.zeros((ROWS, 64), f32)], axis=1)
    for c in range(8):
        out_ref[c, :, 0:128] = solved[:, 0:128]
        out_ref[c, :, 128:256] = jnp.where(lane < 64, tail, cells_ref[c])


def out_kernel(got_ref, solution_ref, forward_ref):
    for part in range(2):
        wide = got_ref[:, CHUNK * part : CHUNK * part + CHUNK, :].reshape(128, 256)
        forward_ref[part, 0:128, :] = wide[:, 0:128].T
        turned = wide[:, 128:256].T
        forward_ref[part, 128:SLAB, :] = turned[0:64]
        for y in range(4):
            solution_ref[part, y] = turned[64 + 6 * y : 70 + 6 * y]


def plane_send(value, source, target, turn=0):
    pairs = [
        (GROUP * source + q, GROUP * target + (q + turn) % GROUP) for q in range(GROUP)
    ]
    return lax.ppermute(value, "row", pairs)


def plane_spread(value, source, target):
    return [plane_send(value, source, target, d) for d in range(GROUP)]


def on_device(source1, source2, coupling, factor1, factor2, diag_inv, front_order):
    row_id = lax.axis_index("row")
    col_id = lax.axis_index("col")
    place = jnp.stack([row_id // GROUP, row_id % GROUP]).astype(jnp.int32)

    def gather_factor(factor):
        turned = factor.reshape(2 * SLAB, 4 * PIECE).T
        return lax.all_gather(turned, "col").reshape(8, 4, PIECE, 2 * SLAB)

    matrix1 = gather_factor(factor1)

    links = jnp.broadcast_to(coupling[..., None], coupling.shape + (128,))
    (packed,) = call(pack_kernel, [SDS((8, CELLS, 128), f32)], [source1, source2, links])
    packed = jnp.broadcast_to(packed[None], (16, 8, CELLS, 128)).reshape(128, CELLS, 128)
    cells = lax.all_to_all(packed, ("row", "col"), 0, 0).reshape(128 * CELLS, 128)

    cell_y = front_order // 48
    cell_x = front_order % 48
    place_of = ((cell_y // 4) * 8 + cell_x // 6) * CELLS + (cell_y % 4) * 6 + cell_x % 6
    own = lax.dynamic_slice_in_dim(place_of, row_id * SLAB, SLAB)
    where = jnp.concatenate([place_of[:BLOCK], own, jnp.zeros((64,), jnp.int32)])
    rhs, link = call(
        front_kernel,
        [SDS((64, 1024), f32), SDS((16, 1024), f32)],
        [where, cells],
        scratch=[pltpu.VMEM((1024, 128), f32)],
    )
    factor2, diag_inv, cells = lax.optimization_barrier((factor2, diag_inv, cells))
    matrix2 = gather_factor(factor2)
    inverse = diag_inv.reshape(2 * BLOCK, SLAB).T

    slab_shape = SDS((ROWS, SLAB), f32)
    block_shape = SDS((ROWS, BLOCK), f32)
    sent_shape = SDS((GROUP, ROWS, SLAB), f32)

    (acc,) = call(start_kernel, [slab_shape], [place, rhs, matrix1], {2: factor_block(0)})
    got = plane_spread(acc, 1, 2)
    acc, kept = call(
        forward_one_kernel,
        [slab_shape, sent_shape],
        [place, acc, *got, matrix1],
        {6: factor_block(1)},
    )
    got = plane_spread(acc, 2, 3)
    sent = plane_send(kept, 2, 3)
    acc, part = call(
        forward_two_kernel,
        [slab_shape, block_shape],
        [place, acc, *got, sent, matrix1, matrix1, inverse],
        {7: factor_block(2), 8: factor_block(1)},
    )
    got = plane_spread(part, 3, 2)
    x3, acc, part = call(
        back_three_kernel,
        [block_shape, slab_shape, block_shape],
        [acc, *got, matrix1, inverse],
        {5: factor_block(3)},
    )
    got = plane_spread(part, 2, 1)
    x3_one = plane_send(x3, 2, 1)
    x3_three = plane_send(x3, 2, 3)
    x23, acc, part = call(
        back_two_kernel,
        [SDS((2, ROWS, BLOCK), f32), slab_shape, block_shape],
        [acc, *got, x3_one, matrix1, matrix1, inverse],
        {6: factor_block(2), 7: factor_block(3)},
    )
    got = plane_spread(part, 1, 0)
    x23_zero = plane_send(x23, 1, 0)
    x2_two = plane_send(x23[0], 1, 2)
    x12, part = call(
        back_one_kernel,
        [SDS((2, ROWS, BLOCK), f32), block_shape],
        [acc, *got, x23_zero, matrix1, matrix1, matrix1, inverse],
        {6: factor_block(1), 7: factor_block(2), 8: factor_block(3)},
    )
    got = plane_spread(part, 0, 1)
    x1_one = plane_send(x12[0], 0, 1)
    x12_three = plane_send(x12, 0, 3)
    x3_all = x3 + x3_one + x3_three + x23_zero[1]
    x2_all = x23[0] + x23_zero[0] + x2_two + x12_three[1]
    x1_some = x12[0] + x1_one + x12_three[0]
    x01, slab, acc = call(
        couple_kernel,
        [SDS((2, ROWS, BLOCK), f32), slab_shape, slab_shape],
        [place, rhs, link, *got, x1_some, x2_all, x3_all, matrix2],
        {10: factor_block(0)},
    )
    got = plane_spread(acc, 1, 2)
    x01_two = plane_send(x01, 1, 2)
    x0_three = plane_send(x01[0], 1, 3)
    x0_zero = plane_send(x01[0], 1, 0)
    x0_all = x01[0] + x01_two[0] + x0_three + x0_zero
    x1_all = x1_some + x01_two[1]
    acc, kept = call(
        second_one_kernel,
        [slab_shape, sent_shape],
        [place, rhs, link, slab, x0_all, *got, matrix2, matrix2],
        {9: factor_block(0), 10: factor_block(1)},
    )
    got = plane_spread(acc, 2, 3)
    sent = plane_send(kept, 2, 3)

    at = jnp.arange(SLAB, dtype=jnp.int32)
    own_c, own_y, own_x = at // CELLS, at % CELLS // 6, at % 6
    own_cells = (row_id * 4 + own_y) * 48 + own_c * 6 + own_x
    hits = front_order[None, :] == own_cells[:, None]
    slots = jnp.sum(jnp.where(hits, jnp.arange(4 * BLOCK, dtype=jnp.int32)[None, :], 0), axis=1)
    (mine,) = call(
        cells_kernel,
        [SDS((8, ROWS, 128), f32)],
        [slots, x0_all, x1_all, x2_all, x3_all],
        scratch=[pltpu.VMEM((4 * BLOCK, 128), f32), pltpu.VMEM((128, 128), f32)],
    )
    (last,) = call(
        second_two_kernel,
        [SDS((8, ROWS, 256), f32)],
        [place, acc, *got, sent, mine, matrix2, matrix2],
        {8: factor_block(2), 9: factor_block(1)},
    )
    arrived = lax.all_to_all(last, "col", 0, 0)
    return call(
        out_kernel, [SDS((2, 4, 6, 128), f32), SDS((2, SLAB, 128), f32)], [arrived]
    )


def solution(mesh):
    in_specs = (
        P(None, "row", "col", None),
        P(None, "row", "col", None),
        P(None, "row", "col"),
        P(None, "row", "col"),
        P(None, "row", "col"),
        P(None, None, "row"),
        P(),
    )
    out_specs = (P(None, "row", "col", None), P(None, "row", None))
    return jax.shard_map(
        on_device, mesh=mesh, in_specs=in_specs, out_specs=out_specs, check_vma=False
    )
```

```python
import functools

import jax
import jax.numpy as jnp
from jax import lax
from jax.experimental import pallas as pl
from jax.experimental.pallas import tpu as pltpu
from jax.sharding import PartitionSpec as P

GROUP = 4
CHUNK = 16
ROWS = 2 * CHUNK
SLAB = 192
BLOCK = 768
PIECE = 96
CELLS = 24
VMEM = 40 * 1024 * 1024

SDS = jax.ShapeDtypeStruct
f32 = jnp.float32


def split(value):
    high = value.astype(jnp.bfloat16)
    return high, (value - high.astype(f32)).astype(jnp.bfloat16)


def complex_dot(vector, weight):
    half = weight.shape[1] // 2
    weight_high, weight_low = split(weight)
    high, low = split(vector)
    both = jnp.dot(
        jnp.concatenate([high, low], axis=0), weight_high, preferred_element_type=f32
    )
    total = both[:ROWS] + both[ROWS:] + jnp.dot(high, weight_low, preferred_element_type=f32)
    real = total[:CHUNK, :half] - total[CHUNK:, half:]
    imag = total[:CHUNK, half:] + total[CHUNK:, :half]
    return jnp.concatenate([real, imag], axis=0)


def block_weight(ref):
    return ref[...].reshape(BLOCK, 2 * SLAB)


def slabs_dot(slabs, weight_ref, q, keep=None):
    total = None
    for d, slab in enumerate(slabs):
        source = lax.rem(q - d + GROUP, GROUP)
        if keep is not None:
            keep[source] = slab
        weight = weight_ref[pl.ds(2 * source, 2)].reshape(SLAB, 2 * SLAB)
        part = complex_dot(slab, weight)
        total = part if total is None else total + part
    return total


def sent_dot(sent_ref, weight_ref):
    total = None
    for s in range(GROUP):
        weight = weight_ref[2 * s : 2 * s + 2].reshape(SLAB, 2 * SLAB)
        part = complex_dot(sent_ref[s], weight)
        total = part if total is None else total + part
    return total


def add_refs(refs):
    total = refs[0][...]
    for ref in refs[1:]:
        total = total + ref[...]
    return total


def call(body, out_shape, inputs, scratch=()):
    specs = []
    for value in inputs:
        if value.dtype == jnp.int32:
            specs.append(pl.BlockSpec(memory_space=pltpu.SMEM))
        else:
            specs.append(pl.BlockSpec(value.shape, lambda i, n=value.ndim: (0,) * n))
    outs = tuple(
        pl.BlockSpec(shape.shape, lambda i, n=len(shape.shape): (0,) * n) for shape in out_shape
    )
    return pl.pallas_call(
        body,
        grid=(1,),
        in_specs=specs,
        out_specs=outs,
        out_shape=tuple(out_shape),
        scratch_shapes=scratch,
        compiler_params=pltpu.CompilerParams(vmem_limit_bytes=VMEM),
    )(*inputs)


def pack_kernel(first_ref, second_ref, link_ref, out_ref):
    lane = lax.broadcasted_iota(jnp.int32, (6, 128), 1)
    for y in range(2):
        parts = []
        for half in range(2):
            for ref in (first_ref, second_ref):
                parts += [ref[0, y + 2 * half], ref[1, y + 2 * half]]
        for c in range(8):
            row = jnp.zeros((6, 128), f32)
            for at, part in enumerate(parts):
                shift = (16 * at - 16 * c) % 128
                moved = pltpu.roll(part, shift, 1) if shift else part
                row = jnp.where((lane >= 16 * at) & (lane < 16 * at + 16), moved, row)
            out_ref[c, 6 * y : 6 * y + 6, :] = row
    for c in range(8):
        out_ref[c, 12:16, :] = jnp.broadcast_to(link_ref[...], (4, 128))


def front_kernel(where_ref, cells_ref, mark_ref, rhs_ref, link_ref, rows_ref, links_ref):
    def some(step, carry):
        for u in range(16):
            at = step * 16 + u
            source = where_ref[at]
            rows_ref[pl.ds(at, 1), :] = cells_ref[pl.ds(source, 1), :]
            links_ref[pl.ds(at, 1), :] = cells_ref[pl.ds(source // 16 * 16 + 15, 1), :]
        return carry

    lax.fori_loop(0, 64, some, 0)
    lane = lax.broadcasted_iota(jnp.int32, (32, 128), 0).astype(f32)
    for part in range(8):
        at = slice(128 * part, 128 * part + 128)
        turned = rows_ref[at, :].T
        upper = mark_ref[0:1, at] > 0.5
        rhs_ref[:, at] = jnp.where(upper, turned[64:128], turned[0:64])
        turned = links_ref[at, :].T
        own = mark_ref[1:2, at] == lane
        real = jnp.sum(jnp.where(own, turned[0:32], 0.0), axis=0, keepdims=True)
        imag = jnp.sum(jnp.where(own, turned[32:64], 0.0), axis=0, keepdims=True)
        link_ref[0:8, at] = jnp.broadcast_to(real, (8, 128))
        link_ref[8:16, at] = jnp.broadcast_to(imag, (8, 128))


def start_kernel(place_ref, rhs_ref, weight_ref, acc_ref):
    product = complex_dot(rhs_ref[0:ROWS, 0:BLOCK], block_weight(weight_ref))
    slab = rhs_ref[0:ROWS, BLOCK : BLOCK + SLAB]
    acc_ref[...] = jnp.where(place_ref[0] > 0, slab - product, slab)


def forward_one_kernel(place_ref, acc_ref, y0, y1, y2, y3, weight_ref, out_ref, keep_ref):
    slabs = [y0[...], y1[...], y2[...], y3[...]]
    acc = acc_ref[...] - slabs_dot(slabs, weight_ref, place_ref[1], keep_ref)
    out_ref[...] = acc
    keep_ref[GROUP] = acc


def forward_two_kernel(
    place_ref, acc_ref, sent_ref, y1, y2, y3, weight2_ref, weight1_ref, inverse_ref, out_ref, part_ref
):
    slabs = [sent_ref[GROUP], y1[...], y2[...], y3[...]]
    solved = (
        acc_ref[...]
        - slabs_dot(slabs, weight2_ref, place_ref[1])
        - sent_dot(sent_ref, weight1_ref)
    )
    out_ref[...] = solved
    part_ref[...] = complex_dot(solved, inverse_ref[...])


def back_three_kernel(
    acc_ref, p0, p1, p2, p3, weight_ref, inverse_ref, x_ref, acc_out_ref, part_ref, pair_ref
):
    x = add_refs([p0, p1, p2, p3])
    acc = acc_ref[...] - complex_dot(x, block_weight(weight_ref))
    part = complex_dot(acc, inverse_ref[...])
    x_ref[...] = x
    acc_out_ref[...] = acc
    part_ref[...] = part
    pair_ref[0] = part
    pair_ref[1] = x


def back_two_kernel(
    acc_ref, got_ref, p1, p2, p3, weight2_ref, weight3_ref, inverse_ref, x_ref, acc_out_ref, part_ref, pair_ref
):
    x = add_refs([got_ref.at[0], p1, p2, p3])
    acc = (
        acc_ref[...]
        - complex_dot(got_ref[1], block_weight(weight3_ref))
        - complex_dot(x, block_weight(weight2_ref))
    )
    part = complex_dot(acc, inverse_ref[...])
    x_ref[...] = x
    acc_out_ref[...] = acc
    part_ref[...] = part
    pair_ref[0] = part
    pair_ref[1] = x


def back_one_kernel(
    acc_ref,
    x3_ref,
    got_ref,
    p1,
    p2,
    p3,
    weight1_ref,
    weight2_ref,
    weight3_ref,
    inverse_ref,
    both_ref,
    part_ref,
    pair_ref,
):
    x = add_refs([got_ref.at[0], p1, p2, p3])
    acc = (
        acc_ref[...]
        - complex_dot(x3_ref[...], block_weight(weight3_ref))
        - complex_dot(got_ref[1], block_weight(weight2_ref))
        - complex_dot(x, block_weight(weight1_ref))
    )
    part = complex_dot(acc, inverse_ref[...])
    both_ref[0] = x
    both_ref[1] = got_ref[1]
    part_ref[...] = part
    pair_ref[0] = part
    pair_ref[1] = x


def coupled(rhs, link_real, link_imag, x):
    real = rhs[:CHUNK] - (link_real * x[:CHUNK] - link_imag * x[CHUNK:])
    imag = rhs[CHUNK:] - (link_real * x[CHUNK:] + link_imag * x[:CHUNK])
    return jnp.concatenate([real, imag], axis=0)


def second_block(rhs_ref, link_ref, x):
    return coupled(
        rhs_ref[ROWS : 2 * ROWS, 0:BLOCK], link_ref[0:1, 0:BLOCK], link_ref[8:9, 0:BLOCK], x
    )


def second_slab(rhs_ref, link_ref, x, q):
    own = x[:, 0:SLAB]
    for s in range(1, GROUP):
        own = jnp.where(q == s, x[:, SLAB * s : SLAB * s + SLAB], own)
    end = BLOCK + SLAB
    return coupled(
        rhs_ref[ROWS : 2 * ROWS, BLOCK:end], link_ref[0:1, BLOCK:end], link_ref[8:9, BLOCK:end], own
    )


def couple_kernel(
    place_ref,
    rhs_ref,
    link_ref,
    got_ref,
    p1,
    p2,
    p3,
    x2_ref,
    x3_ref,
    weight_ref,
    x0_ref,
    x1_ref,
    slab_ref,
    out_ref,
    send_ref,
):
    plane, q = place_ref[0], place_ref[1]
    x0 = add_refs([got_ref.at[0], p1, p2, p3])
    x1 = got_ref[1]
    own = jnp.where(plane == 1, x1, jnp.where(plane == 2, x2_ref[...], x3_ref[...]))
    slab = second_slab(rhs_ref, link_ref, own, q)
    solved = slab - complex_dot(second_block(rhs_ref, link_ref, x0), block_weight(weight_ref))
    x0_ref[...] = x0
    x1_ref[...] = x1
    slab_ref[...] = slab
    out_ref[...] = solved
    send_ref[:, 0:BLOCK] = x0
    send_ref[:, BLOCK : BLOCK + SLAB] = solved
    send_ref[:, BLOCK + SLAB :] = jnp.zeros((ROWS, 64), f32)


def second_one_kernel(
    place_ref,
    rhs_ref,
    link_ref,
    slab_ref,
    x0_own,
    x0_zero,
    x0_three,
    got_ref,
    f1,
    f2,
    f3,
    weight0_ref,
    weight1_ref,
    out_ref,
    keep_ref,
    x0_ref,
):
    plane, q = place_ref[0], place_ref[1]
    x0 = x0_own[...] + x0_zero[...] + x0_three[...] + got_ref[:, 0:BLOCK]
    x0_ref[...] = x0
    first = second_slab(rhs_ref, link_ref, x0, q)
    slabs = [got_ref[:, BLOCK : BLOCK + SLAB], f1[...], f2[...], f3[...]]
    product = complex_dot(second_block(rhs_ref, link_ref, x0), block_weight(weight0_ref))
    later = slab_ref[...] - product - slabs_dot(slabs, weight1_ref, q, keep_ref)
    solved = jnp.where(plane == 0, first, later)
    out_ref[...] = solved
    keep_ref[GROUP] = solved


def cells_kernel(
    where_ref,
    x0_ref,
    both_zero,
    x1_one,
    x1_two,
    both_three,
    x2_one,
    x2_two,
    x3_zero,
    pair_one,
    x3_two,
    x3_three,
    out_ref,
    front_ref,
    rows_ref,
):
    blocks = (
        x0_ref[...],
        both_zero[0] + x1_one[...] + x1_two[...] + both_three[0],
        both_zero[1] + x2_one[...] + x2_two[...] + both_three[1],
        x3_zero[...] + pair_one[1] + x3_two[...] + x3_three[...],
    )
    for k, x in enumerate(blocks):
        for part in range(6):
            at = BLOCK * k + 128 * part
            piece = x[:, 128 * part : 128 * part + 128]
            wide = jnp.concatenate([piece, jnp.zeros((128 - ROWS, 128), f32)], axis=0)
            front_ref[at : at + 128, :] = wide.T
    rows_ref[...] = jnp.zeros_like(rows_ref)
    for c in range(8):
        for u in range(CELLS):
            rows_ref[64 + u : 65 + u, :] = front_ref[pl.ds(where_ref[CELLS * c + u], 1), :]
        out_ref[c] = rows_ref[...].T[:ROWS]


def second_two_kernel(
    place_ref, acc_ref, sent_ref, f1, f2, f3, cells_ref, weight2_ref, weight1_ref, out_ref
):
    slabs = [sent_ref[GROUP], f1[...], f2[...], f3[...]]
    solved = (
        acc_ref[...]
        - slabs_dot(slabs, weight2_ref, place_ref[1])
        - sent_dot(sent_ref, weight1_ref)
    )
    lane = lax.broadcasted_iota(jnp.int32, (ROWS, 128), 1)
    tail = jnp.concatenate([solved[:, 128:], jnp.zeros((ROWS, 64), f32)], axis=1)
    for c in range(8):
        out_ref[c, :, 0:128] = solved[:, 0:128]
        out_ref[c, :, 128:256] = jnp.where(lane < 64, tail, cells_ref[c])


def out_kernel(got_ref, solution_ref, forward_ref):
    for part in range(2):
        wide = got_ref[:, CHUNK * part : CHUNK * part + CHUNK, :].reshape(128, 256)
        forward_ref[part, 0:128, :] = wide[:, 0:128].T
        turned = wide[:, 128:256].T
        forward_ref[part, 128:SLAB, :] = turned[0:64]
        for y in range(4):
            solution_ref[part, y] = turned[64 + 6 * y : 70 + 6 * y]


def plane_send(value, source, target, turn=0):
    pairs = [
        (GROUP * source + q, GROUP * target + (q + turn) % GROUP) for q in range(GROUP)
    ]
    return lax.ppermute(value, "row", pairs)


def plane_spread(value, source, target, first=None):
    return [
        plane_send(value if first is None or d else first, source, target, d)
        for d in range(GROUP)
    ]


def after(value, arrived):
    return lax.optimization_barrier((value, arrived))[0]


def on_device(source1, source2, coupling, factor1, factor2, diag_inv, front_order):
    row_id = lax.axis_index("row")
    col_id = lax.axis_index("col")
    place = jnp.stack([row_id // GROUP, row_id % GROUP]).astype(jnp.int32)

    def gather_blocks(turned, first, count):
        piece = turned[PIECE * first : PIECE * (first + count)]
        whole = lax.all_gather(piece, "col").reshape(8, count, PIECE, 2 * SLAB)
        return [whole[:, at] for at in range(count)]

    turned1 = factor1.reshape(2 * SLAB, 4 * PIECE).T
    matrix1 = gather_blocks(turned1, 0, 1)

    links = jnp.pad(coupling.reshape(2, CELLS), ((0, 0), (0, 32 - CELLS))).reshape(1, 64)
    links = jnp.pad(links, ((0, 0), (0, 64)))
    (packed,) = call(pack_kernel, [SDS((8, 16, 128), f32)], [source1, source2, links])
    turned1, packed = lax.optimization_barrier((turned1, packed))
    matrix1 += gather_blocks(turned1, 1, 1)
    matrix1 += gather_blocks(turned1, 2, 1)
    matrix1 += gather_blocks(turned1, 3, 1)
    packed = jnp.broadcast_to(packed[None], (16, 8, 16, 128)).reshape(128, 16, 128)
    cells = lax.all_to_all(packed, ("row", "col"), 0, 0).reshape(128 * 16, 128)

    cell_y = front_order // 48
    cell_x = front_order % 48
    place_of = ((cell_y // 4) * 8 + cell_x // 6) * 16 + (cell_y % 2) * 6 + cell_x % 6
    upper = (cell_y % 4) // 2
    inner = (cell_y % 4) * 6 + cell_x % 6
    every = jnp.stack([place_of, upper, inner])
    own = lax.dynamic_slice_in_dim(every, row_id * SLAB, SLAB, 1)
    every = jnp.concatenate([every[:, :BLOCK], own, jnp.zeros((3, 64), jnp.int32)], axis=1)
    rhs, link = call(
        front_kernel,
        [SDS((64, 1024), f32), SDS((16, 1024), f32)],
        [every[0], cells, every[1:].astype(f32)],
        scratch=[pltpu.VMEM((1024, 128), f32), pltpu.VMEM((1024, 128), f32)],
    )
    factor2, diag_inv, cells = lax.optimization_barrier((factor2, diag_inv, cells))
    turned2 = factor2.reshape(2 * SLAB, 4 * PIECE).T
    matrix2 = gather_blocks(turned2, 0, 3)
    inverse = diag_inv.reshape(2 * BLOCK, SLAB).T

    slab_shape = SDS((ROWS, SLAB), f32)
    block_shape = SDS((ROWS, BLOCK), f32)
    pair_shape = SDS((2, ROWS, BLOCK), f32)
    sent_shape = SDS((GROUP + 1, ROWS, SLAB), f32)

    (acc,) = call(start_kernel, [slab_shape], [place, rhs, matrix1[0]])
    got = plane_spread(acc, 1, 2)
    acc, kept = call(
        forward_one_kernel, [slab_shape, sent_shape], [place, acc, *got, matrix1[1]]
    )
    got = plane_spread(acc, 2, 3, kept)
    acc, part = call(
        forward_two_kernel,
        [slab_shape, block_shape],
        [place, acc, *got, matrix1[2], matrix1[1], inverse],
    )
    got = plane_spread(part, 3, 2)
    x3_two, acc, part, pair = call(
        back_three_kernel,
        [block_shape, slab_shape, block_shape, pair_shape],
        [acc, *got, matrix1[3], inverse],
    )
    got = plane_spread(part, 2, 1, pair)
    pair_one = got[0]
    x3_three = plane_send(after(x3_two, got[1]), 2, 3)
    x2_one, acc, part, pair = call(
        back_two_kernel,
        [block_shape, slab_shape, block_shape, pair_shape],
        [acc, *got, matrix1[2], matrix1[3], inverse],
    )
    matrix2, part, pair = lax.optimization_barrier((matrix2, part, pair))
    got = plane_spread(part, 1, 0, pair)
    x3_zero = plane_send(x3_three, 3, 0)
    x2_two = plane_send(after(x2_one, got[1]), 1, 2)
    both_zero, part, pair = call(
        back_one_kernel,
        [pair_shape, block_shape, pair_shape],
        [acc, x3_zero, *got, matrix1[1], matrix1[2], matrix1[3], inverse],
    )
    got = plane_spread(part, 0, 1, pair)
    both_three = plane_send(after(both_zero, got[1]), 0, 3)
    x0_one, x1_one, slab, acc, send = call(
        couple_kernel,
        [block_shape, block_shape, slab_shape, slab_shape, SDS((ROWS, 1024), f32)],
        [place, rhs, link, *got, x2_two, x3_three, matrix2[0]],
    )
    got = plane_spread(acc, 1, 2, send)
    x0_zero = plane_send(after(x0_one, got[1]), 1, 0)
    x0_three = plane_send(after(x0_one, got[1]), 1, 3)
    x1_two = plane_send(after(x1_one, got[2]), 1, 2)
    acc, kept, x0_all = call(
        second_one_kernel,
        [slab_shape, sent_shape, block_shape],
        [place, rhs, link, slab, x0_one, x0_zero, x0_three, *got, matrix2[0], matrix2[1]],
    )
    got = plane_spread(acc, 2, 3, kept)

    at = jnp.arange(SLAB, dtype=jnp.int32)
    own_c, own_y, own_x = at // CELLS, at % CELLS // 6, at % 6
    own_cells = (row_id * 4 + own_y) * 48 + own_c * 6 + own_x
    hits = front_order[None, :] == own_cells[:, None]
    slots = jnp.sum(jnp.where(hits, jnp.arange(4 * BLOCK, dtype=jnp.int32)[None, :], 0), axis=1)
    (mine,) = call(
        cells_kernel,
        [SDS((8, ROWS, 128), f32)],
        [
            slots,
            x0_all,
            both_zero,
            x1_one,
            x1_two,
            both_three,
            x2_one,
            x2_two,
            x3_zero,
            pair_one,
            x3_two,
            x3_three,
        ],
        scratch=[pltpu.VMEM((4 * BLOCK, 128), f32), pltpu.VMEM((128, 128), f32)],
    )
    (last,) = call(
        second_two_kernel,
        [SDS((8, ROWS, 256), f32)],
        [place, acc, *got, mine, matrix2[2], matrix2[1]],
    )
    arrived = lax.all_to_all(last, "col", 0, 0)
    return call(
        out_kernel, [SDS((2, 4, 6, 128), f32), SDS((2, SLAB, 128), f32)], [arrived]
    )


def solution(mesh):
    in_specs = (
        P(None, "row", "col", None),
        P(None, "row", "col", None),
        P(None, "row", "col"),
        P(None, "row", "col"),
        P(None, "row", "col"),
        P(None, None, "row"),
        P(),
    )
    out_specs = (P(None, "row", "col", None), P(None, "row", None))
    return jax.shard_map(
        on_device, mesh=mesh, in_specs=in_specs, out_specs=out_specs, check_vma=False
    )
```

```python
import functools

import jax
import jax.numpy as jnp
from jax import lax
from jax.experimental import pallas as pl
from jax.experimental.pallas import tpu as pltpu
from jax.sharding import PartitionSpec as P

GROUP = 4
CHUNK = 16
ROWS = 2 * CHUNK
SLAB = 192
BLOCK = 768
PIECE = 96
CELLS = 24
VMEM = 40 * 1024 * 1024

SDS = jax.ShapeDtypeStruct
f32 = jnp.float32


def split(value):
    high = value.astype(jnp.bfloat16)
    return high, (value - high.astype(f32)).astype(jnp.bfloat16)


def complex_dot(vector, weight):
    half = weight.shape[1] // 2
    weight_high, weight_low = split(weight)
    high, low = split(vector)
    both = jnp.dot(
        jnp.concatenate([high, low], axis=0), weight_high, preferred_element_type=f32
    )
    total = both[:ROWS] + both[ROWS:] + jnp.dot(high, weight_low, preferred_element_type=f32)
    real = total[:CHUNK, :half] - total[CHUNK:, half:]
    imag = total[:CHUNK, half:] + total[CHUNK:, :half]
    return jnp.concatenate([real, imag], axis=0)


def slot_of(plane, block):
    return jnp.minimum(jnp.where(plane < block, block - 1, block), GROUP - 2)


def block_weight(ref, slot):
    return ref[:, slot].reshape(BLOCK, 2 * SLAB)


def slabs_dot(slabs, weight_ref, slot, q, keep=None):
    total = None
    for d, slab in enumerate(slabs):
        source = lax.rem(q - d + GROUP, GROUP)
        if keep is not None:
            keep[source] = slab
        weight = weight_ref[pl.ds(2 * source, 2), slot].reshape(SLAB, 2 * SLAB)
        part = complex_dot(slab, weight)
        total = part if total is None else total + part
    return total


def sent_dot(sent_ref, weight_ref, slot):
    total = None
    for s in range(GROUP):
        weight = weight_ref[2 * s : 2 * s + 2, slot].reshape(SLAB, 2 * SLAB)
        part = complex_dot(sent_ref[s], weight)
        total = part if total is None else total + part
    return total


def add_refs(refs):
    total = refs[0][...]
    for ref in refs[1:]:
        total = total + ref[...]
    return total


def call(body, out_shape, inputs, scratch=()):
    specs = []
    for value in inputs:
        if value.dtype == jnp.int32:
            specs.append(pl.BlockSpec(memory_space=pltpu.SMEM))
        else:
            specs.append(pl.BlockSpec(value.shape, lambda i, n=value.ndim: (0,) * n))
    outs = tuple(
        pl.BlockSpec(shape.shape, lambda i, n=len(shape.shape): (0,) * n) for shape in out_shape
    )
    return pl.pallas_call(
        body,
        grid=(1,),
        in_specs=specs,
        out_specs=outs,
        out_shape=tuple(out_shape),
        scratch_shapes=scratch,
        compiler_params=pltpu.CompilerParams(vmem_limit_bytes=VMEM),
    )(*inputs)


def turn_first_kernel(place_ref, factor_ref, out_ref, turned_ref):
    rows = factor_ref[...].reshape(2 * SLAB, 4 * PIECE)
    for part in range(3):
        turned_ref[128 * part : 128 * part + 128, :] = rows[:, 128 * part : 128 * part + 128].T
    for slot in range(GROUP - 1):
        block = slot + jnp.where(place_ref[0] > slot, 0, 1)
        out_ref[PIECE * slot : PIECE * slot + PIECE, :] = turned_ref[pl.ds(block * PIECE, PIECE), :]


def pack_kernel(first_ref, second_ref, link_ref, out_ref):
    lane = lax.broadcasted_iota(jnp.int32, (6, 128), 1)
    for y in range(2):
        parts = []
        for half in range(2):
            for ref in (first_ref, second_ref):
                parts += [ref[0, y + 2 * half], ref[1, y + 2 * half]]
        for c in range(8):
            row = jnp.zeros((6, 128), f32)
            for at, part in enumerate(parts):
                shift = (16 * at - 16 * c) % 128
                moved = pltpu.roll(part, shift, 1) if shift else part
                row = jnp.where((lane >= 16 * at) & (lane < 16 * at + 16), moved, row)
            out_ref[c, 6 * y : 6 * y + 6, :] = row
    for c in range(8):
        out_ref[c, 12:16, :] = jnp.broadcast_to(link_ref[...], (4, 128))


def front_kernel(where_ref, cells_ref, mark_ref, rhs_ref, link_ref, rows_ref, links_ref):
    def some(step, carry):
        for u in range(16):
            at = step * 16 + u
            source = where_ref[at]
            rows_ref[pl.ds(at, 1), :] = cells_ref[pl.ds(source, 1), :]
            links_ref[pl.ds(at, 1), :] = cells_ref[pl.ds(source | 15, 1), :]
        return carry

    lax.fori_loop(0, 64, some, 0)
    lane = lax.broadcasted_iota(jnp.int32, (32, 128), 0).astype(f32)
    for part in range(8):
        at = slice(128 * part, 128 * part + 128)
        turned = rows_ref[at, :].T
        upper = mark_ref[0:1, at] > 0.5
        rhs_ref[:, at] = jnp.where(upper, turned[64:128], turned[0:64])
        turned = links_ref[at, :].T
        own = mark_ref[1:2, at] == lane
        real = jnp.sum(jnp.where(own, turned[0:32], 0.0), axis=0, keepdims=True)
        imag = jnp.sum(jnp.where(own, turned[32:64], 0.0), axis=0, keepdims=True)
        link_ref[0:8, at] = jnp.broadcast_to(real, (8, 128))
        link_ref[8:16, at] = jnp.broadcast_to(imag, (8, 128))


def start_kernel(place_ref, rhs_ref, weight_ref, acc_ref):
    slot = slot_of(place_ref[0], 0)
    product = complex_dot(rhs_ref[0:ROWS, 0:BLOCK], block_weight(weight_ref, slot))
    slab = rhs_ref[0:ROWS, BLOCK : BLOCK + SLAB]
    acc_ref[...] = jnp.where(place_ref[0] > 0, slab - product, slab)


def forward_one_kernel(place_ref, acc_ref, y0, y1, y2, y3, weight_ref, out_ref, keep_ref):
    slabs = [y0[...], y1[...], y2[...], y3[...]]
    slot = slot_of(place_ref[0], 1)
    out_ref[...] = acc_ref[...] - slabs_dot(slabs, weight_ref, slot, place_ref[1], keep_ref)


def forward_two_kernel(
    place_ref, acc_ref, sent_ref, y0, y1, y2, y3, weight_ref, inverse_ref, out_ref, part_ref
):
    plane, q = place_ref[0], place_ref[1]
    slabs = [y0[...], y1[...], y2[...], y3[...]]
    solved = (
        acc_ref[...]
        - sent_dot(sent_ref, weight_ref, slot_of(plane, 1))
        - slabs_dot(slabs, weight_ref, slot_of(plane, 2), q)
    )
    out_ref[...] = solved
    part_ref[...] = complex_dot(solved, inverse_ref[...])


def back_three_kernel(
    place_ref, acc_ref, p0, p1, p2, p3, weight_ref, inverse_ref, x_ref, acc_out_ref, part_ref
):
    x = add_refs([p0, p1, p2, p3])
    acc = acc_ref[...] - complex_dot(x, block_weight(weight_ref, slot_of(place_ref[0], 3)))
    x_ref[...] = x
    acc_out_ref[...] = acc
    part_ref[...] = complex_dot(acc, inverse_ref[...])


def back_two_kernel(
    place_ref, acc_ref, p0, p1, p2, p3, x3_ref, weight_ref, inverse_ref, x_ref, acc_out_ref, part_ref
):
    plane = place_ref[0]
    x = add_refs([p0, p1, p2, p3])
    acc = (
        acc_ref[...]
        - complex_dot(x3_ref[...], block_weight(weight_ref, slot_of(plane, 3)))
        - complex_dot(x, block_weight(weight_ref, slot_of(plane, 2)))
    )
    x_ref[...] = x
    acc_out_ref[...] = acc
    part_ref[...] = complex_dot(acc, inverse_ref[...])


def back_one_kernel(
    place_ref,
    acc_ref,
    p0,
    p1,
    p2,
    p3,
    x2_ref,
    x3_ref,
    weight_ref,
    inverse_ref,
    x_ref,
    both_ref,
    part_ref,
):
    plane = place_ref[0]
    x = add_refs([p0, p1, p2, p3])
    acc = (
        acc_ref[...]
        - complex_dot(x3_ref[...], block_weight(weight_ref, slot_of(plane, 3)))
        - complex_dot(x2_ref[...], block_weight(weight_ref, slot_of(plane, 2)))
        - complex_dot(x, block_weight(weight_ref, slot_of(plane, 1)))
    )
    part_ref[...] = complex_dot(acc, inverse_ref[...])
    x_ref[...] = x
    both_ref[0] = x
    both_ref[1] = x2_ref[...]


def coupled(rhs, link_real, link_imag, x):
    real = rhs[:CHUNK] - (link_real * x[:CHUNK] - link_imag * x[CHUNK:])
    imag = rhs[CHUNK:] - (link_real * x[CHUNK:] + link_imag * x[:CHUNK])
    return jnp.concatenate([real, imag], axis=0)


def second_block(rhs_ref, link_ref, x):
    return coupled(
        rhs_ref[ROWS : 2 * ROWS, 0:BLOCK], link_ref[0:1, 0:BLOCK], link_ref[8:9, 0:BLOCK], x
    )


def second_slab(rhs_ref, link_ref, x, q):
    own = x[:, 0:SLAB]
    for s in range(1, GROUP):
        own = jnp.where(q == s, x[:, SLAB * s : SLAB * s + SLAB], own)
    end = BLOCK + SLAB
    return coupled(
        rhs_ref[ROWS : 2 * ROWS, BLOCK:end], link_ref[0:1, BLOCK:end], link_ref[8:9, BLOCK:end], own
    )


def couple_kernel(
    place_ref,
    rhs_ref,
    link_ref,
    p0,
    p1,
    p2,
    p3,
    x1_ref,
    x2_ref,
    x3_ref,
    weight_ref,
    x0_ref,
    slab_ref,
    out_ref,
):
    plane, q = place_ref[0], place_ref[1]
    x0 = add_refs([p0, p1, p2, p3])
    own = jnp.where(plane == 1, x1_ref[...], jnp.where(plane == 2, x2_ref[...], x3_ref[...]))
    slab = second_slab(rhs_ref, link_ref, own, q)
    x0_ref[...] = x0
    slab_ref[...] = slab
    out_ref[...] = slab - complex_dot(
        second_block(rhs_ref, link_ref, x0), block_weight(weight_ref, 0)
    )


def second_one_kernel(
    place_ref,
    rhs_ref,
    link_ref,
    slab_ref,
    x0_one,
    x0_two,
    x0_zero,
    x0_three,
    f0,
    f1,
    f2,
    f3,
    weight_ref,
    out_ref,
    keep_ref,
    x0_ref,
):
    plane, q = place_ref[0], place_ref[1]
    x0 = add_refs([x0_one, x0_two, x0_zero, x0_three])
    x0_ref[...] = x0
    first = second_slab(rhs_ref, link_ref, x0, q)
    slabs = [f0[...], f1[...], f2[...], f3[...]]
    product = complex_dot(second_block(rhs_ref, link_ref, x0), block_weight(weight_ref, 0))
    later = slab_ref[...] - product - slabs_dot(slabs, weight_ref, 1, q, keep_ref)
    out_ref[...] = jnp.where(plane == 0, first, later)


def cells_kernel(
    where_ref,
    x0_ref,
    both_zero,
    x1_one,
    x1_two,
    both_three,
    x2_one,
    x2_two,
    x3_zero,
    x3_one,
    x3_two,
    x3_three,
    out_ref,
    front_ref,
    rows_ref,
):
    blocks = (
        x0_ref[...],
        both_zero[0] + x1_one[...] + x1_two[...] + both_three[0],
        both_zero[1] + x2_one[...] + x2_two[...] + both_three[1],
        x3_zero[...] + x3_one[...] + x3_two[...] + x3_three[...],
    )
    for k, x in enumerate(blocks):
        for part in range(6):
            at = BLOCK * k + 128 * part
            piece = x[:, 128 * part : 128 * part + 128]
            wide = jnp.concatenate([piece, jnp.zeros((128 - ROWS, 128), f32)], axis=0)
            front_ref[at : at + 128, :] = wide.T
    rows_ref[...] = jnp.zeros_like(rows_ref)
    for c in range(8):
        for u in range(CELLS):
            rows_ref[64 + u : 65 + u, :] = front_ref[pl.ds(where_ref[CELLS * c + u], 1), :]
        out_ref[c] = rows_ref[...].T[:ROWS]


def second_two_kernel(
    place_ref, acc_ref, sent_ref, f0, f1, f2, f3, cells_ref, weight_ref, out_ref
):
    slabs = [f0[...], f1[...], f2[...], f3[...]]
    solved = (
        acc_ref[...]
        - sent_dot(sent_ref, weight_ref, 1)
        - slabs_dot(slabs, weight_ref, 2, place_ref[1])
    )
    lane = lax.broadcasted_iota(jnp.int32, (ROWS, 128), 1)
    tail = jnp.concatenate([solved[:, 128:], jnp.zeros((ROWS, 64), f32)], axis=1)
    for c in range(8):
        out_ref[c, :, 0:128] = solved[:, 0:128]
        out_ref[c, :, 128:256] = jnp.where(lane < 64, tail, cells_ref[c])


def out_kernel(got_ref, solution_ref, forward_ref):
    for part in range(2):
        wide = got_ref[:, CHUNK * part : CHUNK * part + CHUNK, :].reshape(128, 256)
        forward_ref[part, 0:128, :] = wide[:, 0:128].T
        turned = wide[:, 128:256].T
        forward_ref[part, 128:SLAB, :] = turned[0:64]
        for y in range(4):
            solution_ref[part, y] = turned[64 + 6 * y : 70 + 6 * y]


def plane_send(value, source, target, turn=0):
    pairs = [
        (GROUP * source + q, GROUP * target + (q + turn) % GROUP) for q in range(GROUP)
    ]
    return lax.ppermute(value, "row", pairs)


def plane_spread(value, source, target):
    return [plane_send(value, source, target, d) for d in range(GROUP)]


def after(value, arrived):
    return lax.optimization_barrier((value, arrived))[0]


def on_device(source1, source2, coupling, factor1, factor2, diag_inv, front_order):
    row_id = lax.axis_index("row")
    col_id = lax.axis_index("col")
    place = jnp.stack([row_id // GROUP, row_id % GROUP]).astype(jnp.int32)

    def gather_blocks(turned):
        return lax.all_gather(turned, "col").reshape(8, GROUP - 1, PIECE, 2 * SLAB)

    (turned1,) = call(
        turn_first_kernel,
        [SDS((3 * PIECE, 2 * SLAB), f32)],
        [place, factor1],
        scratch=[pltpu.VMEM((4 * PIECE, 2 * SLAB), f32)],
    )
    matrix1 = gather_blocks(turned1)

    links = jnp.pad(coupling.reshape(2, CELLS), ((0, 0), (0, 32 - CELLS))).reshape(1, 64)
    links = jnp.pad(links, ((0, 0), (0, 64)))
    (packed,) = call(pack_kernel, [SDS((8, 16, 128), f32)], [source1, source2, links])
    packed = lax.all_to_all(packed, "col", 0, 0)
    packed = jnp.broadcast_to(packed[None], (16, 8, 16, 128))
    cells = lax.all_to_all(packed, "row", 0, 0).reshape(128 * 16, 128)

    cell_y = front_order // 48
    cell_x = front_order % 48
    place_of = ((cell_y // 4) * 8 + cell_x // 6) * 16 + (cell_y % 2) * 6 + cell_x % 6
    upper = (cell_y % 4) // 2
    inner = (cell_y % 4) * 6 + cell_x % 6
    every = jnp.stack([place_of, upper, inner])
    own = lax.dynamic_slice_in_dim(every, row_id * SLAB, SLAB, 1)
    every = jnp.concatenate([every[:, :BLOCK], own, jnp.zeros((3, 64), jnp.int32)], axis=1)
    rhs, link = call(
        front_kernel,
        [SDS((64, 1024), f32), SDS((16, 1024), f32)],
        [every[0], cells, every[1:].astype(f32)],
        scratch=[pltpu.VMEM((1024, 128), f32), pltpu.VMEM((1024, 128), f32)],
    )
    factor2, diag_inv, cells = lax.optimization_barrier((factor2, diag_inv, cells))
    turned2 = factor2[:, :, : 3 * PIECE].reshape(2 * SLAB, 3 * PIECE).T
    matrix2 = gather_blocks(turned2)
    inverse = diag_inv.reshape(2 * BLOCK, SLAB).T

    slab_shape = SDS((ROWS, SLAB), f32)
    block_shape = SDS((ROWS, BLOCK), f32)
    pair_shape = SDS((2, ROWS, BLOCK), f32)
    sent_shape = SDS((GROUP, ROWS, SLAB), f32)

    (acc,) = call(start_kernel, [slab_shape], [place, rhs, matrix1])
    got = plane_spread(acc, 1, 2)
    acc, kept = call(
        forward_one_kernel, [slab_shape, sent_shape], [place, acc, *got, matrix1]
    )
    got = plane_spread(acc, 2, 3)
    sent = plane_send(kept, 2, 3)
    acc, part = call(
        forward_two_kernel,
        [slab_shape, block_shape],
        [place, acc, sent, *got, matrix1, inverse],
    )
    got = plane_spread(part, 3, 2)
    x3_two, acc, part = call(
        back_three_kernel,
        [block_shape, slab_shape, block_shape],
        [place, acc, *got, matrix1, inverse],
    )
    got = plane_spread(part, 2, 1)
    x3_one = plane_send(x3_two, 2, 1)
    x3_three = plane_send(after(x3_two, got[1]), 2, 3)
    x2_one, acc, part = call(
        back_two_kernel,
        [block_shape, slab_shape, block_shape],
        [place, acc, *got, x3_one, matrix1, inverse],
    )
    matrix2, part = lax.optimization_barrier((matrix2, part))
    got = plane_spread(part, 1, 0)
    x2_zero = plane_send(x2_one, 1, 0)
    x3_zero = plane_send(x3_three, 3, 0)
    x2_two = plane_send(after(x2_one, got[1]), 1, 2)
    x1_zero, both_zero, part = call(
        back_one_kernel,
        [block_shape, pair_shape, block_shape],
        [place, acc, *got, x2_zero, x3_zero, matrix1, inverse],
    )
    got = plane_spread(part, 0, 1)
    x1_one = plane_send(x1_zero, 0, 1)
    both_three = plane_send(after(both_zero, got[1]), 0, 3)
    x0_one, slab, acc = call(
        couple_kernel,
        [block_shape, slab_shape, slab_shape],
        [place, rhs, link, *got, x1_one, x2_two, x3_three, matrix2],
    )
    got = plane_spread(acc, 1, 2)
    x0_two = plane_send(x0_one, 1, 2)
    x0_zero = plane_send(after(x0_one, got[1]), 1, 0)
    x0_three = plane_send(after(x0_one, got[1]), 1, 3)
    x1_two = plane_send(after(x1_one, got[2]), 1, 2)
    acc, kept, x0_all = call(
        second_one_kernel,
        [slab_shape, sent_shape, block_shape],
        [place, rhs, link, slab, x0_one, x0_two, x0_zero, x0_three, *got, matrix2],
    )
    got = plane_spread(acc, 2, 3)
    sent = plane_send(kept, 2, 3)

    at = jnp.arange(SLAB, dtype=jnp.int32)
    own_c, own_y, own_x = at // CELLS, at % CELLS // 6, at % 6
    own_cells = (row_id * 4 + own_y) * 48 + own_c * 6 + own_x
    hits = front_order[None, :] == own_cells[:, None]
    slots = jnp.sum(jnp.where(hits, jnp.arange(4 * BLOCK, dtype=jnp.int32)[None, :], 0), axis=1)
    (mine,) = call(
        cells_kernel,
        [SDS((8, ROWS, 128), f32)],
        [
            slots,
            x0_all,
            both_zero,
            x1_one,
            x1_two,
            both_three,
            x2_one,
            x2_two,
            x3_zero,
            x3_one,
            x3_two,
            x3_three,
        ],
        scratch=[pltpu.VMEM((4 * BLOCK, 128), f32), pltpu.VMEM((128, 128), f32)],
    )
    (last,) = call(
        second_two_kernel,
        [SDS((8, ROWS, 256), f32)],
        [place, acc, sent, *got, mine, matrix2],
    )
    arrived = lax.all_to_all(last, "col", 0, 0)
    return call(
        out_kernel, [SDS((2, 4, 6, 128), f32), SDS((2, SLAB, 128), f32)], [arrived]
    )


def solution(mesh):
    in_specs = (
        P(None, "row", "col", None),
        P(None, "row", "col", None),
        P(None, "row", "col"),
        P(None, "row", "col"),
        P(None, "row", "col"),
        P(None, None, "row"),
        P(),
    )
    out_specs = (P(None, "row", "col", None), P(None, "row", None))
    return jax.shard_map(
        on_device, mesh=mesh, in_specs=in_specs, out_specs=out_specs, check_vma=False
    )
```

```python
import functools

import jax
import jax.numpy as jnp
from jax import lax
from jax.experimental import pallas as pl
from jax.experimental.pallas import tpu as pltpu
from jax.sharding import PartitionSpec as P

GROUP = 4
CHUNK = 16
ROWS = 2 * CHUNK
SLAB = 192
BLOCK = 768
PIECE = 96
CELLS = 24
VMEM = 16 * 1024 * 1024

SDS = jax.ShapeDtypeStruct
f32 = jnp.float32


def split(value):
    high = value.astype(jnp.bfloat16)
    return high, (value - high.astype(f32)).astype(jnp.bfloat16)


def complex_dot(vector, weight):
    half = weight.shape[1] // 2
    weight_high, weight_low = split(weight)
    high, low = split(vector)
    both = jnp.dot(
        jnp.concatenate([high, low], axis=0), weight_high, preferred_element_type=f32
    )
    total = both[:ROWS] + both[ROWS:] + jnp.dot(high, weight_low, preferred_element_type=f32)
    real = total[:CHUNK, :half] - total[CHUNK:, half:]
    imag = total[:CHUNK, half:] + total[CHUNK:, :half]
    return jnp.concatenate([real, imag], axis=0)


def own_block(block):
    return lambda i, place: (
        0,
        jnp.minimum(jnp.where(place[0] < block, block - 1, block), GROUP - 2),
        0,
        0,
    )


def second_factor(block):
    return lambda i, place: (0, block, 0, 0)


def block_weight(ref):
    return ref[:, 0].reshape(BLOCK, 2 * SLAB)


def slabs_dot(slabs, weight_ref, q, keep=None):
    total = None
    for d, slab in enumerate(slabs):
        source = lax.rem(q - d + GROUP, GROUP)
        if keep is not None:
            keep[source] = slab
        weight = weight_ref[pl.ds(2 * source, 2), 0].reshape(SLAB, 2 * SLAB)
        part = complex_dot(slab, weight)
        total = part if total is None else total + part
    return total


def sent_dot(sent_ref, weight_ref):
    total = None
    for s in range(GROUP):
        weight = weight_ref[2 * s : 2 * s + 2, 0].reshape(SLAB, 2 * SLAB)
        part = complex_dot(sent_ref[s], weight)
        total = part if total is None else total + part
    return total


def add_refs(refs):
    total = refs[0][...]
    for ref in refs[1:]:
        total = total + ref[...]
    return total


def call(body, out_shape, scalars, inputs, blocks=(), scratch=()):
    def whole(shape):
        return pl.BlockSpec(
            shape, lambda i, place, n=len(shape): (0,) * n, pipeline_mode=pl.Buffered(1)
        )

    specs = [whole(value.shape) for value in inputs]
    for _, at in blocks:
        specs.append(
            pl.BlockSpec((8, 1, PIECE, 2 * SLAB), at, pipeline_mode=pl.Buffered(1))
        )
    return pl.pallas_call(
        body,
        grid_spec=pltpu.PrefetchScalarGridSpec(
            num_scalar_prefetch=1,
            grid=(1,),
            in_specs=specs,
            out_specs=tuple(whole(shape.shape) for shape in out_shape),
            scratch_shapes=scratch,
        ),
        out_shape=tuple(out_shape),
        compiler_params=pltpu.CompilerParams(vmem_limit_bytes=VMEM),
    )(scalars, *inputs, *[array for array, _ in blocks])


def turn_first_kernel(place_ref, factor_ref, out_ref, turned_ref):
    rows = factor_ref[...].reshape(2 * SLAB, 4 * PIECE)
    for part in range(3):
        turned_ref[128 * part : 128 * part + 128, :] = rows[:, 128 * part : 128 * part + 128].T
    for slot in range(GROUP - 1):
        block = slot + jnp.where(place_ref[0] > slot, 0, 1)
        out_ref[PIECE * slot : PIECE * slot + PIECE, :] = turned_ref[pl.ds(block * PIECE, PIECE), :]


def pack_kernel(place_ref, first_ref, second_ref, link_ref, out_ref):
    lane = lax.broadcasted_iota(jnp.int32, (6, 128), 1)
    for y in range(2):
        parts = []
        for half in range(2):
            for ref in (first_ref, second_ref):
                parts += [ref[0, y + 2 * half], ref[1, y + 2 * half]]
        for c in range(8):
            row = jnp.zeros((6, 128), f32)
            for at, part in enumerate(parts):
                shift = (16 * at - 16 * c) % 128
                moved = pltpu.roll(part, shift, 1) if shift else part
                row = jnp.where((lane >= 16 * at) & (lane < 16 * at + 16), moved, row)
            out_ref[c, 6 * y : 6 * y + 6, :] = row
    for c in range(8):
        out_ref[c, 12:16, :] = jnp.broadcast_to(link_ref[...], (4, 128))


def front_kernel(where_ref, cells_ref, mark_ref, rhs_ref, link_ref, rows_ref, links_ref):
    def some(step, carry):
        for u in range(16):
            at = step * 16 + u
            source = where_ref[at]
            rows_ref[pl.ds(at, 1), :] = cells_ref[pl.ds(source, 1), :]
            links_ref[pl.ds(at, 1), :] = cells_ref[pl.ds(where_ref[1024 + at], 1), :]
        return carry

    lax.fori_loop(0, 64, some, 0)
    lane = lax.broadcasted_iota(jnp.int32, (32, 128), 0).astype(f32)
    for part in range(8):
        at = slice(128 * part, 128 * part + 128)
        turned = rows_ref[at, :].T
        upper = mark_ref[0:1, at] > 0.5
        rhs_ref[:, at] = jnp.where(upper, turned[64:128], turned[0:64])
        turned = links_ref[at, :].T
        own = mark_ref[1:2, at] == lane
        real = jnp.sum(jnp.where(own, turned[0:32], 0.0), axis=0, keepdims=True)
        imag = jnp.sum(jnp.where(own, turned[32:64], 0.0), axis=0, keepdims=True)
        link_ref[0:8, at] = jnp.broadcast_to(real, (8, 128))
        link_ref[8:16, at] = jnp.broadcast_to(imag, (8, 128))


def start_kernel(place_ref, rhs_ref, weight_ref, acc_ref):
    product = complex_dot(rhs_ref[0:ROWS, 0:BLOCK], block_weight(weight_ref))
    slab = rhs_ref[0:ROWS, BLOCK : BLOCK + SLAB]
    acc_ref[...] = jnp.where(place_ref[0] > 0, slab - product, slab)


def forward_one_kernel(place_ref, acc_ref, y0, y1, y2, y3, weight_ref, out_ref, keep_ref):
    slabs = [y0[...], y1[...], y2[...], y3[...]]
    out_ref[...] = acc_ref[...] - slabs_dot(slabs, weight_ref, place_ref[1], keep_ref)


def forward_two_kernel(
    place_ref, acc_ref, inverse_ref, sent_ref, y0, y1, y2, y3, weight1_ref, weight2_ref, out_ref, part_ref
):
    slabs = [y0[...], y1[...], y2[...], y3[...]]
    solved = (
        acc_ref[...]
        - sent_dot(sent_ref, weight1_ref)
        - slabs_dot(slabs, weight2_ref, place_ref[1])
    )
    out_ref[...] = solved
    part_ref[...] = complex_dot(solved, inverse_ref[...])


def back_three_kernel(
    place_ref, acc_ref, inverse_ref, p0, p1, p2, p3, weight_ref, x_ref, acc_out_ref, part_ref
):
    x = add_refs([p0, p1, p2, p3])
    acc = acc_ref[...] - complex_dot(x, block_weight(weight_ref))
    x_ref[...] = x
    acc_out_ref[...] = acc
    part_ref[...] = complex_dot(acc, inverse_ref[...])


def back_two_kernel(
    place_ref,
    acc_ref,
    inverse_ref,
    p0,
    p1,
    p2,
    p3,
    x3_ref,
    weight2_ref,
    weight3_ref,
    x_ref,
    acc_out_ref,
    part_ref,
):
    x = add_refs([p0, p1, p2, p3])
    acc = (
        acc_ref[...]
        - complex_dot(x3_ref[...], block_weight(weight3_ref))
        - complex_dot(x, block_weight(weight2_ref))
    )
    x_ref[...] = x
    acc_out_ref[...] = acc
    part_ref[...] = complex_dot(acc, inverse_ref[...])


def back_one_kernel(
    place_ref,
    acc_ref,
    inverse_ref,
    p0,
    p1,
    p2,
    p3,
    x2_ref,
    x3_ref,
    weight1_ref,
    weight2_ref,
    weight3_ref,
    x_ref,
    both_ref,
    part_ref,
):
    x = add_refs([p0, p1, p2, p3])
    acc = (
        acc_ref[...]
        - complex_dot(x3_ref[...], block_weight(weight3_ref))
        - complex_dot(x2_ref[...], block_weight(weight2_ref))
        - complex_dot(x, block_weight(weight1_ref))
    )
    part_ref[...] = complex_dot(acc, inverse_ref[...])
    x_ref[...] = x
    both_ref[0] = x
    both_ref[1] = x2_ref[...]


def coupled(rhs, link_real, link_imag, x):
    real = rhs[:CHUNK] - (link_real * x[:CHUNK] - link_imag * x[CHUNK:])
    imag = rhs[CHUNK:] - (link_real * x[CHUNK:] + link_imag * x[:CHUNK])
    return jnp.concatenate([real, imag], axis=0)


def second_block(rhs_ref, link_ref, x):
    return coupled(
        rhs_ref[ROWS : 2 * ROWS, 0:BLOCK], link_ref[0:1, 0:BLOCK], link_ref[8:9, 0:BLOCK], x
    )


def second_slab(rhs_ref, link_ref, x, q):
    own = x[:, 0:SLAB]
    for s in range(1, GROUP):
        own = jnp.where(q == s, x[:, SLAB * s : SLAB * s + SLAB], own)
    end = BLOCK + SLAB
    return coupled(
        rhs_ref[ROWS : 2 * ROWS, BLOCK:end], link_ref[0:1, BLOCK:end], link_ref[8:9, BLOCK:end], own
    )


def couple_kernel(
    place_ref, rhs_ref, link_ref, p0, p1, p2, p3, x1_ref, weight_ref, x0_ref, out_ref
):
    x0 = add_refs([p0, p1, p2, p3])
    x0_ref[...] = x0
    slab = second_slab(rhs_ref, link_ref, x1_ref[...], place_ref[1])
    out_ref[...] = slab - complex_dot(
        second_block(rhs_ref, link_ref, x0), block_weight(weight_ref)
    )


def second_one_kernel(
    place_ref,
    rhs_ref,
    link_ref,
    acc_ref,
    x0_ref,
    x2_ref,
    f0,
    f1,
    f2,
    f3,
    weight0_ref,
    weight1_ref,
    out_ref,
    keep_ref,
):
    q = place_ref[1]
    slab = second_slab(rhs_ref, link_ref, x2_ref[...], q)
    product = complex_dot(second_block(rhs_ref, link_ref, x0_ref[...]), block_weight(weight0_ref))
    slabs = [f0[...], f1[...], f2[...], f3[...]]
    solved = slab - product - slabs_dot(slabs, weight1_ref, q, keep_ref)
    out_ref[...] = jnp.where(place_ref[0] == 1, acc_ref[...], solved)


def second_base_kernel(
    place_ref, rhs_ref, link_ref, acc_ref, x0_zero, x0_three, x3_ref, weight_ref, out_ref
):
    plane, q = place_ref[0], place_ref[1]
    x0 = x0_zero[...] + x0_three[...]
    own = jnp.where(plane == 0, x0, x3_ref[...])
    slab = second_slab(rhs_ref, link_ref, own, q)
    product = complex_dot(second_block(rhs_ref, link_ref, x0), block_weight(weight_ref))
    out_ref[...] = jnp.where(
        plane == 0, slab, jnp.where(plane == 3, slab - product, acc_ref[...])
    )


def cells_kernel(
    where_ref,
    x0_one,
    x0_two,
    x0_zero,
    x0_three,
    both_zero,
    x1_one,
    x1_two,
    both_three,
    x2_one,
    x2_two,
    x3_zero,
    x3_one,
    x3_two,
    x3_three,
    out_ref,
    front_ref,
    rows_ref,
):
    blocks = (
        x0_one[...] + x0_two[...] + x0_zero[...] + x0_three[...],
        both_zero[0] + x1_one[...] + x1_two[...] + both_three[0],
        both_zero[1] + x2_one[...] + x2_two[...] + both_three[1],
        x3_zero[...] + x3_one[...] + x3_two[...] + x3_three[...],
    )
    for k, x in enumerate(blocks):
        for part in range(6):
            at = BLOCK * k + 128 * part
            piece = x[:, 128 * part : 128 * part + 128]
            wide = jnp.concatenate([piece, jnp.zeros((128 - ROWS, 128), f32)], axis=0)
            front_ref[at : at + 128, :] = wide.T
    rows_ref[...] = jnp.zeros_like(rows_ref)
    for c in range(8):
        for u in range(CELLS):
            rows_ref[64 + u : 65 + u, :] = front_ref[pl.ds(where_ref[CELLS * c + u], 1), :]
        out_ref[c] = rows_ref[...].T[:ROWS]


def second_two_kernel(
    place_ref, acc_ref, cells_ref, sent_ref, f0, f1, f2, f3, weight1_ref, weight2_ref, out_ref
):
    slabs = [f0[...], f1[...], f2[...], f3[...]]
    solved = (
        acc_ref[...]
        - sent_dot(sent_ref, weight1_ref)
        - slabs_dot(slabs, weight2_ref, place_ref[1])
    )
    lane = lax.broadcasted_iota(jnp.int32, (ROWS, 128), 1)
    tail = jnp.concatenate([solved[:, 128:], jnp.zeros((ROWS, 64), f32)], axis=1)
    for c in range(8):
        out_ref[c, :, 0:128] = solved[:, 0:128]
        out_ref[c, :, 128:256] = jnp.where(lane < 64, tail, cells_ref[c])


def out_kernel(place_ref, got_ref, solution_ref, forward_ref):
    for part in range(2):
        wide = got_ref[:, CHUNK * part : CHUNK * part + CHUNK, :].reshape(128, 256)
        forward_ref[part, 0:128, :] = wide[:, 0:128].T
        turned = wide[:, 128:256].T
        forward_ref[part, 128:SLAB, :] = turned[0:64]
        for y in range(4):
            solution_ref[part, y] = turned[64 + 6 * y : 70 + 6 * y]


def plane_send(value, source, target, turn=0):
    pairs = [
        (GROUP * source + q, GROUP * target + (q + turn) % GROUP) for q in range(GROUP)
    ]
    return lax.ppermute(value, "row", pairs)


def plane_spread(value, source, target):
    return [plane_send(value, source, target, d) for d in range(GROUP)]


def after(value, arrived):
    return lax.optimization_barrier((value, arrived))[0]


def on_device(source1, source2, coupling, factor1, factor2, diag_inv, front_order):
    row_id = lax.axis_index("row")
    col_id = lax.axis_index("col")
    place = jnp.stack([row_id // GROUP, row_id % GROUP]).astype(jnp.int32)

    def gather_blocks(turned):
        return lax.all_gather(turned, "col").reshape(8, GROUP - 1, PIECE, 2 * SLAB)

    (turned1,) = call(
        turn_first_kernel,
        [SDS((3 * PIECE, 2 * SLAB), f32)],
        place,
        [factor1],
        scratch=[pltpu.VMEM((4 * PIECE, 2 * SLAB), f32)],
    )
    matrix1 = gather_blocks(turned1)

    links = jnp.pad(coupling.reshape(2, CELLS), ((0, 0), (0, 32 - CELLS))).reshape(1, 64)
    links = jnp.pad(links, ((0, 0), (0, 64)))
    (packed,) = call(
        pack_kernel, [SDS((8, 16, 128), f32)], place, [source1, source2, links]
    )
    packed = lax.all_to_all(packed, "col", 0, 0)
    packed = jnp.broadcast_to(packed[:, :13].reshape(1, 104, 128), (16, 104, 128))
    cells = lax.all_to_all(packed, "row", 0, 0).reshape(16 * 104, 128)

    cell_y = front_order // 48
    cell_x = front_order % 48
    group_of = (cell_y // 4) * 104 + (cell_x // 6) * 13
    place_of = group_of + (cell_y % 2) * 6 + cell_x % 6
    upper = (cell_y % 4) // 2
    inner = (cell_y % 4) * 6 + cell_x % 6
    every = jnp.stack([place_of, group_of + 12, upper, inner])
    own = lax.dynamic_slice_in_dim(every, row_id * SLAB, SLAB, 1)
    every = jnp.concatenate([every[:, :BLOCK], own, jnp.zeros((4, 64), jnp.int32)], axis=1)
    rhs, link = call(
        front_kernel,
        [SDS((64, 1024), f32), SDS((16, 1024), f32)],
        every[:2].reshape(2048),
        [cells, every[2:].astype(f32)],
        scratch=[pltpu.VMEM((1024, 128), f32), pltpu.VMEM((1024, 128), f32)],
    )
    factor2, diag_inv, cells = lax.optimization_barrier((factor2, diag_inv, cells))
    turned2 = factor2[:, :, : 3 * PIECE].reshape(2 * SLAB, 3 * PIECE).T
    matrix2 = gather_blocks(turned2)
    inverse = diag_inv.reshape(2 * BLOCK, SLAB).T

    slab_shape = SDS((ROWS, SLAB), f32)
    block_shape = SDS((ROWS, BLOCK), f32)
    pair_shape = SDS((2, ROWS, BLOCK), f32)
    sent_shape = SDS((GROUP, ROWS, SLAB), f32)

    def first_blocks(*blocks):
        return [(matrix1, own_block(block)) for block in blocks]

    (acc,) = call(start_kernel, [slab_shape], place, [rhs], first_blocks(0))
    got = plane_spread(acc, 1, 2)
    acc, kept = call(
        forward_one_kernel, [slab_shape, sent_shape], place, [acc, *got], first_blocks(1)
    )
    got = plane_spread(acc, 2, 3)
    sent = plane_send(kept, 2, 3)
    acc, part = call(
        forward_two_kernel,
        [slab_shape, block_shape],
        place,
        [acc, inverse, sent, *got],
        first_blocks(1, 2),
    )
    got = plane_spread(part, 3, 2)
    x3_two, acc, part = call(
        back_three_kernel,
        [block_shape, slab_shape, block_shape],
        place,
        [acc, inverse, *got],
        first_blocks(3),
    )
    got = plane_spread(part, 2, 1)
    x3_one = plane_send(x3_two, 2, 1)
    x3_three = plane_send(after(x3_two, got[1]), 2, 3)
    x3_zero = plane_send(after(x3_two, got[1]), 2, 0)
    x2_one, acc, part = call(
        back_two_kernel,
        [block_shape, slab_shape, block_shape],
        place,
        [acc, inverse, *got, x3_one],
        first_blocks(2, 3),
    )
    matrix2, part = lax.optimization_barrier((matrix2, part))

    def second_blocks(*blocks):
        return [(matrix2, second_factor(block)) for block in blocks]

    got = plane_spread(part, 1, 0)
    x2_zero = plane_send(x2_one, 1, 0)
    x2_two = plane_send(after(x2_one, got[1]), 1, 2)
    x1_zero, both_zero, part = call(
        back_one_kernel,
        [block_shape, pair_shape, block_shape],
        place,
        [acc, inverse, *got, x2_zero, x3_zero],
        first_blocks(1, 2, 3),
    )
    got = plane_spread(part, 0, 1)
    x1_one = plane_send(x1_zero, 0, 1)
    x0_one, acc = call(
        couple_kernel,
        [block_shape, slab_shape],
        place,
        [rhs, link, *got, x1_one],
        second_blocks(0),
    )
    got = plane_spread(acc, 1, 2)
    x0_two = plane_send(x0_one, 1, 2)
    x0_zero = plane_send(after(x0_one, got[1]), 1, 0)
    x0_three = plane_send(after(x0_one, got[1]), 1, 3)
    both_three = plane_send(after(both_zero, got[1]), 0, 3)
    acc, kept = call(
        second_one_kernel,
        [slab_shape, sent_shape],
        place,
        [rhs, link, acc, x0_two, x2_two, *got],
        second_blocks(0, 1),
    )
    got = plane_spread(acc, 2, 3)
    sent = plane_send(kept, 2, 3)
    x1_two = plane_send(after(x1_one, got[1]), 1, 2)
    (acc,) = call(
        second_base_kernel,
        [slab_shape],
        place,
        [rhs, link, acc, x0_zero, x0_three, x3_three],
        second_blocks(0),
    )

    at = jnp.arange(SLAB, dtype=jnp.int32)
    own_c, own_y, own_x = at // CELLS, at % CELLS // 6, at % 6
    own_cells = (row_id * 4 + own_y) * 48 + own_c * 6 + own_x
    hits = front_order[None, :] == own_cells[:, None]
    slots = jnp.sum(jnp.where(hits, jnp.arange(4 * BLOCK, dtype=jnp.int32)[None, :], 0), axis=1)
    (mine,) = call(
        cells_kernel,
        [SDS((8, ROWS, 128), f32)],
        slots,
        [
            x0_one,
            x0_two,
            x0_zero,
            x0_three,
            both_zero,
            x1_one,
            x1_two,
            both_three,
            x2_one,
            x2_two,
            x3_zero,
            x3_one,
            x3_two,
            x3_three,
        ],
        scratch=[pltpu.VMEM((4 * BLOCK, 128), f32), pltpu.VMEM((128, 128), f32)],
    )
    (last,) = call(
        second_two_kernel,
        [SDS((8, ROWS, 256), f32)],
        place,
        [acc, mine, sent, *got],
        second_blocks(1, 2),
    )
    arrived = lax.all_to_all(last, "col", 0, 0)
    return call(
        out_kernel,
        [SDS((2, 4, 6, 128), f32), SDS((2, SLAB, 128), f32)],
        place,
        [arrived],
    )


def solution(mesh):
    in_specs = (
        P(None, "row", "col", None),
        P(None, "row", "col", None),
        P(None, "row", "col"),
        P(None, "row", "col"),
        P(None, "row", "col"),
        P(None, None, "row"),
        P(),
    )
    out_specs = (P(None, "row", "col", None), P(None, "row", None))
    return jax.shard_map(
        on_device, mesh=mesh, in_specs=in_specs, out_specs=out_specs, check_vma=False
    )
```

```python
import functools

import jax
import jax.numpy as jnp
from jax import lax
from jax.experimental import pallas as pl
from jax.experimental.pallas import tpu as pltpu
from jax.sharding import PartitionSpec as P

GROUP = 4
CHUNK = 16
ROWS = 2 * CHUNK
SLAB = 192
BLOCK = 768
PIECE = 96
CELLS = 24
VMEM = 16 * 1024 * 1024

SDS = jax.ShapeDtypeStruct
f32 = jnp.float32


def split(value):
    high = value.astype(jnp.bfloat16)
    return high, (value - high.astype(f32)).astype(jnp.bfloat16)


def complex_dot(vector, weight):
    half = weight.shape[1] // 2
    weight_high, weight_low = split(weight)
    high, low = split(vector)
    both = jnp.dot(
        jnp.concatenate([high, low], axis=0), weight_high, preferred_element_type=f32
    )
    total = both[:ROWS] + both[ROWS:] + jnp.dot(high, weight_low, preferred_element_type=f32)
    real = total[:CHUNK, :half] - total[CHUNK:, half:]
    imag = total[:CHUNK, half:] + total[CHUNK:, :half]
    return jnp.concatenate([real, imag], axis=0)


def own_block(block):
    return lambda i, place: (
        0,
        jnp.minimum(jnp.where(place[0] < block, block - 1, block), GROUP - 2),
        0,
        0,
    )


def second_factor(block):
    return lambda i, place: (0, block, 0, 0)


def block_weight(ref):
    return ref[:, 0].reshape(BLOCK, 2 * SLAB)


def slabs_dot(slabs, weight_ref, q, keep=None):
    total = None
    for d, slab in enumerate(slabs):
        source = lax.rem(q - d + GROUP, GROUP)
        if keep is not None:
            keep[source] = slab
        weight = weight_ref[pl.ds(2 * source, 2), 0].reshape(SLAB, 2 * SLAB)
        part = complex_dot(slab, weight)
        total = part if total is None else total + part
    return total


def sent_dot(sent_ref, weight_ref):
    total = None
    for s in range(GROUP):
        weight = weight_ref[2 * s : 2 * s + 2, 0].reshape(SLAB, 2 * SLAB)
        part = complex_dot(sent_ref[s], weight)
        total = part if total is None else total + part
    return total


def add_refs(refs):
    total = refs[0][...]
    for ref in refs[1:]:
        total = total + ref[...]
    return total


def call(body, out_shape, scalars, inputs, blocks=(), scratch=()):
    vmem = pl.BlockSpec(memory_space=pltpu.VMEM)
    specs = [vmem] * len(inputs)
    for _, at in blocks:
        specs.append(
            pl.BlockSpec((8, 1, PIECE, 2 * SLAB), at, pipeline_mode=pl.Buffered(1))
        )
    near = [pltpu.with_memory_space_constraint(value, pltpu.VMEM) for value in inputs]
    far = [pltpu.with_memory_space_constraint(array, pltpu.HBM) for array, _ in blocks]
    return pl.pallas_call(
        body,
        grid_spec=pltpu.PrefetchScalarGridSpec(
            num_scalar_prefetch=1,
            grid=(1,),
            in_specs=specs,
            out_specs=(vmem,) * len(out_shape),
            scratch_shapes=scratch,
        ),
        out_shape=tuple(pltpu.VMEM(shape.shape, shape.dtype) for shape in out_shape),
        compiler_params=pltpu.CompilerParams(vmem_limit_bytes=VMEM),
    )(scalars, *near, *far)


def turn_first_kernel(place_ref, factor_ref, out_ref, turned_ref):
    rows = factor_ref[...].reshape(2 * SLAB, 4 * PIECE)
    for part in range(3):
        turned_ref[128 * part : 128 * part + 128, :] = rows[:, 128 * part : 128 * part + 128].T
    for slot in range(GROUP - 1):
        block = slot + jnp.where(place_ref[0] > slot, 0, 1)
        out_ref[PIECE * slot : PIECE * slot + PIECE, :] = turned_ref[pl.ds(block * PIECE, PIECE), :]


def pack_kernel(place_ref, first_ref, second_ref, link_ref, out_ref):
    lane = lax.broadcasted_iota(jnp.int32, (6, 128), 1)
    for y in range(2):
        parts = []
        for half in range(2):
            for ref in (first_ref, second_ref):
                parts += [ref[0, y + 2 * half], ref[1, y + 2 * half]]
        for c in range(8):
            row = jnp.zeros((6, 128), f32)
            for at, part in enumerate(parts):
                shift = (16 * at - 16 * c) % 128
                moved = pltpu.roll(part, shift, 1) if shift else part
                row = jnp.where((lane >= 16 * at) & (lane < 16 * at + 16), moved, row)
            out_ref[c, 6 * y : 6 * y + 6, :] = row
    for c in range(8):
        out_ref[c, 12:16, :] = jnp.broadcast_to(link_ref[...], (4, 128))


def front_kernel(where_ref, cells_ref, mark_ref, rhs_ref, link_ref, rows_ref, links_ref):
    def some(step, carry):
        for u in range(16):
            at = step * 16 + u
            source = where_ref[at]
            rows_ref[pl.ds(at, 1), :] = cells_ref[pl.ds(source, 1), :]
            links_ref[pl.ds(at, 1), :] = cells_ref[pl.ds(where_ref[1024 + at], 1), :]
        return carry

    lax.fori_loop(0, 64, some, 0)
    lane = lax.broadcasted_iota(jnp.int32, (32, 128), 0).astype(f32)
    for part in range(8):
        at = slice(128 * part, 128 * part + 128)
        turned = rows_ref[at, :].T
        upper = mark_ref[0:1, at] > 0.5
        rhs_ref[:, at] = jnp.where(upper, turned[64:128], turned[0:64])
        turned = links_ref[at, :].T
        own = mark_ref[1:2, at] == lane
        real = jnp.sum(jnp.where(own, turned[0:32], 0.0), axis=0, keepdims=True)
        imag = jnp.sum(jnp.where(own, turned[32:64], 0.0), axis=0, keepdims=True)
        link_ref[0:8, at] = jnp.broadcast_to(real, (8, 128))
        link_ref[8:16, at] = jnp.broadcast_to(imag, (8, 128))


def start_kernel(place_ref, rhs_ref, weight_ref, acc_ref):
    product = complex_dot(rhs_ref[0:ROWS, 0:BLOCK], block_weight(weight_ref))
    slab = rhs_ref[0:ROWS, BLOCK : BLOCK + SLAB]
    acc_ref[...] = jnp.where(place_ref[0] > 0, slab - product, slab)


def forward_one_kernel(place_ref, acc_ref, y0, y1, y2, y3, weight_ref, out_ref, keep_ref):
    slabs = [y0[...], y1[...], y2[...], y3[...]]
    out_ref[...] = acc_ref[...] - slabs_dot(slabs, weight_ref, place_ref[1], keep_ref)


def forward_two_kernel(
    place_ref, acc_ref, inverse_ref, sent_ref, y0, y1, y2, y3, weight1_ref, weight2_ref, out_ref, part_ref
):
    slabs = [y0[...], y1[...], y2[...], y3[...]]
    solved = (
        acc_ref[...]
        - sent_dot(sent_ref, weight1_ref)
        - slabs_dot(slabs, weight2_ref, place_ref[1])
    )
    out_ref[...] = solved
    part_ref[...] = complex_dot(solved, inverse_ref[...])


def back_three_kernel(
    place_ref, acc_ref, inverse_ref, p0, p1, p2, p3, weight_ref, x_ref, acc_out_ref, part_ref
):
    x = add_refs([p0, p1, p2, p3])
    acc = acc_ref[...] - complex_dot(x, block_weight(weight_ref))
    x_ref[...] = x
    acc_out_ref[...] = acc
    part_ref[...] = complex_dot(acc, inverse_ref[...])


def back_two_kernel(
    place_ref,
    acc_ref,
    inverse_ref,
    p0,
    p1,
    p2,
    p3,
    x3_ref,
    weight2_ref,
    weight3_ref,
    both_ref,
    acc_out_ref,
    part_ref,
):
    x = add_refs([p0, p1, p2, p3])
    acc = (
        acc_ref[...]
        - complex_dot(x3_ref[...], block_weight(weight3_ref))
        - complex_dot(x, block_weight(weight2_ref))
    )
    both_ref[0] = x
    both_ref[1] = x3_ref[...]
    acc_out_ref[...] = acc
    part_ref[...] = complex_dot(acc, inverse_ref[...])


def back_one_kernel(
    place_ref,
    acc_ref,
    inverse_ref,
    p0,
    p1,
    p2,
    p3,
    later_ref,
    x2_ref,
    x3_ref,
    weight1_ref,
    weight2_ref,
    weight3_ref,
    newest_ref,
    both_ref,
    part_ref,
):
    x = add_refs([p0, p1, p2, p3])
    acc = (
        acc_ref[...]
        - complex_dot(later_ref[1], block_weight(weight3_ref))
        - complex_dot(later_ref[0], block_weight(weight2_ref))
        - complex_dot(x, block_weight(weight1_ref))
    )
    part_ref[...] = complex_dot(acc, inverse_ref[...])
    newest_ref[...] = x + x2_ref[0] + x3_ref[...]
    both_ref[0] = x
    both_ref[1] = later_ref[0]


def coupled(rhs, link_real, link_imag, x):
    real = rhs[:CHUNK] - (link_real * x[:CHUNK] - link_imag * x[CHUNK:])
    imag = rhs[CHUNK:] - (link_real * x[CHUNK:] + link_imag * x[:CHUNK])
    return jnp.concatenate([real, imag], axis=0)


def second_block(rhs_ref, link_ref, x):
    return coupled(
        rhs_ref[ROWS : 2 * ROWS, 0:BLOCK], link_ref[0:1, 0:BLOCK], link_ref[8:9, 0:BLOCK], x
    )


def second_slab(rhs_ref, link_ref, x, q):
    own = x[:, 0:SLAB]
    for s in range(1, GROUP):
        own = jnp.where(q == s, x[:, SLAB * s : SLAB * s + SLAB], own)
    end = BLOCK + SLAB
    return coupled(
        rhs_ref[ROWS : 2 * ROWS, BLOCK:end], link_ref[0:1, BLOCK:end], link_ref[8:9, BLOCK:end], own
    )


def couple_kernel(
    place_ref, rhs_ref, link_ref, p0, p1, p2, p3, own_ref, zero_ref, weight_ref, pass_ref, out_ref
):
    x0 = add_refs([p0, p1, p2, p3])
    slab = second_slab(rhs_ref, link_ref, own_ref[...], place_ref[1])
    out_ref[...] = slab - complex_dot(
        second_block(rhs_ref, link_ref, x0), block_weight(weight_ref)
    )
    zero = place_ref[0] == 0
    pass_ref[0] = jnp.where(zero, zero_ref[0], x0)
    pass_ref[1] = jnp.where(zero, zero_ref[1], own_ref[...])


def second_one_kernel(
    place_ref,
    rhs_ref,
    link_ref,
    acc_ref,
    own_ref,
    sent_ref,
    got_ref,
    f0,
    f1,
    f2,
    f3,
    weight0_ref,
    weight1_ref,
    out_ref,
    keep_ref,
):
    plane, q = place_ref[0], place_ref[1]
    x0 = jnp.where(plane == 1, sent_ref[0], got_ref[0])
    for s in range(GROUP):
        keep_ref[GROUP + s] = x0[:, SLAB * s : SLAB * s + SLAB]
    slab = second_slab(rhs_ref, link_ref, own_ref[...], q)
    product = complex_dot(second_block(rhs_ref, link_ref, x0), block_weight(weight0_ref))
    slabs = [f0[...], f1[...], f2[...], f3[...]]
    solved = slab - product - slabs_dot(slabs, weight1_ref, q, keep_ref)
    out_ref[...] = jnp.where(plane == 1, acc_ref[...], solved)


def joined(ref, first):
    return jnp.concatenate([ref[first + s] for s in range(GROUP)], axis=1)


def second_base_kernel(
    place_ref, rhs_ref, link_ref, acc_ref, got_ref, own_ref, weight_ref, out_ref
):
    plane, q = place_ref[0], place_ref[1]
    x0 = joined(got_ref, GROUP)
    own = jnp.where(plane == 0, x0, own_ref[...])
    slab = second_slab(rhs_ref, link_ref, own, q)
    product = complex_dot(second_block(rhs_ref, link_ref, x0), block_weight(weight_ref))
    out_ref[...] = jnp.where(
        plane == 0, slab, jnp.where(plane == 3, slab - product, acc_ref[...])
    )


def cells_kernel(
    where_ref, got_ref, pass_ref, passed_ref, newest_ref, own_ref, both_zero, later_ref, x3_one, out_ref, front_ref, rows_ref
):
    plane = where_ref[SLAB]

    def pick(*by_plane):
        value = by_plane[0]
        for at in range(1, GROUP):
            value = jnp.where(plane == at, by_plane[at], value)
        return value

    last = joined(got_ref, GROUP)
    blocks = (
        pick(last, pass_ref[0], passed_ref[0], last),
        pick(newest_ref[...], own_ref[...], passed_ref[1], passed_ref[0]),
        pick(both_zero[1], newest_ref[...], own_ref[...], passed_ref[1]),
        pick(later_ref[1], x3_one[...], newest_ref[...], own_ref[...]),
    )
    for k, x in enumerate(blocks):
        for part in range(6):
            at = BLOCK * k + 128 * part
            piece = x[:, 128 * part : 128 * part + 128]
            wide = jnp.concatenate([piece, jnp.zeros((128 - ROWS, 128), f32)], axis=0)
            front_ref[at : at + 128, :] = wide.T
    rows_ref[...] = jnp.zeros_like(rows_ref)
    for c in range(8):
        for u in range(CELLS):
            rows_ref[64 + u : 65 + u, :] = front_ref[pl.ds(where_ref[CELLS * c + u], 1), :]
        out_ref[c] = rows_ref[...].T[:ROWS]


def second_two_kernel(
    place_ref, acc_ref, cells_ref, sent_ref, f0, f1, f2, f3, weight1_ref, weight2_ref, out_ref
):
    slabs = [f0[...], f1[...], f2[...], f3[...]]
    solved = (
        acc_ref[...]
        - sent_dot(sent_ref, weight1_ref)
        - slabs_dot(slabs, weight2_ref, place_ref[1])
    )
    lane = lax.broadcasted_iota(jnp.int32, (ROWS, 128), 1)
    tail = jnp.concatenate([solved[:, 128:], jnp.zeros((ROWS, 64), f32)], axis=1)
    for c in range(8):
        out_ref[c, :, 0:128] = solved[:, 0:128]
        out_ref[c, :, 128:256] = jnp.where(lane < 64, tail, cells_ref[c])


def out_kernel(place_ref, got_ref, solution_ref, forward_ref):
    for part in range(2):
        wide = got_ref[:, CHUNK * part : CHUNK * part + CHUNK, :].reshape(128, 256)
        forward_ref[part, 0:128, :] = wide[:, 0:128].T
        turned = wide[:, 128:256].T
        forward_ref[part, 128:SLAB, :] = turned[0:64]
        for y in range(4):
            solution_ref[part, y] = turned[64 + 6 * y : 70 + 6 * y]


def plane_send(value, *moves, turn=0):
    pairs = [
        (GROUP * source + q, GROUP * target + (q + turn) % GROUP)
        for source, target in moves
        for q in range(GROUP)
    ]
    return lax.ppermute(value, "row", pairs)


def plane_spread(value, source, target):
    return [plane_send(value, (source, target), turn=d) for d in range(GROUP)]


def on_device(source1, source2, coupling, factor1, factor2, diag_inv, front_order):
    row_id = lax.axis_index("row")
    col_id = lax.axis_index("col")
    place = jnp.stack([row_id // GROUP, row_id % GROUP]).astype(jnp.int32)

    def gather_blocks(turned):
        return lax.all_gather(turned, "col").reshape(8, GROUP - 1, PIECE, 2 * SLAB)

    (turned1,) = call(
        turn_first_kernel,
        [SDS((3 * PIECE, 2 * SLAB), f32)],
        place,
        [factor1],
        scratch=[pltpu.VMEM((4 * PIECE, 2 * SLAB), f32)],
    )
    matrix1 = gather_blocks(turned1)

    links = jnp.pad(coupling.reshape(2, CELLS), ((0, 0), (0, 32 - CELLS))).reshape(1, 64)
    links = jnp.pad(links, ((0, 0), (0, 64)))
    (packed,) = call(
        pack_kernel, [SDS((8, 16, 128), f32)], place, [source1, source2, links]
    )
    packed = lax.all_to_all(packed, "col", 0, 0)
    packed = jnp.broadcast_to(packed[:, :13].reshape(1, 104, 128), (16, 104, 128))
    cells = lax.all_to_all(packed, "row", 0, 0).reshape(16 * 104, 128)

    cell_y = front_order // 48
    cell_x = front_order % 48
    group_of = (cell_y // 4) * 104 + (cell_x // 6) * 13
    place_of = group_of + (cell_y % 2) * 6 + cell_x % 6
    upper = (cell_y % 4) // 2
    inner = (cell_y % 4) * 6 + cell_x % 6
    every = jnp.stack([place_of, group_of + 12, upper, inner])
    own = lax.dynamic_slice_in_dim(every, row_id * SLAB, SLAB, 1)
    every = jnp.concatenate([every[:, :BLOCK], own, jnp.zeros((4, 64), jnp.int32)], axis=1)
    rhs, link = call(
        front_kernel,
        [SDS((64, 1024), f32), SDS((16, 1024), f32)],
        every[:2].reshape(2048),
        [cells, every[2:].astype(f32)],
        scratch=[pltpu.VMEM((1024, 128), f32), pltpu.VMEM((1024, 128), f32)],
    )
    factor2, diag_inv, cells = lax.optimization_barrier((factor2, diag_inv, cells))
    turned2 = factor2[:, :, : 3 * PIECE].reshape(2 * SLAB, 3 * PIECE).T
    matrix2 = gather_blocks(turned2)
    inverse = diag_inv.reshape(2 * BLOCK, SLAB).T

    slab_shape = SDS((ROWS, SLAB), f32)
    block_shape = SDS((ROWS, BLOCK), f32)
    pair_shape = SDS((2, ROWS, BLOCK), f32)
    sent_shape = SDS((GROUP, ROWS, SLAB), f32)

    def first_blocks(*blocks):
        return [(matrix1, own_block(block)) for block in blocks]

    (acc,) = call(start_kernel, [slab_shape], place, [rhs], first_blocks(0))
    got = plane_spread(acc, 1, 2)
    acc, kept = call(
        forward_one_kernel, [slab_shape, sent_shape], place, [acc, *got], first_blocks(1)
    )
    sent = plane_send(kept, (2, 3))
    got = plane_spread(acc, 2, 3)
    acc, part = call(
        forward_two_kernel,
        [slab_shape, block_shape],
        place,
        [acc, inverse, sent, *got],
        first_blocks(1, 2),
    )
    got = plane_spread(part, 3, 2)
    x3_two, acc, part = call(
        back_three_kernel,
        [block_shape, slab_shape, block_shape],
        place,
        [acc, inverse, *got],
        first_blocks(3),
    )
    x3_one = plane_send(x3_two, (2, 1))
    got = plane_spread(part, 2, 1)
    both_one, acc, part = call(
        back_two_kernel,
        [pair_shape, slab_shape, block_shape],
        place,
        [acc, inverse, *got, x3_one],
        first_blocks(2, 3),
    )
    matrix2, part = lax.optimization_barrier((matrix2, part))

    def second_blocks(*blocks):
        return [(matrix2, second_factor(block)) for block in blocks]

    later = plane_send(both_one, (1, 0))
    got = plane_spread(part, 1, 0)
    newest, both_zero, part = call(
        back_one_kernel,
        [block_shape, pair_shape, block_shape],
        place,
        [acc, inverse, *got, later, both_one, x3_two],
        first_blocks(1, 2, 3),
    )
    own = plane_send(newest, (0, 1), (1, 2), (2, 3))
    got = plane_spread(part, 0, 1)
    passing, acc = call(
        couple_kernel,
        [pair_shape, slab_shape],
        place,
        [rhs, link, *got, own, both_zero],
        second_blocks(0),
    )
    passed = plane_send(passing, (1, 2), (0, 3))
    got = plane_spread(acc, 1, 2)
    acc, kept = call(
        second_one_kernel,
        [slab_shape, SDS((2 * GROUP, ROWS, SLAB), f32)],
        place,
        [rhs, link, acc, own, passing, passed, *got],
        second_blocks(0, 1),
    )
    sent = plane_send(kept, (2, 3), (1, 0))
    got = plane_spread(acc, 2, 3)
    (acc,) = call(
        second_base_kernel,
        [slab_shape],
        place,
        [rhs, link, acc, sent, own],
        second_blocks(0),
    )

    at = jnp.arange(SLAB, dtype=jnp.int32)
    own_c, own_y, own_x = at // CELLS, at % CELLS // 6, at % 6
    own_cells = (row_id * 4 + own_y) * 48 + own_c * 6 + own_x
    hits = front_order[None, :] == own_cells[:, None]
    slots = jnp.sum(jnp.where(hits, jnp.arange(4 * BLOCK, dtype=jnp.int32)[None, :], 0), axis=1)
    (mine,) = call(
        cells_kernel,
        [SDS((8, ROWS, 128), f32)],
        jnp.concatenate([slots, place]),
        [sent, passing, passed, newest, own, both_zero, later, x3_one],
        scratch=[pltpu.VMEM((4 * BLOCK, 128), f32), pltpu.VMEM((128, 128), f32)],
    )
    (last,) = call(
        second_two_kernel,
        [SDS((8, ROWS, 256), f32)],
        place,
        [acc, mine, sent, *got],
        second_blocks(1, 2),
    )
    arrived = lax.all_to_all(last, "col", 0, 0)
    return call(
        out_kernel,
        [SDS((2, 4, 6, 128), f32), SDS((2, SLAB, 128), f32)],
        place,
        [arrived],
    )


def solution(mesh):
    in_specs = (
        P(None, "row", "col", None),
        P(None, "row", "col", None),
        P(None, "row", "col"),
        P(None, "row", "col"),
        P(None, "row", "col"),
        P(None, None, "row"),
        P(),
    )
    out_specs = (P(None, "row", "col", None), P(None, "row", None))
    return jax.shard_map(
        on_device, mesh=mesh, in_specs=in_specs, out_specs=out_specs, check_vma=False
    )
```

```python
import functools

import jax
import jax.numpy as jnp
from jax import lax
from jax.experimental import pallas as pl
from jax.experimental.pallas import tpu as pltpu
from jax.sharding import PartitionSpec as P

GROUP = 4
CHUNK = 16
ROWS = 2 * CHUNK
SLAB = 192
BLOCK = 768
PIECE = 96
CELLS = 24
VMEM = 16 * 1024 * 1024

SDS = jax.ShapeDtypeStruct
f32 = jnp.float32


def split(value):
    high = value.astype(jnp.bfloat16)
    return high, (value - high.astype(f32)).astype(jnp.bfloat16)


def complex_dot(vector, weight):
    weight_high, weight_low = weight
    half = weight_high.shape[1] // 2
    high, low = split(vector)
    both = jnp.dot(
        jnp.concatenate([high, low], axis=0), weight_high, preferred_element_type=f32
    )
    total = both[:ROWS] + both[ROWS:] + jnp.dot(high, weight_low, preferred_element_type=f32)
    real = total[:CHUNK, :half] - total[CHUNK:, half:]
    imag = total[:CHUNK, half:] + total[CHUNK:, :half]
    return jnp.concatenate([real, imag], axis=0)


def slot_of(plane, block):
    return jnp.minimum(jnp.where(plane < block, block - 1, block), GROUP - 2)


def block_weight(parts, slot):
    return tuple(ref[slot] for ref in parts)


def slab_weight(parts, slot, source):
    at = pl.multiple_of(SLAB * source, SLAB)
    return tuple(ref[slot, pl.ds(at, SLAB), :] for ref in parts)


def slabs_dot(slabs, parts, slot, q, keep=None):
    total = None
    for d, slab in enumerate(slabs):
        source = lax.rem(q - d + GROUP, GROUP)
        if keep is not None:
            keep[source] = slab
        part = complex_dot(slab, slab_weight(parts, slot, source))
        total = part if total is None else total + part
    return total


def sent_dot(sent_ref, parts, slot):
    total = None
    for s in range(GROUP):
        part = complex_dot(sent_ref[s], slab_weight(parts, slot, s))
        total = part if total is None else total + part
    return total


def add_refs(refs):
    total = refs[0][...]
    for ref in refs[1:]:
        total = total + ref[...]
    return total


def call(body, out_shape, scalars, inputs, blocks=(), scratch=(), steps=1):
    vmem = pl.BlockSpec(memory_space=pltpu.VMEM)
    specs = [vmem] * len(inputs)
    for _, at in blocks:
        specs.append(pl.BlockSpec((8, 1, PIECE, 2 * SLAB), at))
    near = [pltpu.with_memory_space_constraint(value, pltpu.VMEM) for value in inputs]
    far = [pltpu.with_memory_space_constraint(array, pltpu.HBM) for array, _ in blocks]
    return pl.pallas_call(
        body,
        grid_spec=pltpu.PrefetchScalarGridSpec(
            num_scalar_prefetch=1,
            grid=(steps,),
            in_specs=specs,
            out_specs=(vmem,) * len(out_shape),
            scratch_shapes=scratch,
        ),
        out_shape=tuple(pltpu.VMEM(shape.shape, shape.dtype) for shape in out_shape),
        compiler_params=pltpu.CompilerParams(vmem_limit_bytes=VMEM),
    )(scalars, *near, *far)


def turn_first_kernel(place_ref, factor_ref, out_ref, turned_ref):
    rows = factor_ref[...].reshape(2 * SLAB, 4 * PIECE)
    for part in range(3):
        turned_ref[128 * part : 128 * part + 128, :] = rows[:, 128 * part : 128 * part + 128].T
    for slot in range(GROUP - 1):
        block = slot + jnp.where(place_ref[0] > slot, 0, 1)
        out_ref[PIECE * slot : PIECE * slot + PIECE, :] = turned_ref[pl.ds(block * PIECE, PIECE), :]


def pack_kernel(place_ref, first_ref, second_ref, link_ref, out_ref):
    lane = lax.broadcasted_iota(jnp.int32, (6, 128), 1)
    for at_row, ref in ((0, first_ref), (8, second_ref)):
        parts = [ref[part, y] for y in range(4) for part in range(2)]
        for c in range(8):
            row = jnp.zeros((6, 128), f32)
            for at, part in enumerate(parts):
                shift = (16 * at - 16 * c) % 128
                moved = pltpu.roll(part, shift, 1) if shift else part
                row = jnp.where((lane >= 16 * at) & (lane < 16 * at + 16), moved, row)
            out_ref[c, at_row : at_row + 6, :] = row
            out_ref[c, at_row + 6 : at_row + 8, :] = jnp.broadcast_to(link_ref[...], (2, 128))


def gather_rows(where_ref, first, cells_ref, rows_ref):
    def some(step, carry):
        for u in range(16):
            at = step * 16 + u
            rows_ref[pl.ds(at, 1), :] = cells_ref[pl.ds(where_ref[first + at], 1), :]
        return carry

    lax.fori_loop(0, 64, some, 0)


def turn_rows(rows_ref, mark_ref, rhs_ref):
    for part in range(8):
        at = slice(128 * part, 128 * part + 128)
        turned = rows_ref[at, :].T
        quarter = mark_ref[0:1, at]
        value = turned[0:32]
        for y in range(1, 4):
            value = jnp.where(quarter == y, turned[32 * y : 32 * y + 32], value)
        rhs_ref[:, at] = value


def first_front_kernel(where_ref, cells_ref, mark_ref, rhs_ref, rows_ref):
    gather_rows(where_ref, 0, cells_ref, rows_ref)
    turn_rows(rows_ref, mark_ref, rhs_ref)


def second_front_kernel(where_ref, cells_ref, mark_ref, rhs_ref, link_ref, rows_ref):
    gather_rows(where_ref, 0, cells_ref, rows_ref)
    turn_rows(rows_ref, mark_ref, rhs_ref)
    gather_rows(where_ref, 1024, cells_ref, rows_ref)
    lane = lax.broadcasted_iota(jnp.int32, (32, 128), 0).astype(f32)
    for part in range(8):
        at = slice(128 * part, 128 * part + 128)
        turned = rows_ref[at, :].T
        own = mark_ref[1:2, at] == lane
        real = jnp.sum(jnp.where(own, turned[0:32], 0.0), axis=0, keepdims=True)
        imag = jnp.sum(jnp.where(own, turned[32:64], 0.0), axis=0, keepdims=True)
        link_ref[0:8, at] = jnp.broadcast_to(real, (8, 128))
        link_ref[8:16, at] = jnp.broadcast_to(imag, (8, 128))


def split_kernel(place_ref, weight_ref, high_ref, low_ref):
    slot = pl.program_id(0)
    high, low = split(weight_ref[:, 0].reshape(BLOCK, 2 * SLAB))
    high_ref[slot] = high
    low_ref[slot] = low


def split_inverse_kernel(place_ref, weight_ref, high_ref, low_ref):
    high_ref[...], low_ref[...] = split(weight_ref[...])


def start_kernel(place_ref, rhs_ref, weight_ref, acc_ref):
    weight = split(weight_ref[:, 0].reshape(BLOCK, 2 * SLAB))
    product = complex_dot(rhs_ref[:, 0:BLOCK], weight)
    slab = rhs_ref[:, BLOCK : BLOCK + SLAB]
    acc_ref[...] = jnp.where(place_ref[0] > 0, slab - product, slab)


def forward_one_kernel(place_ref, acc_ref, y0, y1, y2, y3, high, low, out_ref, keep_ref):
    plane, q = place_ref[0], place_ref[1]
    slabs = [y0[...], y1[...], y2[...], y3[...]]
    out_ref[...] = acc_ref[...] - slabs_dot(slabs, (high, low), slot_of(plane, 1), q, keep_ref)


def forward_two_kernel(
    place_ref, acc_ref, inverse_high, inverse_low, sent_ref, y0, y1, y2, y3, high, low, out_ref, part_ref
):
    plane, q = place_ref[0], place_ref[1]
    slabs = [y0[...], y1[...], y2[...], y3[...]]
    solved = (
        acc_ref[...]
        - sent_dot(sent_ref, (high, low), slot_of(plane, 1))
        - slabs_dot(slabs, (high, low), slot_of(plane, 2), q)
    )
    out_ref[...] = solved
    part_ref[...] = complex_dot(solved, (inverse_high[...], inverse_low[...]))


def back_three_kernel(
    place_ref,
    acc_ref,
    inverse_high,
    inverse_low,
    p0,
    p1,
    p2,
    p3,
    high,
    low,
    x_ref,
    acc_out_ref,
    part_ref,
):
    x = add_refs([p0, p1, p2, p3])
    weight = block_weight((high, low), slot_of(place_ref[0], 3))
    acc = acc_ref[...] - complex_dot(x, weight)
    x_ref[...] = x
    acc_out_ref[...] = acc
    part_ref[...] = complex_dot(acc, (inverse_high[...], inverse_low[...]))


def back_two_kernel(
    place_ref,
    acc_ref,
    inverse_high,
    inverse_low,
    p0,
    p1,
    p2,
    p3,
    x3_ref,
    high,
    low,
    both_ref,
    acc_out_ref,
    part_ref,
):
    plane = place_ref[0]
    x = add_refs([p0, p1, p2, p3])
    acc = (
        acc_ref[...]
        - complex_dot(x3_ref[...], block_weight((high, low), slot_of(plane, 3)))
        - complex_dot(x, block_weight((high, low), slot_of(plane, 2)))
    )
    both_ref[0] = x
    both_ref[1] = x3_ref[...]
    acc_out_ref[...] = acc
    part_ref[...] = complex_dot(acc, (inverse_high[...], inverse_low[...]))


def back_one_kernel(
    place_ref,
    acc_ref,
    inverse_high,
    inverse_low,
    p0,
    p1,
    p2,
    p3,
    later_ref,
    x2_ref,
    x3_ref,
    high,
    low,
    newest_ref,
    both_ref,
    part_ref,
):
    plane = place_ref[0]
    x = add_refs([p0, p1, p2, p3])
    acc = (
        acc_ref[...]
        - complex_dot(later_ref[1], block_weight((high, low), slot_of(plane, 3)))
        - complex_dot(later_ref[0], block_weight((high, low), slot_of(plane, 2)))
        - complex_dot(x, block_weight((high, low), slot_of(plane, 1)))
    )
    part_ref[...] = complex_dot(acc, (inverse_high[...], inverse_low[...]))
    newest_ref[...] = x + x2_ref[0] + x3_ref[...]
    both_ref[0] = x
    both_ref[1] = later_ref[0]


def coupled(rhs, link_real, link_imag, x):
    real = rhs[:CHUNK] - (link_real * x[:CHUNK] - link_imag * x[CHUNK:])
    imag = rhs[CHUNK:] - (link_real * x[CHUNK:] + link_imag * x[:CHUNK])
    return jnp.concatenate([real, imag], axis=0)


def second_block(rhs_ref, link_ref, x):
    return coupled(
        rhs_ref[:, 0:BLOCK], link_ref[0:1, 0:BLOCK], link_ref[8:9, 0:BLOCK], x
    )


def second_slab(rhs_ref, link_ref, x, q):
    own = x[:, 0:SLAB]
    for s in range(1, GROUP):
        own = jnp.where(q == s, x[:, SLAB * s : SLAB * s + SLAB], own)
    end = BLOCK + SLAB
    return coupled(
        rhs_ref[:, BLOCK:end], link_ref[0:1, BLOCK:end], link_ref[8:9, BLOCK:end], own
    )


def couple_kernel(
    place_ref, rhs_ref, link_ref, p0, p1, p2, p3, own_ref, zero_ref, high, low, pass_ref, out_ref
):
    x0 = add_refs([p0, p1, p2, p3])
    slab = second_slab(rhs_ref, link_ref, own_ref[...], place_ref[1])
    out_ref[...] = slab - complex_dot(
        second_block(rhs_ref, link_ref, x0), block_weight((high, low), 0)
    )
    zero = place_ref[0] == 0
    pass_ref[0] = jnp.where(zero, zero_ref[0], x0)
    pass_ref[1] = jnp.where(zero, zero_ref[1], own_ref[...])


def second_one_kernel(
    place_ref,
    rhs_ref,
    link_ref,
    acc_ref,
    own_ref,
    sent_ref,
    got_ref,
    f0,
    f1,
    f2,
    f3,
    high,
    low,
    out_ref,
    keep_ref,
):
    plane, q = place_ref[0], place_ref[1]
    x0 = jnp.where(plane == 1, sent_ref[0], got_ref[0])
    for s in range(GROUP):
        keep_ref[GROUP + s] = x0[:, SLAB * s : SLAB * s + SLAB]
    slab = second_slab(rhs_ref, link_ref, own_ref[...], q)
    product = complex_dot(second_block(rhs_ref, link_ref, x0), block_weight((high, low), 0))
    slabs = [f0[...], f1[...], f2[...], f3[...]]
    solved = slab - product - slabs_dot(slabs, (high, low), 1, q, keep_ref)
    out_ref[...] = jnp.where(plane == 1, acc_ref[...], solved)


def joined(ref, first):
    return jnp.concatenate([ref[first + s] for s in range(GROUP)], axis=1)


def second_base_kernel(
    place_ref, rhs_ref, link_ref, acc_ref, got_ref, own_ref, high, low, out_ref
):
    plane, q = place_ref[0], place_ref[1]
    x0 = joined(got_ref, GROUP)
    own = jnp.where(plane == 0, x0, own_ref[...])
    slab = second_slab(rhs_ref, link_ref, own, q)
    product = complex_dot(second_block(rhs_ref, link_ref, x0), block_weight((high, low), 0))
    out_ref[...] = jnp.where(
        plane == 0, slab, jnp.where(plane == 3, slab - product, acc_ref[...])
    )


def cells_kernel(
    where_ref, got_ref, pass_ref, passed_ref, newest_ref, own_ref, both_zero, later_ref, x3_one, out_ref, front_ref, rows_ref
):
    plane = where_ref[SLAB]

    def pick(*by_plane):
        value = by_plane[0]
        for at in range(1, GROUP):
            value = jnp.where(plane == at, by_plane[at], value)
        return value

    last = joined(got_ref, GROUP)
    blocks = (
        pick(last, pass_ref[0], passed_ref[0], last),
        pick(newest_ref[...], own_ref[...], passed_ref[1], passed_ref[0]),
        pick(both_zero[1], newest_ref[...], own_ref[...], passed_ref[1]),
        pick(later_ref[1], x3_one[...], newest_ref[...], own_ref[...]),
    )
    for k, x in enumerate(blocks):
        for part in range(6):
            at = BLOCK * k + 128 * part
            piece = x[:, 128 * part : 128 * part + 128]
            wide = jnp.concatenate([piece, jnp.zeros((128 - ROWS, 128), f32)], axis=0)
            front_ref[at : at + 128, :] = wide.T
    rows_ref[...] = jnp.zeros_like(rows_ref)
    for c in range(8):
        for u in range(CELLS):
            rows_ref[64 + u : 65 + u, :] = front_ref[pl.ds(where_ref[CELLS * c + u], 1), :]
        out_ref[c] = rows_ref[...].T[:ROWS]


def second_two_kernel(
    place_ref, acc_ref, cells_ref, sent_ref, f0, f1, f2, f3, high, low, out_ref
):
    slabs = [f0[...], f1[...], f2[...], f3[...]]
    solved = (
        acc_ref[...]
        - sent_dot(sent_ref, (high, low), 1)
        - slabs_dot(slabs, (high, low), 2, place_ref[1])
    )
    lane = lax.broadcasted_iota(jnp.int32, (ROWS, 128), 1)
    tail = jnp.concatenate([solved[:, 128:], jnp.zeros((ROWS, 64), f32)], axis=1)
    for c in range(8):
        out_ref[c, :, 0:128] = solved[:, 0:128]
        out_ref[c, :, 128:256] = jnp.where(lane < 64, tail, cells_ref[c])


def out_kernel(place_ref, got_ref, solution_ref, forward_ref):
    for part in range(2):
        wide = got_ref[:, CHUNK * part : CHUNK * part + CHUNK, :].reshape(128, 256)
        forward_ref[part, 0:128, :] = wide[:, 0:128].T
        turned = wide[:, 128:256].T
        forward_ref[part, 128:SLAB, :] = turned[0:64]
        for y in range(4):
            solution_ref[part, y] = turned[64 + 6 * y : 70 + 6 * y]


def plane_send(value, *moves, turn=0):
    pairs = [
        (GROUP * source + q, GROUP * target + (q + turn) % GROUP)
        for source, target in moves
        for q in range(GROUP)
    ]
    return lax.ppermute(value, "row", pairs)


def plane_spread(value, source, target):
    return [plane_send(value, (source, target), turn=d) for d in range(GROUP)]


def after(value, arrived):
    return lax.optimization_barrier((value, arrived))[0]


def on_device(source1, source2, coupling, factor1, factor2, diag_inv, front_order):
    row_id = lax.axis_index("row")
    col_id = lax.axis_index("col")
    place = jnp.stack([row_id // GROUP, row_id % GROUP]).astype(jnp.int32)

    def gather_blocks(turned):
        return lax.all_gather(turned, "col").reshape(8, GROUP - 1, PIECE, 2 * SLAB)

    (turned1,) = call(
        turn_first_kernel,
        [SDS((3 * PIECE, 2 * SLAB), f32)],
        place,
        [factor1],
        scratch=[pltpu.VMEM((4 * PIECE, 2 * SLAB), f32)],
    )
    matrix1 = gather_blocks(turned1)

    links = jnp.pad(coupling.reshape(2, CELLS), ((0, 0), (0, 32 - CELLS))).reshape(1, 64)
    links = jnp.pad(links, ((0, 0), (0, 64)))
    (packed,) = call(
        pack_kernel, [SDS((8, 16, 128), f32)], place, [source1, source2, links]
    )
    packed = lax.all_to_all(packed, "col", 0, 0)
    early = jnp.broadcast_to(packed[:, :8].reshape(1, 64, 128), (16, 64, 128))
    early = lax.all_to_all(early, "row", 0, 0).reshape(1024, 128)
    late = packed[:, 8:].reshape(64, 128)

    cell_y = front_order // 48
    cell_x = front_order % 48
    group_of = (cell_y // 4) * 64 + (cell_x // 6) * 8
    quarter = cell_y % 4
    inner = quarter * 6 + cell_x % 6
    every = jnp.stack([group_of + cell_x % 6, group_of + 6, quarter, inner])
    own = lax.dynamic_slice_in_dim(every, row_id * SLAB, SLAB, 1)
    every = jnp.concatenate([every[:, :BLOCK], own, jnp.zeros((4, 64), jnp.int32)], axis=1)
    where, mark = every[:2].reshape(2048), every[2:].astype(f32)
    rows_shape = SDS((ROWS, 1024), f32)
    rows_scratch = [pltpu.VMEM((1024, 128), f32)]
    (rhs,) = call(first_front_kernel, [rows_shape], where, [early, mark], scratch=rows_scratch)

    slab_shape = SDS((ROWS, SLAB), f32)
    block_shape = SDS((ROWS, BLOCK), f32)
    pair_shape = SDS((2, ROWS, BLOCK), f32)
    sent_shape = SDS((GROUP, ROWS, SLAB), f32)

    def split_factor(matrix):
        shape = SDS((GROUP - 1, BLOCK, 2 * SLAB), jnp.bfloat16)
        blocks = [(matrix, lambda i, place: (0, i, 0, 0))]
        return call(split_kernel, [shape, shape], place, [], blocks, steps=GROUP - 1)

    first = [(matrix1, lambda i, place: (0, slot_of(place[0], 0), 0, 0))]
    (acc,) = call(start_kernel, [slab_shape], place, [rhs], first)
    got = plane_spread(acc, 1, 2)
    matrix1, diag_inv = after((matrix1, diag_inv), acc)
    parts1 = split_factor(matrix1)
    inverse = diag_inv.reshape(2 * BLOCK, SLAB).T
    shape = SDS((SLAB, 2 * BLOCK), jnp.bfloat16)
    inverse = call(split_inverse_kernel, [shape, shape], place, [inverse])
    acc, kept = call(
        forward_one_kernel, [slab_shape, sent_shape], place, [acc, *got, *parts1]
    )
    late, factor2 = after((late, factor2), acc)
    late = jnp.broadcast_to(late[None], (16, 64, 128))
    late = lax.all_to_all(late, "row", 0, 0).reshape(1024, 128)
    turned2 = factor2[:, :, : 3 * PIECE].reshape(2 * SLAB, 3 * PIECE).T
    matrix2 = gather_blocks(turned2)

    sent = plane_send(kept, (2, 3))
    got = plane_spread(acc, 2, 3)
    acc, part = call(
        forward_two_kernel,
        [slab_shape, block_shape],
        place,
        [acc, *inverse, sent, *got, *parts1],
    )
    got = plane_spread(part, 3, 2)
    x3_two, acc, part = call(
        back_three_kernel,
        [block_shape, slab_shape, block_shape],
        place,
        [acc, *inverse, *got, *parts1],
    )
    x3_one = plane_send(x3_two, (2, 1))
    got = plane_spread(part, 2, 1)
    both_one, acc, part = call(
        back_two_kernel,
        [pair_shape, slab_shape, block_shape],
        place,
        [acc, *inverse, *got, x3_one, *parts1],
    )
    later = plane_send(both_one, (1, 0))
    got = plane_spread(part, 1, 0)
    late = after(late, part)
    rhs, link = call(
        second_front_kernel,
        [rows_shape, SDS((16, 1024), f32)],
        where,
        [late, mark],
        scratch=rows_scratch,
    )
    newest, both_zero, part = call(
        back_one_kernel,
        [block_shape, pair_shape, block_shape],
        place,
        [acc, *inverse, *got, later, both_one, x3_two, *parts1],
    )
    own = plane_send(newest, (0, 1), (1, 2), (2, 3))
    got = plane_spread(part, 0, 1)
    parts2 = split_factor(after(matrix2, part))
    passing, acc = call(
        couple_kernel,
        [pair_shape, slab_shape],
        place,
        [rhs, link, *got, own, both_zero, *parts2],
    )
    passed = plane_send(passing, (1, 2), (0, 3))
    got = plane_spread(acc, 1, 2)
    acc, kept = call(
        second_one_kernel,
        [slab_shape, SDS((2 * GROUP, ROWS, SLAB), f32)],
        place,
        [rhs, link, acc, own, passing, passed, *got, *parts2],
    )
    sent = plane_send(kept, (2, 3), (1, 0))
    got = plane_spread(acc, 2, 3)
    (acc,) = call(
        second_base_kernel,
        [slab_shape],
        place,
        [rhs, link, acc, sent, own, *parts2],
    )

    at = jnp.arange(SLAB, dtype=jnp.int32)
    own_c, own_y, own_x = at // CELLS, at % CELLS // 6, at % 6
    own_cells = (row_id * 4 + own_y) * 48 + own_c * 6 + own_x
    hits = front_order[None, :] == own_cells[:, None]
    slots = jnp.sum(jnp.where(hits, jnp.arange(4 * BLOCK, dtype=jnp.int32)[None, :], 0), axis=1)
    (mine,) = call(
        cells_kernel,
        [SDS((8, ROWS, 128), f32)],
        jnp.concatenate([slots, place]),
        [sent, passing, passed, newest, own, both_zero, later, x3_one],
        scratch=[pltpu.VMEM((4 * BLOCK, 128), f32), pltpu.VMEM((128, 128), f32)],
    )
    (last,) = call(
        second_two_kernel,
        [SDS((8, ROWS, 256), f32)],
        place,
        [acc, mine, sent, *got, *parts2],
    )
    arrived = lax.all_to_all(last, "col", 0, 0)
    return call(
        out_kernel,
        [SDS((2, 4, 6, 128), f32), SDS((2, SLAB, 128), f32)],
        place,
        [arrived],
    )


def solution(mesh):
    in_specs = (
        P(None, "row", "col", None),
        P(None, "row", "col", None),
        P(None, "row", "col"),
        P(None, "row", "col"),
        P(None, "row", "col"),
        P(None, None, "row"),
        P(),
    )
    out_specs = (P(None, "row", "col", None), P(None, "row", None))
    return jax.shard_map(
        on_device, mesh=mesh, in_specs=in_specs, out_specs=out_specs, check_vma=False
    )
```

```python
import functools

import jax
import jax.numpy as jnp
from jax import lax
from jax.experimental import pallas as pl
from jax.experimental.pallas import tpu as pltpu
from jax.sharding import PartitionSpec as P

GROUP = 4
CHUNK = 16
ROWS = 2 * CHUNK
SLAB = 192
BLOCK = 768
PIECE = 96
CELLS = 24
LATE = 5
VMEM = 16 * 1024 * 1024

SDS = jax.ShapeDtypeStruct
f32 = jnp.float32


def split(value):
    high = value.astype(jnp.bfloat16)
    return high, (value - high.astype(f32)).astype(jnp.bfloat16)


def complex_dot(vector, weight):
    weight_high, weight_low = split(weight)
    half = weight.shape[1] // 2
    high, low = split(vector)
    both = jnp.dot(
        jnp.concatenate([high, low], axis=0), weight_high, preferred_element_type=f32
    )
    total = both[:ROWS] + both[ROWS:] + jnp.dot(high, weight_low, preferred_element_type=f32)
    real = total[:CHUNK, :half] - total[CHUNK:, half:]
    imag = total[:CHUNK, half:] + total[CHUNK:, :half]
    return jnp.concatenate([real, imag], axis=0)


def slot_of(plane, block):
    return jnp.minimum(jnp.where(plane < block, block - 1, block), GROUP - 2)


def slab_weight(ref, source):
    at = pl.multiple_of(SLAB * source, SLAB)
    return ref[pl.ds(at, SLAB), :]


def slabs_dot(slabs, ref, q, keep=None):
    total = None
    for d, slab in enumerate(slabs):
        source = lax.rem(q - d + GROUP, GROUP)
        if keep is not None:
            keep[source] = slab
        part = complex_dot(slab, slab_weight(ref, source))
        total = part if total is None else total + part
    return total


def sent_dot(sent_ref, ref):
    total = None
    for s in range(GROUP):
        part = complex_dot(sent_ref[s], slab_weight(ref, s))
        total = part if total is None else total + part
    return total


def add_refs(refs):
    total = refs[0][...]
    for ref in refs[1:]:
        total = total + ref[...]
    return total


def call(body, out_shape, scalars, inputs, blocks=(), scratch=()):
    vmem = pl.BlockSpec(memory_space=pltpu.VMEM)
    specs = [vmem] * len(inputs)
    for _, shape, at in blocks:
        specs.append(pl.BlockSpec(shape, at, pipeline_mode=pl.Buffered(1)))
    near = [pltpu.with_memory_space_constraint(value, pltpu.VMEM) for value in inputs]
    far = [pltpu.with_memory_space_constraint(array, pltpu.HBM) for array, _, _ in blocks]
    return pl.pallas_call(
        body,
        grid_spec=pltpu.PrefetchScalarGridSpec(
            num_scalar_prefetch=1,
            grid=(1,),
            in_specs=specs,
            out_specs=(vmem,) * len(out_shape),
            scratch_shapes=scratch,
        ),
        out_shape=tuple(pltpu.VMEM(shape.shape, shape.dtype) for shape in out_shape),
        compiler_params=pltpu.CompilerParams(vmem_limit_bytes=VMEM),
    )(scalars, *near, *far)


def turn_first_kernel(place_ref, factor_ref, out_ref, turned_ref):
    rows = factor_ref[...].reshape(2 * SLAB, 4 * PIECE)
    for part in range(3):
        turned_ref[128 * part : 128 * part + 128, :] = rows[:, 128 * part : 128 * part + 128].T
    for slot in range(GROUP - 1):
        block = slot + jnp.where(place_ref[0] > slot, 0, 1)
        out_ref[PIECE * slot : PIECE * slot + PIECE, :] = turned_ref[pl.ds(block * PIECE, PIECE), :]


def pack_kernel(place_ref, first_ref, second_ref, link_ref, out_ref):
    lane = lax.broadcasted_iota(jnp.int32, (6, 128), 1)
    for at_row, ref in ((0, first_ref), (8, second_ref)):
        parts = [ref[part, y] for y in range(4) for part in range(2)]
        for c in range(8):
            row = jnp.zeros((6, 128), f32)
            for at, part in enumerate(parts):
                shift = (16 * at - 16 * c) % 128
                moved = pltpu.roll(part, shift, 1) if shift else part
                row = jnp.where((lane >= 16 * at) & (lane < 16 * at + 16), moved, row)
            out_ref[c, at_row : at_row + 6, :] = row
            out_ref[c, at_row + 6 : at_row + 8, :] = jnp.broadcast_to(link_ref[...], (2, 128))


def gather_rows(where_ref, first, cells_ref, rows_ref):
    def some(step, carry):
        for u in range(16):
            at = step * 16 + u
            rows_ref[pl.ds(at, 1), :] = cells_ref[pl.ds(where_ref[first + at], 1), :]
        return carry

    lax.fori_loop(0, 64, some, 0)


def turn_rows(rows_ref, mark_ref, rhs_ref):
    for part in range(8):
        at = slice(128 * part, 128 * part + 128)
        turned = rows_ref[at, :].T
        quarter = mark_ref[0:1, at]
        value = turned[0:32]
        for y in range(1, 4):
            value = jnp.where(quarter == y, turned[32 * y : 32 * y + 32], value)
        rhs_ref[:, at] = value


def first_front_kernel(where_ref, cells_ref, mark_ref, rhs_ref, rows_ref):
    gather_rows(where_ref, 0, cells_ref, rows_ref)
    turn_rows(rows_ref, mark_ref, rhs_ref)


def second_front_kernel(where_ref, mark_ref, late_ref, rhs_ref, link_ref, cells_ref, rows_ref):
    cells_ref[...] = late_ref[...].reshape(1024, 128)
    gather_rows(where_ref, 0, cells_ref, rows_ref)
    turn_rows(rows_ref, mark_ref, rhs_ref)
    gather_rows(where_ref, 1024, cells_ref, rows_ref)
    lane = lax.broadcasted_iota(jnp.int32, (32, 128), 0).astype(f32)
    for part in range(8):
        at = slice(128 * part, 128 * part + 128)
        turned = rows_ref[at, :].T
        own = mark_ref[1:2, at] == lane
        real = jnp.sum(jnp.where(own, turned[0:32], 0.0), axis=0, keepdims=True)
        imag = jnp.sum(jnp.where(own, turned[32:64], 0.0), axis=0, keepdims=True)
        link_ref[0:8, at] = jnp.broadcast_to(real, (8, 128))
        link_ref[8:16, at] = jnp.broadcast_to(imag, (8, 128))


def load_kernel(place_ref, *refs):
    count = len(refs) // 2
    for block_ref, out_ref in zip(refs[:count], refs[count:]):
        out_ref[...] = block_ref[:, 0].reshape(BLOCK, 2 * SLAB)


def start_kernel(place_ref, rhs_ref, weight_ref, acc_ref):
    product = complex_dot(rhs_ref[:, 0:BLOCK], weight_ref[:, 0].reshape(BLOCK, 2 * SLAB))
    slab = rhs_ref[:, BLOCK : BLOCK + SLAB]
    acc_ref[...] = jnp.where(place_ref[0] > 0, slab - product, slab)


def forward_one_kernel(place_ref, acc_ref, y0, y1, y2, y3, weight_ref, out_ref, keep_ref):
    slabs = [y0[...], y1[...], y2[...], y3[...]]
    out_ref[...] = acc_ref[...] - slabs_dot(slabs, weight_ref, place_ref[1], keep_ref)


def forward_two_kernel(
    place_ref, acc_ref, inverse_ref, sent_ref, y0, y1, y2, y3, weight1_ref, weight2_ref, out_ref, part_ref
):
    slabs = [y0[...], y1[...], y2[...], y3[...]]
    solved = (
        acc_ref[...]
        - sent_dot(sent_ref, weight1_ref)
        - slabs_dot(slabs, weight2_ref, place_ref[1])
    )
    out_ref[...] = solved
    part_ref[...] = complex_dot(solved, inverse_ref[...])


def back_three_kernel(
    place_ref,
    acc_ref,
    inverse_ref,
    p0,
    p1,
    p2,
    p3,
    weight_ref,
    x_ref,
    acc_out_ref,
    part_ref,
):
    x = add_refs([p0, p1, p2, p3])
    acc = acc_ref[...] - complex_dot(x, weight_ref[...])
    x_ref[...] = x
    acc_out_ref[...] = acc
    part_ref[...] = complex_dot(acc, inverse_ref[...])


def back_two_kernel(
    place_ref,
    acc_ref,
    inverse_ref,
    p0,
    p1,
    p2,
    p3,
    x3_ref,
    weight2_ref,
    weight3_ref,
    both_ref,
    acc_out_ref,
    part_ref,
):
    x = add_refs([p0, p1, p2, p3])
    acc = (
        acc_ref[...]
        - complex_dot(x3_ref[...], weight3_ref[...])
        - complex_dot(x, weight2_ref[...])
    )
    both_ref[0] = x
    both_ref[1] = x3_ref[...]
    acc_out_ref[...] = acc
    part_ref[...] = complex_dot(acc, inverse_ref[...])


def back_one_kernel(
    place_ref,
    acc_ref,
    inverse_ref,
    p0,
    p1,
    p2,
    p3,
    later_ref,
    x2_ref,
    x3_ref,
    weight1_ref,
    weight2_ref,
    weight3_ref,
    newest_ref,
    both_ref,
    part_ref,
):
    x = add_refs([p0, p1, p2, p3])
    acc = (
        acc_ref[...]
        - complex_dot(later_ref[1], weight3_ref[...])
        - complex_dot(later_ref[0], weight2_ref[...])
        - complex_dot(x, weight1_ref[...])
    )
    part_ref[...] = complex_dot(acc, inverse_ref[...])
    newest_ref[...] = x + x2_ref[0] + x3_ref[...]
    both_ref[0] = x
    both_ref[1] = later_ref[0]


def coupled(rhs, link_real, link_imag, x):
    real = rhs[:CHUNK] - (link_real * x[:CHUNK] - link_imag * x[CHUNK:])
    imag = rhs[CHUNK:] - (link_real * x[CHUNK:] + link_imag * x[:CHUNK])
    return jnp.concatenate([real, imag], axis=0)


def second_block(rhs_ref, link_ref, x):
    return coupled(
        rhs_ref[:, 0:BLOCK], link_ref[0:1, 0:BLOCK], link_ref[8:9, 0:BLOCK], x
    )


def second_slab(rhs_ref, link_ref, x, q):
    own = x[:, 0:SLAB]
    for s in range(1, GROUP):
        own = jnp.where(q == s, x[:, SLAB * s : SLAB * s + SLAB], own)
    end = BLOCK + SLAB
    return coupled(
        rhs_ref[:, BLOCK:end], link_ref[0:1, BLOCK:end], link_ref[8:9, BLOCK:end], own
    )


def couple_kernel(
    place_ref, rhs_ref, link_ref, p0, p1, p2, p3, own_ref, zero_ref, weight_ref, pass_ref, out_ref
):
    x0 = add_refs([p0, p1, p2, p3])
    slab = second_slab(rhs_ref, link_ref, own_ref[...], place_ref[1])
    out_ref[...] = slab - complex_dot(
        second_block(rhs_ref, link_ref, x0), weight_ref[...]
    )
    zero = place_ref[0] == 0
    pass_ref[0] = jnp.where(zero, zero_ref[0], x0)
    pass_ref[1] = jnp.where(zero, zero_ref[1], own_ref[...])


def second_one_kernel(
    place_ref,
    rhs_ref,
    link_ref,
    acc_ref,
    own_ref,
    sent_ref,
    got_ref,
    f0,
    f1,
    f2,
    f3,
    weight0_ref,
    weight1_ref,
    out_ref,
    keep_ref,
):
    plane, q = place_ref[0], place_ref[1]
    x0 = jnp.where(plane == 1, sent_ref[0], got_ref[0])
    for s in range(GROUP):
        keep_ref[GROUP + s] = x0[:, SLAB * s : SLAB * s + SLAB]
    slab = second_slab(rhs_ref, link_ref, own_ref[...], q)
    product = complex_dot(second_block(rhs_ref, link_ref, x0), weight0_ref[...])
    slabs = [f0[...], f1[...], f2[...], f3[...]]
    solved = slab - product - slabs_dot(slabs, weight1_ref, q, keep_ref)
    out_ref[...] = jnp.where(plane == 1, acc_ref[...], solved)


def joined(ref, first):
    return jnp.concatenate([ref[first + s] for s in range(GROUP)], axis=1)


def second_base_kernel(
    place_ref, rhs_ref, link_ref, acc_ref, got_ref, own_ref, weight_ref, out_ref
):
    plane, q = place_ref[0], place_ref[1]
    x0 = joined(got_ref, GROUP)
    own = jnp.where(plane == 0, x0, own_ref[...])
    slab = second_slab(rhs_ref, link_ref, own, q)
    product = complex_dot(second_block(rhs_ref, link_ref, x0), weight_ref[...])
    out_ref[...] = jnp.where(
        plane == 0, slab, jnp.where(plane == 3, slab - product, acc_ref[...])
    )


def cells_kernel(
    where_ref, got_ref, pass_ref, passed_ref, newest_ref, own_ref, both_zero, later_ref, x3_one, out_ref, front_ref, rows_ref
):
    plane = where_ref[SLAB]

    def pick(*by_plane):
        value = by_plane[0]
        for at in range(1, GROUP):
            value = jnp.where(plane == at, by_plane[at], value)
        return value

    last = joined(got_ref, GROUP)
    blocks = (
        pick(last, pass_ref[0], passed_ref[0], last),
        pick(newest_ref[...], own_ref[...], passed_ref[1], passed_ref[0]),
        pick(both_zero[1], newest_ref[...], own_ref[...], passed_ref[1]),
        pick(later_ref[1], x3_one[...], newest_ref[...], own_ref[...]),
    )
    for k, x in enumerate(blocks):
        for part in range(6):
            at = BLOCK * k + 128 * part
            piece = x[:, 128 * part : 128 * part + 128]
            wide = jnp.concatenate([piece, jnp.zeros((128 - ROWS, 128), f32)], axis=0)
            front_ref[at : at + 128, :] = wide.T
    rows_ref[...] = jnp.zeros_like(rows_ref)
    for c in range(8):
        for u in range(CELLS):
            rows_ref[64 + u : 65 + u, :] = front_ref[pl.ds(where_ref[CELLS * c + u], 1), :]
        out_ref[c] = rows_ref[...].T[:ROWS]


def second_two_kernel(
    place_ref, acc_ref, cells_ref, sent_ref, f0, f1, f2, f3, weight1_ref, weight2_ref, out_ref
):
    slabs = [f0[...], f1[...], f2[...], f3[...]]
    solved = (
        acc_ref[...]
        - sent_dot(sent_ref, weight1_ref)
        - slabs_dot(slabs, weight2_ref, place_ref[1])
    )
    lane = lax.broadcasted_iota(jnp.int32, (ROWS, 128), 1)
    tail = jnp.concatenate([solved[:, 128:], jnp.zeros((ROWS, 64), f32)], axis=1)
    for c in range(8):
        out_ref[c, :, 0:128] = solved[:, 0:128]
        out_ref[c, :, 128:256] = jnp.where(lane < 64, tail, cells_ref[c])


def out_kernel(place_ref, got_ref, solution_ref, forward_ref):
    for part in range(2):
        wide = got_ref[:, CHUNK * part : CHUNK * part + CHUNK, :].reshape(128, 256)
        forward_ref[part, 0:128, :] = wide[:, 0:128].T
        turned = wide[:, 128:256].T
        forward_ref[part, 128:SLAB, :] = turned[0:64]
        for y in range(4):
            solution_ref[part, y] = turned[64 + 6 * y : 70 + 6 * y]


def plane_send(value, *moves, turn=0):
    pairs = [
        (GROUP * source + q, GROUP * target + (q + turn) % GROUP)
        for source, target in moves
        for q in range(GROUP)
    ]
    return lax.ppermute(value, "row", pairs)


def plane_spread(value, source, target):
    return [plane_send(value, (source, target), turn=d) for d in range(GROUP)]


def after(value, arrived):
    return lax.optimization_barrier((value, arrived))[0]


def on_device(source1, source2, coupling, factor1, factor2, diag_inv, front_order):
    row_id = lax.axis_index("row")
    col_id = lax.axis_index("col")
    place = jnp.stack([row_id // GROUP, row_id % GROUP]).astype(jnp.int32)

    def gather_blocks(turned):
        return lax.all_gather(turned, "col").reshape(8, GROUP - 1, PIECE, 2 * SLAB)

    (turned1,) = call(
        turn_first_kernel,
        [SDS((3 * PIECE, 2 * SLAB), f32)],
        place,
        [factor1],
        scratch=[pltpu.VMEM((4 * PIECE, 2 * SLAB), f32)],
    )
    matrix1 = gather_blocks(turned1)

    links = jnp.pad(coupling.reshape(2, CELLS), ((0, 0), (0, 32 - CELLS))).reshape(1, 64)
    links = jnp.pad(links, ((0, 0), (0, 64)))
    (packed,) = call(
        pack_kernel, [SDS((8, 16, 128), f32)], place, [source1, source2, links]
    )
    factor2 = after(factor2, packed)
    turned2 = factor2[:, :, : 3 * PIECE].reshape(2 * SLAB, 3 * PIECE).T
    packed = lax.all_to_all(packed, "col", 0, 0)
    early = jnp.broadcast_to(packed[:, :8].reshape(1, 64, 128), (16, 64, 128))
    early = lax.all_to_all(early, "row", 0, 0).reshape(1024, 128)
    late = packed[:, 8:].reshape(64, 128)
    late = jnp.broadcast_to(late[:, None], (64, LATE, 128)).reshape(64, LATE * 128)

    cell_y = front_order // 48
    cell_x = front_order % 48
    group_of = (cell_y // 4) * 64 + (cell_x // 6) * 8
    quarter = cell_y % 4
    inner = quarter * 6 + cell_x % 6
    every = jnp.stack([group_of + cell_x % 6, group_of + 6, quarter, inner])
    own = lax.dynamic_slice_in_dim(every, row_id * SLAB, SLAB, 1)
    every = jnp.concatenate([every[:, :BLOCK], own, jnp.zeros((4, 64), jnp.int32)], axis=1)
    where, mark = every[:2].reshape(2048), every[2:].astype(f32)
    rows_shape = SDS((ROWS, 1024), f32)
    rows_scratch = [pltpu.VMEM((1024, 128), f32)]
    (rhs,) = call(first_front_kernel, [rows_shape], where, [early, mark], scratch=rows_scratch)

    slab_shape = SDS((ROWS, SLAB), f32)
    block_shape = SDS((ROWS, BLOCK), f32)
    pair_shape = SDS((2, ROWS, BLOCK), f32)
    sent_shape = SDS((GROUP, ROWS, SLAB), f32)

    def load(matrix, numbers, arrived, second=False):
        matrix = after(matrix, arrived)
        blocks = [
            (
                matrix,
                (8, 1, PIECE, 2 * SLAB),
                (lambda i, place, n=number: (0, n, 0, 0))
                if second
                else (lambda i, place, n=number: (0, slot_of(place[0], n), 0, 0)),
            )
            for number in numbers
        ]
        shapes = [SDS((BLOCK, 2 * SLAB), f32)] * len(numbers)
        return call(load_kernel, shapes, place, [], blocks)

    first = [
        (matrix1, (8, 1, PIECE, 2 * SLAB), lambda i, place: (0, slot_of(place[0], 0), 0, 0))
    ]
    (acc,) = call(start_kernel, [slab_shape], place, [rhs], first)
    got = plane_spread(acc, 1, 2)
    late, turned2, diag_inv = after((late, turned2, diag_inv), acc)
    late = lax.all_gather(late, "row")
    matrix2 = gather_blocks(turned2)
    weights = load(matrix1, [1], acc)
    inverse = diag_inv.reshape(2 * BLOCK, SLAB).T
    acc, kept = call(
        forward_one_kernel, [slab_shape, sent_shape], place, [acc, *got, *weights]
    )
    sent = plane_send(kept, (2, 3))
    got = plane_spread(acc, 2, 3)
    weights = load(matrix1, [1, 2], acc)
    acc, part = call(
        forward_two_kernel,
        [slab_shape, block_shape],
        place,
        [acc, inverse, sent, *got, *weights],
    )
    got = plane_spread(part, 3, 2)
    weights = load(matrix1, [3], part)
    x3_two, acc, part = call(
        back_three_kernel,
        [block_shape, slab_shape, block_shape],
        place,
        [acc, inverse, *got, *weights],
    )
    x3_one = plane_send(x3_two, (2, 1))
    got = plane_spread(part, 2, 1)
    weights = load(matrix1, [2, 3], part)
    both_one, acc, part = call(
        back_two_kernel,
        [pair_shape, slab_shape, block_shape],
        place,
        [acc, inverse, *got, x3_one, *weights],
    )
    later = plane_send(both_one, (1, 0))
    got = plane_spread(part, 1, 0)
    weights = load(matrix1, [1, 2, 3], part)
    newest, both_zero, part = call(
        back_one_kernel,
        [block_shape, pair_shape, block_shape],
        place,
        [acc, inverse, *got, later, both_one, x3_two, *weights],
    )
    own = plane_send(newest, (0, 1), (1, 2), (2, 3))
    got = plane_spread(part, 0, 1)
    late = after(late, part)
    rhs, link = call(
        second_front_kernel,
        [rows_shape, SDS((16, 1024), f32)],
        where,
        [mark],
        [(late, (16, 64, 128), lambda i, place: (0, 0, 0))],
        scratch=rows_scratch * 2,
    )
    weights = load(matrix2, [0], part, True)
    passing, acc = call(
        couple_kernel,
        [pair_shape, slab_shape],
        place,
        [rhs, link, *got, own, both_zero, *weights],
    )
    passed = plane_send(passing, (1, 2), (0, 3))
    got = plane_spread(acc, 1, 2)
    weights = load(matrix2, [0, 1], acc, True)
    acc, kept = call(
        second_one_kernel,
        [slab_shape, SDS((2 * GROUP, ROWS, SLAB), f32)],
        place,
        [rhs, link, acc, own, passing, passed, *got, *weights],
    )
    sent = plane_send(kept, (2, 3), (1, 0))
    got = plane_spread(acc, 2, 3)
    weights = load(matrix2, [0, 1, 2], acc, True)
    (acc,) = call(
        second_base_kernel,
        [slab_shape],
        place,
        [rhs, link, acc, sent, own, weights[0]],
    )

    at = jnp.arange(SLAB, dtype=jnp.int32)
    own_c, own_y, own_x = at // CELLS, at % CELLS // 6, at % 6
    own_cells = (row_id * 4 + own_y) * 48 + own_c * 6 + own_x
    hits = front_order[None, :] == own_cells[:, None]
    slots = jnp.sum(jnp.where(hits, jnp.arange(4 * BLOCK, dtype=jnp.int32)[None, :], 0), axis=1)
    (mine,) = call(
        cells_kernel,
        [SDS((8, ROWS, 128), f32)],
        jnp.concatenate([slots, place]),
        [sent, passing, passed, newest, own, both_zero, later, x3_one],
        scratch=[pltpu.VMEM((4 * BLOCK, 128), f32), pltpu.VMEM((128, 128), f32)],
    )
    (last,) = call(
        second_two_kernel,
        [SDS((8, ROWS, 256), f32)],
        place,
        [acc, mine, sent, *got, *weights[1:]],
    )
    arrived = lax.all_to_all(last, "col", 0, 0)
    return call(
        out_kernel,
        [SDS((2, 4, 6, 128), f32), SDS((2, SLAB, 128), f32)],
        place,
        [arrived],
    )


def solution(mesh):
    in_specs = (
        P(None, "row", "col", None),
        P(None, "row", "col", None),
        P(None, "row", "col"),
        P(None, "row", "col"),
        P(None, "row", "col"),
        P(None, None, "row"),
        P(),
    )
    out_specs = (P(None, "row", "col", None), P(None, "row", None))
    return jax.shard_map(
        on_device, mesh=mesh, in_specs=in_specs, out_specs=out_specs, check_vma=False
    )
```

```python
import functools

import jax
import jax.numpy as jnp
from jax import lax
from jax.experimental import pallas as pl
from jax.experimental.pallas import tpu as pltpu
from jax.sharding import PartitionSpec as P

GROUP = 4
CHUNK = 16
ROWS = 2 * CHUNK
SLAB = 192
BLOCK = 768
PIECE = 96
CELLS = 24
LATE = 2
VMEM = 16 * 1024 * 1024

SDS = jax.ShapeDtypeStruct
f32 = jnp.float32


def split(value):
    high = value.astype(jnp.bfloat16)
    return high, (value - high.astype(f32)).astype(jnp.bfloat16)


def complex_dot(vector, weight):
    weight_high, weight_low = split(weight)
    half = weight.shape[1] // 2
    high, low = split(vector)
    both = jnp.dot(
        jnp.concatenate([high, low], axis=0), weight_high, preferred_element_type=f32
    )
    total = both[:ROWS] + both[ROWS:] + jnp.dot(high, weight_low, preferred_element_type=f32)
    real = total[:CHUNK, :half] - total[CHUNK:, half:]
    imag = total[:CHUNK, half:] + total[CHUNK:, :half]
    return jnp.concatenate([real, imag], axis=0)


def slot_of(plane, block):
    return jnp.minimum(jnp.where(plane < block, block - 1, block), GROUP - 2)


def slab_weight(ref, source):
    at = pl.multiple_of(SLAB * source, SLAB)
    return ref[pl.ds(at, SLAB), :]


def slabs_dot(slabs, ref, q, keep=None):
    total = None
    for d, slab in enumerate(slabs):
        source = lax.rem(q - d + GROUP, GROUP)
        if keep is not None:
            keep[source] = slab
        part = complex_dot(slab, slab_weight(ref, source))
        total = part if total is None else total + part
    return total


def sent_dot(sent_ref, ref):
    total = None
    for s in range(GROUP):
        part = complex_dot(sent_ref[s], slab_weight(ref, s))
        total = part if total is None else total + part
    return total


def add_refs(refs):
    total = refs[0][...]
    for ref in refs[1:]:
        total = total + ref[...]
    return total


def call(body, out_shape, scalars, inputs, blocks=(), scratch=()):
    vmem = pl.BlockSpec(memory_space=pltpu.VMEM)
    specs = [vmem] * len(inputs)
    for _, shape, at in blocks:
        specs.append(pl.BlockSpec(shape, at, pipeline_mode=pl.Buffered(1)))
    near = [pltpu.with_memory_space_constraint(value, pltpu.VMEM) for value in inputs]
    far = [pltpu.with_memory_space_constraint(array, pltpu.HBM) for array, _, _ in blocks]
    return pl.pallas_call(
        body,
        grid_spec=pltpu.PrefetchScalarGridSpec(
            num_scalar_prefetch=1,
            grid=(1,),
            in_specs=specs,
            out_specs=(vmem,) * len(out_shape),
            scratch_shapes=scratch,
        ),
        out_shape=tuple(pltpu.VMEM(shape.shape, shape.dtype) for shape in out_shape),
        compiler_params=pltpu.CompilerParams(vmem_limit_bytes=VMEM),
    )(scalars, *near, *far)


def turn_first_kernel(place_ref, factor_ref, out_ref, turned_ref):
    rows = factor_ref[...].reshape(2 * SLAB, 4 * PIECE)
    for part in range(3):
        turned_ref[128 * part : 128 * part + 128, :] = rows[:, 128 * part : 128 * part + 128].T
    for slot in range(GROUP - 1):
        block = slot + jnp.where(place_ref[0] > slot, 0, 1)
        out_ref[PIECE * slot : PIECE * slot + PIECE, :] = turned_ref[pl.ds(block * PIECE, PIECE), :]


def pack_kernel(place_ref, first_ref, second_ref, link_ref, out_ref):
    lane = lax.broadcasted_iota(jnp.int32, (6, 128), 1)
    for at_row, ref in ((0, first_ref), (8, second_ref)):
        parts = [ref[part, y] for y in range(4) for part in range(2)]
        for c in range(8):
            row = jnp.zeros((6, 128), f32)
            for at, part in enumerate(parts):
                shift = (16 * at - 16 * c) % 128
                moved = pltpu.roll(part, shift, 1) if shift else part
                row = jnp.where((lane >= 16 * at) & (lane < 16 * at + 16), moved, row)
            out_ref[c, at_row : at_row + 6, :] = row
            out_ref[c, at_row + 6 : at_row + 8, :] = jnp.broadcast_to(link_ref[...], (2, 128))


def gather_rows(where_ref, first, cells_ref, rows_ref):
    def some(step, carry):
        for u in range(16):
            at = step * 16 + u
            rows_ref[pl.ds(at, 1), :] = cells_ref[pl.ds(where_ref[first + at], 1), :]
        return carry

    lax.fori_loop(0, 64, some, 0)


def turn_rows(rows_ref, mark_ref, rhs_ref):
    for part in range(8):
        at = slice(128 * part, 128 * part + 128)
        turned = rows_ref[at, :].T
        quarter = mark_ref[0:1, at]
        value = turned[0:32]
        for y in range(1, 4):
            value = jnp.where(quarter == y, turned[32 * y : 32 * y + 32], value)
        rhs_ref[:, at] = value


def first_front_kernel(where_ref, cells_ref, mark_ref, rhs_ref, rows_ref):
    gather_rows(where_ref, 0, cells_ref, rows_ref)
    turn_rows(rows_ref, mark_ref, rhs_ref)


def second_front_kernel(where_ref, mark_ref, late_ref, rhs_ref, link_ref, cells_ref, rows_ref):
    cells_ref[...] = late_ref[...].reshape(1024, 128)
    gather_rows(where_ref, 0, cells_ref, rows_ref)
    turn_rows(rows_ref, mark_ref, rhs_ref)
    gather_rows(where_ref, 1024, cells_ref, rows_ref)
    lane = lax.broadcasted_iota(jnp.int32, (32, 128), 0).astype(f32)
    for part in range(8):
        at = slice(128 * part, 128 * part + 128)
        turned = rows_ref[at, :].T
        own = mark_ref[1:2, at] == lane
        real = jnp.sum(jnp.where(own, turned[0:32], 0.0), axis=0, keepdims=True)
        imag = jnp.sum(jnp.where(own, turned[32:64], 0.0), axis=0, keepdims=True)
        link_ref[0:8, at] = jnp.broadcast_to(real, (8, 128))
        link_ref[8:16, at] = jnp.broadcast_to(imag, (8, 128))


def load_kernel(place_ref, *refs):
    count = len(refs) // 2
    for block_ref, out_ref in zip(refs[:count], refs[count:]):
        out_ref[...] = block_ref[:, 0].reshape(BLOCK, 2 * SLAB)


def start_kernel(place_ref, rhs_ref, weight_ref, acc_ref):
    product = complex_dot(rhs_ref[:, 0:BLOCK], weight_ref[:, 0].reshape(BLOCK, 2 * SLAB))
    slab = rhs_ref[:, BLOCK : BLOCK + SLAB]
    acc_ref[...] = jnp.where(place_ref[0] > 0, slab - product, slab)


def forward_one_kernel(place_ref, acc_ref, y0, y1, y2, y3, weight_ref, out_ref, keep_ref):
    slabs = [y0[...], y1[...], y2[...], y3[...]]
    out_ref[...] = acc_ref[...] - slabs_dot(slabs, weight_ref, place_ref[1], keep_ref)


def forward_two_kernel(
    place_ref, acc_ref, inverse_ref, sent_ref, y0, y1, y2, y3, weight1_ref, weight2_ref, out_ref, part_ref
):
    slabs = [y0[...], y1[...], y2[...], y3[...]]
    solved = (
        acc_ref[...]
        - sent_dot(sent_ref, weight1_ref)
        - slabs_dot(slabs, weight2_ref, place_ref[1])
    )
    out_ref[...] = solved
    part_ref[...] = complex_dot(solved, inverse_ref[...])


def back_three_kernel(
    place_ref,
    acc_ref,
    inverse_ref,
    p0,
    p1,
    p2,
    p3,
    weight_ref,
    x_ref,
    acc_out_ref,
    part_ref,
):
    x = add_refs([p0, p1, p2, p3])
    acc = acc_ref[...] - complex_dot(x, weight_ref[...])
    x_ref[...] = x
    acc_out_ref[...] = acc
    part_ref[...] = complex_dot(acc, inverse_ref[...])


def back_two_kernel(
    place_ref,
    acc_ref,
    inverse_ref,
    p0,
    p1,
    p2,
    p3,
    x3_ref,
    weight2_ref,
    weight3_ref,
    both_ref,
    acc_out_ref,
    part_ref,
):
    x = add_refs([p0, p1, p2, p3])
    acc = (
        acc_ref[...]
        - complex_dot(x3_ref[...], weight3_ref[...])
        - complex_dot(x, weight2_ref[...])
    )
    both_ref[0] = x
    both_ref[1] = x3_ref[...]
    acc_out_ref[...] = acc
    part_ref[...] = complex_dot(acc, inverse_ref[...])


def back_one_kernel(
    place_ref,
    acc_ref,
    inverse_ref,
    p0,
    p1,
    p2,
    p3,
    later_ref,
    x2_ref,
    x3_ref,
    weight1_ref,
    weight2_ref,
    weight3_ref,
    newest_ref,
    both_ref,
    part_ref,
):
    x = add_refs([p0, p1, p2, p3])
    acc = (
        acc_ref[...]
        - complex_dot(later_ref[1], weight3_ref[...])
        - complex_dot(later_ref[0], weight2_ref[...])
        - complex_dot(x, weight1_ref[...])
    )
    part_ref[...] = complex_dot(acc, inverse_ref[...])
    newest_ref[...] = x + x2_ref[0] + x3_ref[...]
    both_ref[0] = x
    both_ref[1] = later_ref[0]


def coupled(rhs, link_real, link_imag, x):
    real = rhs[:CHUNK] - (link_real * x[:CHUNK] - link_imag * x[CHUNK:])
    imag = rhs[CHUNK:] - (link_real * x[CHUNK:] + link_imag * x[:CHUNK])
    return jnp.concatenate([real, imag], axis=0)


def second_block(rhs_ref, link_ref, x):
    return coupled(
        rhs_ref[:, 0:BLOCK], link_ref[0:1, 0:BLOCK], link_ref[8:9, 0:BLOCK], x
    )


def second_slab(rhs_ref, link_ref, x, q):
    own = x[:, 0:SLAB]
    for s in range(1, GROUP):
        own = jnp.where(q == s, x[:, SLAB * s : SLAB * s + SLAB], own)
    end = BLOCK + SLAB
    return coupled(
        rhs_ref[:, BLOCK:end], link_ref[0:1, BLOCK:end], link_ref[8:9, BLOCK:end], own
    )


def couple_kernel(
    place_ref, rhs_ref, link_ref, p0, p1, p2, p3, own_ref, zero_ref, weight_ref, x0_ref, pass_ref, out_ref
):
    x0 = add_refs([p0, p1, p2, p3])
    slab = second_slab(rhs_ref, link_ref, own_ref[...], place_ref[1])
    out_ref[...] = slab - complex_dot(
        second_block(rhs_ref, link_ref, x0), weight_ref[...]
    )
    x0_ref[...] = x0
    zero = place_ref[0] == 0
    pass_ref[0] = jnp.where(zero, zero_ref[0], x0)
    pass_ref[1] = jnp.where(zero, zero_ref[1], own_ref[...])


def second_one_kernel(
    place_ref,
    rhs_ref,
    link_ref,
    acc_ref,
    own_ref,
    sent_ref,
    got_ref,
    f0,
    f1,
    f2,
    f3,
    weight0_ref,
    weight1_ref,
    out_ref,
    keep_ref,
):
    plane, q = place_ref[0], place_ref[1]
    x0 = jnp.where(plane == 1, sent_ref[0], got_ref[0])
    slab = second_slab(rhs_ref, link_ref, own_ref[...], q)
    product = complex_dot(second_block(rhs_ref, link_ref, x0), weight0_ref[...])
    slabs = [f0[...], f1[...], f2[...], f3[...]]
    solved = slab - product - slabs_dot(slabs, weight1_ref, q, keep_ref)
    out_ref[...] = jnp.where(plane == 1, acc_ref[...], solved)
    for s in range(GROUP):
        keep_ref[s] = jnp.where(plane == 1, x0[:, SLAB * s : SLAB * s + SLAB], keep_ref[s])


def joined(ref):
    return jnp.concatenate([ref[s] for s in range(GROUP)], axis=1)


def second_base_kernel(
    place_ref, rhs_ref, link_ref, acc_ref, got_ref, x0_three, own_ref, weight_ref, out_ref
):
    plane, q = place_ref[0], place_ref[1]
    x0 = jnp.where(plane == 0, joined(got_ref), x0_three[...])
    own = jnp.where(plane == 0, x0, own_ref[...])
    slab = second_slab(rhs_ref, link_ref, own, q)
    product = complex_dot(second_block(rhs_ref, link_ref, x0), weight_ref[...])
    out_ref[...] = jnp.where(
        plane == 0, slab, jnp.where(plane == 3, slab - product, acc_ref[...])
    )


def cells_kernel(
    where_ref, got_ref, x0_three, pass_ref, passed_ref, newest_ref, own_ref, both_zero, later_ref, x3_one, out_ref, front_ref, rows_ref
):
    plane = where_ref[SLAB]

    def pick(*by_plane):
        value = by_plane[0]
        for at in range(1, GROUP):
            value = jnp.where(plane == at, by_plane[at], value)
        return value

    blocks = (
        pick(joined(got_ref), pass_ref[0], passed_ref[0], x0_three[...]),
        pick(newest_ref[...], own_ref[...], passed_ref[1], passed_ref[0]),
        pick(both_zero[1], newest_ref[...], own_ref[...], passed_ref[1]),
        pick(later_ref[1], x3_one[...], newest_ref[...], own_ref[...]),
    )
    for k, x in enumerate(blocks):
        for part in range(6):
            at = BLOCK * k + 128 * part
            piece = x[:, 128 * part : 128 * part + 128]
            wide = jnp.concatenate([piece, jnp.zeros((128 - ROWS, 128), f32)], axis=0)
            front_ref[at : at + 128, :] = wide.T
    rows_ref[...] = jnp.zeros_like(rows_ref)
    for c in range(8):
        for u in range(CELLS):
            rows_ref[64 + u : 65 + u, :] = front_ref[pl.ds(where_ref[CELLS * c + u], 1), :]
        out_ref[c] = rows_ref[...].T[:ROWS]


def second_two_kernel(
    place_ref, acc_ref, cells_ref, sent_ref, f0, f1, f2, f3, weight1_ref, weight2_ref, out_ref
):
    slabs = [f0[...], f1[...], f2[...], f3[...]]
    solved = (
        acc_ref[...]
        - sent_dot(sent_ref, weight1_ref)
        - slabs_dot(slabs, weight2_ref, place_ref[1])
    )
    solved = jnp.where(place_ref[0] == 0, acc_ref[...], solved)
    lane = lax.broadcasted_iota(jnp.int32, (ROWS, 128), 1)
    tail = jnp.concatenate([solved[:, 128:], jnp.zeros((ROWS, 64), f32)], axis=1)
    for c in range(8):
        out_ref[c, :, 0:128] = solved[:, 0:128]
        out_ref[c, :, 128:256] = jnp.where(lane < 64, tail, cells_ref[c])


def out_kernel(place_ref, got_ref, solution_ref, forward_ref):
    for part in range(2):
        wide = got_ref[:, CHUNK * part : CHUNK * part + CHUNK, :].reshape(128, 256)
        forward_ref[part, 0:128, :] = wide[:, 0:128].T
        turned = wide[:, 128:256].T
        forward_ref[part, 128:SLAB, :] = turned[0:64]
        for y in range(4):
            solution_ref[part, y] = turned[64 + 6 * y : 70 + 6 * y]


def plane_send(value, *moves, turn=0):
    pairs = [
        (GROUP * source + q, GROUP * target + (q + turn) % GROUP)
        for source, target in moves
        for q in range(GROUP)
    ]
    return lax.ppermute(value, "row", pairs)


def plane_spread(value, source, target):
    return [plane_send(value, (source, target), turn=d) for d in range(GROUP)]


def after(value, arrived):
    return lax.optimization_barrier((value, arrived))[0]


def on_device(source1, source2, coupling, factor1, factor2, diag_inv, front_order):
    row_id = lax.axis_index("row")
    col_id = lax.axis_index("col")
    place = jnp.stack([row_id // GROUP, row_id % GROUP]).astype(jnp.int32)

    def gather_blocks(turned):
        return lax.all_gather(turned, "col").reshape(8, GROUP - 1, PIECE, 2 * SLAB)

    (turned1,) = call(
        turn_first_kernel,
        [SDS((3 * PIECE, 2 * SLAB), f32)],
        place,
        [],
        [(factor1, factor1.shape, lambda i, place: (0, 0, 0))],
        [pltpu.VMEM((4 * PIECE, 2 * SLAB), f32)],
    )
    matrix1 = gather_blocks(turned1)

    links = jnp.pad(coupling.reshape(2, CELLS), ((0, 0), (0, 32 - CELLS))).reshape(1, 64)
    links = jnp.pad(links, ((0, 0), (0, 64)))
    (packed,) = call(
        pack_kernel, [SDS((8, 16, 128), f32)], place, [source1, source2, links]
    )
    factor2 = after(factor2, packed)
    turned2 = factor2[:, :, : 3 * PIECE].reshape(2 * SLAB, 3 * PIECE).T
    packed = lax.all_to_all(packed, "col", 0, 0)
    early = jnp.broadcast_to(packed[:, :8].reshape(1, 64, 128), (16, 64, 128))
    early = lax.all_to_all(early, "row", 0, 0).reshape(1024, 128)
    late = packed[:, 8:].reshape(64, 128)
    late = jnp.broadcast_to(late[:, None], (64, LATE, 128)).reshape(64, LATE * 128)

    cell_y = front_order // 48
    cell_x = front_order % 48
    group_of = (cell_y // 4) * 64 + (cell_x // 6) * 8
    quarter = cell_y % 4
    inner = quarter * 6 + cell_x % 6
    every = jnp.stack([group_of + cell_x % 6, group_of + 6, quarter, inner])
    own = lax.dynamic_slice_in_dim(every, row_id * SLAB, SLAB, 1)
    every = jnp.concatenate([every[:, :BLOCK], own, jnp.zeros((4, 64), jnp.int32)], axis=1)
    where, mark = every[:2].reshape(2048), every[2:].astype(f32)
    rows_shape = SDS((ROWS, 1024), f32)
    rows_scratch = [pltpu.VMEM((1024, 128), f32)]
    (rhs,) = call(first_front_kernel, [rows_shape], where, [early, mark], scratch=rows_scratch)

    slab_shape = SDS((ROWS, SLAB), f32)
    block_shape = SDS((ROWS, BLOCK), f32)
    pair_shape = SDS((2, ROWS, BLOCK), f32)
    sent_shape = SDS((GROUP, ROWS, SLAB), f32)

    def load(matrix, numbers, arrived, second=False):
        matrix = after(matrix, arrived)
        blocks = [
            (
                matrix,
                (8, 1, PIECE, 2 * SLAB),
                (lambda i, place, n=number: (0, n, 0, 0))
                if second
                else (lambda i, place, n=number: (0, slot_of(place[0], n), 0, 0)),
            )
            for number in numbers
        ]
        shapes = [SDS((BLOCK, 2 * SLAB), f32)] * len(numbers)
        return call(load_kernel, shapes, place, [], blocks)

    first = [
        (matrix1, (8, 1, PIECE, 2 * SLAB), lambda i, place: (0, slot_of(place[0], 0), 0, 0))
    ]
    (acc,) = call(start_kernel, [slab_shape], place, [rhs], first)
    got = plane_spread(acc, 1, 2)
    late, turned2, diag_inv = after((late, turned2, diag_inv), acc)
    late = lax.all_gather(late, "row")
    matrix2 = gather_blocks(turned2)
    weights = load(matrix1, [1], acc)
    inverse = diag_inv.reshape(2 * BLOCK, SLAB).T
    acc, kept = call(
        forward_one_kernel, [slab_shape, sent_shape], place, [acc, *got, *weights]
    )
    sent = plane_send(kept, (2, 3))
    got = plane_spread(acc, 2, 3)
    weights = load(matrix1, [1, 2], acc)
    acc, part = call(
        forward_two_kernel,
        [slab_shape, block_shape],
        place,
        [acc, inverse, sent, *got, *weights],
    )
    got = plane_spread(part, 3, 2)
    weights = load(matrix1, [3], part)
    x3_two, acc, part = call(
        back_three_kernel,
        [block_shape, slab_shape, block_shape],
        place,
        [acc, inverse, *got, *weights],
    )
    x3_one = plane_send(x3_two, (2, 1))
    got = plane_spread(part, 2, 1)
    weights = load(matrix1, [2, 3], part)
    both_one, acc, part = call(
        back_two_kernel,
        [pair_shape, slab_shape, block_shape],
        place,
        [acc, inverse, *got, x3_one, *weights],
    )
    later = plane_send(both_one, (1, 0))
    got = plane_spread(part, 1, 0)
    weights = load(matrix1, [1, 2, 3], part)
    newest, both_zero, part = call(
        back_one_kernel,
        [block_shape, pair_shape, block_shape],
        place,
        [acc, inverse, *got, later, both_one, x3_two, *weights],
    )
    own = plane_send(newest, (0, 1), (1, 2), (2, 3))
    got = plane_spread(part, 0, 1)
    late = after(late, part)
    rhs, link = call(
        second_front_kernel,
        [rows_shape, SDS((16, 1024), f32)],
        where,
        [mark],
        [(late, (16, 64, 128), lambda i, place: (0, 0, 0))],
        scratch=rows_scratch * 2,
    )
    weights = load(matrix2, [0], part, True)
    x0_one, passing, acc = call(
        couple_kernel,
        [block_shape, pair_shape, slab_shape],
        place,
        [rhs, link, *got, own, both_zero, *weights],
    )
    passed = plane_send(passing, (1, 2), (0, 3))
    got = plane_spread(acc, 1, 2)
    x0_three = plane_send(after(x0_one, got[1]), (1, 3))
    weights = load(matrix2, [0, 1], acc, True)
    acc, kept = call(
        second_one_kernel,
        [slab_shape, sent_shape],
        place,
        [rhs, link, acc, own, passing, passed, *got, *weights],
    )
    acc, kept, x0_three = lax.optimization_barrier((acc, kept, x0_three))
    sent = plane_send(kept, (2, 3), (1, 0))
    got = plane_spread(acc, 2, 3)
    weights = load(matrix2, [0, 1, 2], acc, True)
    (acc,) = call(
        second_base_kernel,
        [slab_shape],
        place,
        [rhs, link, acc, sent, x0_three, own, weights[0]],
    )

    at = jnp.arange(SLAB, dtype=jnp.int32)
    own_c, own_y, own_x = at // CELLS, at % CELLS // 6, at % 6
    own_cells = (row_id * 4 + own_y) * 48 + own_c * 6 + own_x
    hits = front_order[None, :] == own_cells[:, None]
    slots = jnp.sum(jnp.where(hits, jnp.arange(4 * BLOCK, dtype=jnp.int32)[None, :], 0), axis=1)
    (mine,) = call(
        cells_kernel,
        [SDS((8, ROWS, 128), f32)],
        jnp.concatenate([slots, place]),
        [sent, x0_three, passing, passed, newest, own, both_zero, later, x3_one],
        scratch=[pltpu.VMEM((4 * BLOCK, 128), f32), pltpu.VMEM((128, 128), f32)],
    )
    (last,) = call(
        second_two_kernel,
        [SDS((8, ROWS, 256), f32)],
        place,
        [acc, mine, sent, *got, *weights[1:]],
    )
    arrived = lax.all_to_all(last, "col", 0, 0)
    return call(
        out_kernel,
        [SDS((2, 4, 6, 128), f32), SDS((2, SLAB, 128), f32)],
        place,
        [arrived],
    )


def solution(mesh):
    in_specs = (
        P(None, "row", "col", None),
        P(None, "row", "col", None),
        P(None, "row", "col"),
        P(None, "row", "col"),
        P(None, "row", "col"),
        P(None, None, "row"),
        P(),
    )
    out_specs = (P(None, "row", "col", None), P(None, "row", None))
    return jax.shard_map(
        on_device, mesh=mesh, in_specs=in_specs, out_specs=out_specs, check_vma=False
    )
```

```python
import functools

import jax
import jax.numpy as jnp
from jax import lax
from jax.experimental import pallas as pl
from jax.experimental.pallas import tpu as pltpu
from jax.sharding import PartitionSpec as P

GROUP = 4
CHUNK = 16
ROWS = 2 * CHUNK
SLAB = 192
BLOCK = 768
PIECE = 96
CELLS = 24
LATE = 2
VMEM = 16 * 1024 * 1024

SDS = jax.ShapeDtypeStruct
f32 = jnp.float32


def split(value):
    high = value.astype(jnp.bfloat16)
    return high, (value - high.astype(f32)).astype(jnp.bfloat16)


def complex_dot(vector, weight):
    weight_high, weight_low = split(weight)
    half = weight.shape[1] // 2
    high, low = split(vector)
    both = jnp.dot(
        jnp.concatenate([high, low], axis=0), weight_high, preferred_element_type=f32
    )
    total = both[:ROWS] + both[ROWS:] + jnp.dot(high, weight_low, preferred_element_type=f32)
    real = total[:CHUNK, :half] - total[CHUNK:, half:]
    imag = total[:CHUNK, half:] + total[CHUNK:, :half]
    return jnp.concatenate([real, imag], axis=0)


def slot_of(plane, block):
    return jnp.minimum(jnp.where(plane < block, block - 1, block), GROUP - 2)


def slab_weight(ref, source):
    at = pl.multiple_of(SLAB * source, SLAB)
    return ref[pl.ds(at, SLAB), :]


def slabs_dot(slabs, ref, q, keep=None):
    total = None
    for d, slab in enumerate(slabs):
        source = lax.rem(q - d + GROUP, GROUP)
        if keep is not None:
            keep[source] = slab
        part = complex_dot(slab, slab_weight(ref, source))
        total = part if total is None else total + part
    return total


def sent_dot(sent_ref, ref):
    total = None
    for s in range(GROUP):
        part = complex_dot(sent_ref[s], slab_weight(ref, s))
        total = part if total is None else total + part
    return total


def add_refs(refs):
    total = refs[0][...]
    for ref in refs[1:]:
        total = total + ref[...]
    return total


def call(body, out_shape, scalars, inputs, blocks=(), scratch=()):
    vmem = pl.BlockSpec(memory_space=pltpu.VMEM)
    specs = [vmem] * len(inputs)
    for _, shape, at in blocks:
        specs.append(pl.BlockSpec(shape, at, pipeline_mode=pl.Buffered(1)))
    near = [pltpu.with_memory_space_constraint(value, pltpu.VMEM) for value in inputs]
    far = [pltpu.with_memory_space_constraint(array, pltpu.HBM) for array, _, _ in blocks]
    return pl.pallas_call(
        body,
        grid_spec=pltpu.PrefetchScalarGridSpec(
            num_scalar_prefetch=1,
            grid=(1,),
            in_specs=specs,
            out_specs=(vmem,) * len(out_shape),
            scratch_shapes=scratch,
        ),
        out_shape=tuple(pltpu.VMEM(shape.shape, shape.dtype) for shape in out_shape),
        compiler_params=pltpu.CompilerParams(vmem_limit_bytes=VMEM),
    )(scalars, *near, *far)


def turn_first_kernel(place_ref, factor_ref, out_ref, turned_ref):
    rows = factor_ref[...].reshape(2 * SLAB, 4 * PIECE)
    for part in range(3):
        turned_ref[128 * part : 128 * part + 128, :] = rows[:, 128 * part : 128 * part + 128].T
    for slot in range(GROUP - 1):
        block = slot + jnp.where(place_ref[0] > slot, 0, 1)
        out_ref[PIECE * slot : PIECE * slot + PIECE, :] = turned_ref[pl.ds(block * PIECE, PIECE), :]


def pack_kernel(place_ref, first_ref, second_ref, link_ref, out_ref):
    lane = lax.broadcasted_iota(jnp.int32, (6, 128), 1)
    for at_row, ref in ((0, first_ref), (8, second_ref)):
        parts = [ref[part, y] for y in range(4) for part in range(2)]
        for c in range(8):
            row = jnp.zeros((6, 128), f32)
            for at, part in enumerate(parts):
                shift = (16 * at - 16 * c) % 128
                moved = pltpu.roll(part, shift, 1) if shift else part
                row = jnp.where((lane >= 16 * at) & (lane < 16 * at + 16), moved, row)
            out_ref[c, at_row : at_row + 6, :] = row
            out_ref[c, at_row + 6 : at_row + 8, :] = jnp.broadcast_to(link_ref[...], (2, 128))


def gather_rows(where_ref, first, cells_ref, rows_ref):
    def some(step, carry):
        for u in range(16):
            at = step * 16 + u
            rows_ref[pl.ds(at, 1), :] = cells_ref[pl.ds(where_ref[first + at], 1), :]
        return carry

    lax.fori_loop(0, 64, some, 0)


def turn_rows(rows_ref, mark_ref, rhs_ref):
    for part in range(8):
        at = slice(128 * part, 128 * part + 128)
        turned = rows_ref[at, :].T
        quarter = mark_ref[0:1, at]
        value = turned[0:32]
        for y in range(1, 4):
            value = jnp.where(quarter == y, turned[32 * y : 32 * y + 32], value)
        rhs_ref[:, at] = value


def first_front_kernel(where_ref, cells_ref, mark_ref, rhs_ref, rows_ref):
    gather_rows(where_ref, 0, cells_ref, rows_ref)
    turn_rows(rows_ref, mark_ref, rhs_ref)


def second_front_kernel(where_ref, mark_ref, late_ref, rhs_ref, link_ref, cells_ref, rows_ref):
    cells_ref[...] = late_ref[...].reshape(1024, 128)
    gather_rows(where_ref, 0, cells_ref, rows_ref)
    turn_rows(rows_ref, mark_ref, rhs_ref)
    gather_rows(where_ref, 1024, cells_ref, rows_ref)
    lane = lax.broadcasted_iota(jnp.int32, (32, 128), 0).astype(f32)
    for part in range(8):
        at = slice(128 * part, 128 * part + 128)
        turned = rows_ref[at, :].T
        own = mark_ref[1:2, at] == lane
        real = jnp.sum(jnp.where(own, turned[0:32], 0.0), axis=0, keepdims=True)
        imag = jnp.sum(jnp.where(own, turned[32:64], 0.0), axis=0, keepdims=True)
        link_ref[0:8, at] = jnp.broadcast_to(real, (8, 128))
        link_ref[8:16, at] = jnp.broadcast_to(imag, (8, 128))


def load_kernel(place_ref, *refs):
    count = len(refs) // 2
    for block_ref, out_ref in zip(refs[:count], refs[count:]):
        out_ref[...] = block_ref[:, 0].reshape(BLOCK, 2 * SLAB)


def start_kernel(place_ref, rhs_ref, weight_ref, acc_ref):
    product = complex_dot(rhs_ref[:, 0:BLOCK], weight_ref[:, 0].reshape(BLOCK, 2 * SLAB))
    slab = rhs_ref[:, BLOCK : BLOCK + SLAB]
    acc_ref[...] = jnp.where(place_ref[0] > 0, slab - product, slab)


def forward_one_kernel(place_ref, acc_ref, y0, y1, y2, y3, weight_ref, out_ref, keep_ref):
    slabs = [y0[...], y1[...], y2[...], y3[...]]
    out_ref[...] = acc_ref[...] - slabs_dot(slabs, weight_ref, place_ref[1], keep_ref)


def forward_two_kernel(
    place_ref, acc_ref, inverse_ref, sent_ref, y0, y1, y2, y3, weight1_ref, weight2_ref, out_ref, part_ref
):
    slabs = [y0[...], y1[...], y2[...], y3[...]]
    solved = (
        acc_ref[...]
        - sent_dot(sent_ref, weight1_ref)
        - slabs_dot(slabs, weight2_ref, place_ref[1])
    )
    out_ref[...] = solved
    part_ref[...] = complex_dot(solved, inverse_ref[...])


def back_three_kernel(
    place_ref,
    acc_ref,
    inverse_ref,
    p0,
    p1,
    p2,
    p3,
    weight_ref,
    x_ref,
    acc_out_ref,
    part_ref,
):
    x = add_refs([p0, p1, p2, p3])
    acc = acc_ref[...] - complex_dot(x, weight_ref[...])
    x_ref[...] = x
    acc_out_ref[...] = acc
    part_ref[...] = complex_dot(acc, inverse_ref[...])


def back_two_kernel(
    place_ref,
    acc_ref,
    inverse_ref,
    p0,
    p1,
    p2,
    p3,
    x3_ref,
    weight2_ref,
    weight3_ref,
    both_ref,
    acc_out_ref,
    part_ref,
):
    x = add_refs([p0, p1, p2, p3])
    acc = (
        acc_ref[...]
        - complex_dot(x3_ref[...], weight3_ref[...])
        - complex_dot(x, weight2_ref[...])
    )
    both_ref[0] = x
    both_ref[1] = x3_ref[...]
    acc_out_ref[...] = acc
    part_ref[...] = complex_dot(acc, inverse_ref[...])


def back_one_kernel(
    place_ref,
    acc_ref,
    inverse_ref,
    p0,
    p1,
    p2,
    p3,
    later_ref,
    x2_ref,
    x3_ref,
    weight1_ref,
    weight2_ref,
    weight3_ref,
    newest_ref,
    both_ref,
    part_ref,
):
    x = add_refs([p0, p1, p2, p3])
    acc = (
        acc_ref[...]
        - complex_dot(later_ref[1], weight3_ref[...])
        - complex_dot(later_ref[0], weight2_ref[...])
        - complex_dot(x, weight1_ref[...])
    )
    part_ref[...] = complex_dot(acc, inverse_ref[...])
    newest_ref[...] = x + x2_ref[0] + x3_ref[...]
    both_ref[0] = x
    both_ref[1] = later_ref[0]


def coupled(rhs, link_real, link_imag, x):
    real = rhs[:CHUNK] - (link_real * x[:CHUNK] - link_imag * x[CHUNK:])
    imag = rhs[CHUNK:] - (link_real * x[CHUNK:] + link_imag * x[:CHUNK])
    return jnp.concatenate([real, imag], axis=0)


def second_block(rhs_ref, link_ref, x):
    return coupled(
        rhs_ref[:, 0:BLOCK], link_ref[0:1, 0:BLOCK], link_ref[8:9, 0:BLOCK], x
    )


def second_slab(rhs_ref, link_ref, x, q):
    own = x[:, 0:SLAB]
    for s in range(1, GROUP):
        own = jnp.where(q == s, x[:, SLAB * s : SLAB * s + SLAB], own)
    end = BLOCK + SLAB
    return coupled(
        rhs_ref[:, BLOCK:end], link_ref[0:1, BLOCK:end], link_ref[8:9, BLOCK:end], own
    )


def couple_kernel(
    place_ref, rhs_ref, link_ref, p0, p1, p2, p3, own_ref, zero_ref, weight_ref, x0_ref, pass_ref, out_ref
):
    x0 = add_refs([p0, p1, p2, p3])
    slab = second_slab(rhs_ref, link_ref, own_ref[...], place_ref[1])
    out_ref[...] = slab - complex_dot(
        second_block(rhs_ref, link_ref, x0), weight_ref[...]
    )
    x0_ref[...] = x0
    zero = place_ref[0] == 0
    pass_ref[0] = jnp.where(zero, zero_ref[0], x0)
    pass_ref[1] = jnp.where(zero, zero_ref[1], own_ref[...])


def second_one_kernel(
    place_ref,
    rhs_ref,
    link_ref,
    acc_ref,
    own_ref,
    sent_ref,
    got_ref,
    f0,
    f1,
    f2,
    f3,
    weight0_ref,
    weight1_ref,
    out_ref,
    keep_ref,
):
    plane, q = place_ref[0], place_ref[1]
    x0 = jnp.where(plane == 1, sent_ref[0], got_ref[0])
    slab = second_slab(rhs_ref, link_ref, own_ref[...], q)
    product = complex_dot(second_block(rhs_ref, link_ref, x0), weight0_ref[...])
    slabs = [f0[...], f1[...], f2[...], f3[...]]
    solved = slab - product - slabs_dot(slabs, weight1_ref, q, keep_ref)
    out_ref[...] = jnp.where(plane == 1, acc_ref[...], solved)


def second_base_kernel(
    place_ref, rhs_ref, link_ref, acc_ref, x0_zero, x0_three, own_ref, weight_ref, out_ref
):
    plane, q = place_ref[0], place_ref[1]
    x0 = x0_zero[...] + x0_three[...]
    own = jnp.where(plane == 0, x0, own_ref[...])
    slab = second_slab(rhs_ref, link_ref, own, q)
    product = complex_dot(second_block(rhs_ref, link_ref, x0), weight_ref[...])
    out_ref[...] = jnp.where(
        plane == 0, slab, jnp.where(plane == 3, slab - product, acc_ref[...])
    )


def cells_kernel(
    where_ref, x0_zero, x0_three, pass_ref, passed_ref, newest_ref, own_ref, both_zero, later_ref, x3_one, out_ref, front_ref, rows_ref
):
    plane = where_ref[SLAB]

    def pick(*by_plane):
        value = by_plane[0]
        for at in range(1, GROUP):
            value = jnp.where(plane == at, by_plane[at], value)
        return value

    blocks = (
        pick(x0_zero[...], pass_ref[0], passed_ref[0], x0_three[...]),
        pick(newest_ref[...], own_ref[...], passed_ref[1], passed_ref[0]),
        pick(both_zero[1], newest_ref[...], own_ref[...], passed_ref[1]),
        pick(later_ref[1], x3_one[...], newest_ref[...], own_ref[...]),
    )
    for k, x in enumerate(blocks):
        for part in range(6):
            at = BLOCK * k + 128 * part
            piece = x[:, 128 * part : 128 * part + 128]
            wide = jnp.concatenate([piece, jnp.zeros((128 - ROWS, 128), f32)], axis=0)
            front_ref[at : at + 128, :] = wide.T
    rows_ref[...] = jnp.zeros_like(rows_ref)
    for c in range(8):
        for u in range(CELLS):
            rows_ref[64 + u : 65 + u, :] = front_ref[pl.ds(where_ref[CELLS * c + u], 1), :]
        out_ref[c] = rows_ref[...].T[:ROWS]


def second_two_kernel(
    place_ref, acc_ref, cells_ref, sent_ref, f0, f1, f2, f3, weight1_ref, weight2_ref, out_ref
):
    slabs = [f0[...], f1[...], f2[...], f3[...]]
    solved = (
        acc_ref[...]
        - sent_dot(sent_ref, weight1_ref)
        - slabs_dot(slabs, weight2_ref, place_ref[1])
    )
    lane = lax.broadcasted_iota(jnp.int32, (ROWS, 128), 1)
    tail = jnp.concatenate([solved[:, 128:], jnp.zeros((ROWS, 64), f32)], axis=1)
    for c in range(8):
        out_ref[c, :, 0:128] = solved[:, 0:128]
        out_ref[c, :, 128:256] = jnp.where(lane < 64, tail, cells_ref[c])


def out_kernel(place_ref, got_ref, solution_ref, forward_ref):
    for part in range(2):
        wide = got_ref[:, CHUNK * part : CHUNK * part + CHUNK, :].reshape(128, 256)
        forward_ref[part, 0:128, :] = wide[:, 0:128].T
        turned = wide[:, 128:256].T
        forward_ref[part, 128:SLAB, :] = turned[0:64]
        for y in range(4):
            solution_ref[part, y] = turned[64 + 6 * y : 70 + 6 * y]


def plane_send(value, *moves, turn=0):
    pairs = [
        (GROUP * source + q, GROUP * target + (q + turn) % GROUP)
        for source, target in moves
        for q in range(GROUP)
    ]
    return lax.ppermute(value, "row", pairs)


def plane_spread(value, source, target):
    return [plane_send(value, (source, target), turn=d) for d in range(GROUP)]


def after(value, arrived):
    return lax.optimization_barrier((value, arrived))[0]


def on_device(source1, source2, coupling, factor1, factor2, diag_inv, front_order):
    row_id = lax.axis_index("row")
    col_id = lax.axis_index("col")
    place = jnp.stack([row_id // GROUP, row_id % GROUP]).astype(jnp.int32)

    def gather_blocks(turned):
        return lax.all_gather(turned, "col").reshape(8, GROUP - 1, PIECE, 2 * SLAB)

    (turned1,) = call(
        turn_first_kernel,
        [SDS((3 * PIECE, 2 * SLAB), f32)],
        place,
        [],
        [(factor1, factor1.shape, lambda i, place: (0, 0, 0))],
        [pltpu.VMEM((4 * PIECE, 2 * SLAB), f32)],
    )
    matrix1 = gather_blocks(turned1)

    links = jnp.pad(coupling.reshape(2, CELLS), ((0, 0), (0, 32 - CELLS))).reshape(1, 64)
    links = jnp.pad(links, ((0, 0), (0, 64)))
    (packed,) = call(
        pack_kernel, [SDS((8, 16, 128), f32)], place, [source1, source2, links]
    )
    factor2 = after(factor2, packed)
    turned2 = factor2[:, :, : 3 * PIECE].reshape(2 * SLAB, 3 * PIECE).T
    packed = lax.all_to_all(packed, "col", 0, 0)
    early = jnp.broadcast_to(packed[:, :8].reshape(1, 64, 128), (16, 64, 128))
    early = lax.all_to_all(early, "row", 0, 0).reshape(1024, 128)
    late = packed[:, 8:].reshape(64, 128)
    late = jnp.broadcast_to(late[:, None], (64, LATE, 128)).reshape(64, LATE * 128)

    cell_y = front_order // 48
    cell_x = front_order % 48
    group_of = (cell_y // 4) * 64 + (cell_x // 6) * 8
    quarter = cell_y % 4
    inner = quarter * 6 + cell_x % 6
    every = jnp.stack([group_of + cell_x % 6, group_of + 6, quarter, inner])
    own = lax.dynamic_slice_in_dim(every, row_id * SLAB, SLAB, 1)
    every = jnp.concatenate([every[:, :BLOCK], own, jnp.zeros((4, 64), jnp.int32)], axis=1)
    where, mark = every[:2].reshape(2048), every[2:].astype(f32)
    rows_shape = SDS((ROWS, 1024), f32)
    rows_scratch = [pltpu.VMEM((1024, 128), f32)]
    (rhs,) = call(first_front_kernel, [rows_shape], where, [early, mark], scratch=rows_scratch)
    late = lax.all_gather(after(late, rhs), "row")

    slab_shape = SDS((ROWS, SLAB), f32)
    block_shape = SDS((ROWS, BLOCK), f32)
    pair_shape = SDS((2, ROWS, BLOCK), f32)
    sent_shape = SDS((GROUP, ROWS, SLAB), f32)

    def load(matrix, numbers, arrived, second=False):
        matrix = after(matrix, arrived)
        blocks = [
            (
                matrix,
                (8, 1, PIECE, 2 * SLAB),
                (lambda i, place, n=number: (0, n, 0, 0))
                if second
                else (lambda i, place, n=number: (0, slot_of(place[0], n), 0, 0)),
            )
            for number in numbers
        ]
        shapes = [SDS((BLOCK, 2 * SLAB), f32)] * len(numbers)
        return call(load_kernel, shapes, place, [], blocks)

    first = [
        (matrix1, (8, 1, PIECE, 2 * SLAB), lambda i, place: (0, slot_of(place[0], 0), 0, 0))
    ]
    (acc,) = call(start_kernel, [slab_shape], place, [rhs], first)
    got = plane_spread(acc, 1, 2)
    turned2, diag_inv = after((turned2, diag_inv), acc)
    matrix2 = gather_blocks(turned2)
    weights = load(matrix1, [1], acc)
    inverse = diag_inv.reshape(2 * BLOCK, SLAB).T
    acc, kept = call(
        forward_one_kernel, [slab_shape, sent_shape], place, [acc, *got, *weights]
    )
    sent = plane_send(kept, (2, 3))
    got = plane_spread(acc, 2, 3)
    weights = load(matrix1, [1, 2], acc)
    acc, part = call(
        forward_two_kernel,
        [slab_shape, block_shape],
        place,
        [acc, inverse, sent, *got, *weights],
    )
    got = plane_spread(part, 3, 2)
    weights = load(matrix1, [3], part)
    x3_two, acc, part = call(
        back_three_kernel,
        [block_shape, slab_shape, block_shape],
        place,
        [acc, inverse, *got, *weights],
    )
    x3_one = plane_send(x3_two, (2, 1))
    got = plane_spread(part, 2, 1)
    weights = load(matrix1, [2, 3], part)
    both_one, acc, part = call(
        back_two_kernel,
        [pair_shape, slab_shape, block_shape],
        place,
        [acc, inverse, *got, x3_one, *weights],
    )
    later = plane_send(both_one, (1, 0))
    got = plane_spread(part, 1, 0)
    weights = load(matrix1, [1, 2, 3], part)
    late = after(late, part)
    rhs, link = call(
        second_front_kernel,
        [rows_shape, SDS((16, 1024), f32)],
        where,
        [mark],
        [(late, (16, 64, 128), lambda i, place: (0, 0, 0))],
        scratch=rows_scratch * 2,
    )
    acc, rhs, link = lax.optimization_barrier((acc, rhs, link))
    newest, both_zero, part = call(
        back_one_kernel,
        [block_shape, pair_shape, block_shape],
        place,
        [acc, inverse, *got, later, both_one, x3_two, *weights],
    )
    own = plane_send(newest, (0, 1), (1, 2), (2, 3))
    got = plane_spread(part, 0, 1)
    weights = load(matrix2, [0], part, True)
    x0_one, passing, acc = call(
        couple_kernel,
        [block_shape, pair_shape, slab_shape],
        place,
        [rhs, link, *got, own, both_zero, *weights],
    )
    passed = plane_send(passing, (1, 2), (0, 3))
    got = plane_spread(acc, 1, 2)
    x0_three = plane_send(after(x0_one, got[1]), (1, 3))
    x0_zero = plane_send(after(x0_one, got[1]), (1, 0))
    weights = load(matrix2, [0, 1], acc, True)
    acc, kept = call(
        second_one_kernel,
        [slab_shape, sent_shape],
        place,
        [rhs, link, acc, own, passing, passed, *got, *weights],
    )
    acc, kept, x0_three, x0_zero = lax.optimization_barrier((acc, kept, x0_three, x0_zero))
    sent = plane_send(kept, (2, 3))
    got = plane_spread(acc, 2, 3)
    weights = load(matrix2, [0, 1, 2], acc, True)
    (acc,) = call(
        second_base_kernel,
        [slab_shape],
        place,
        [rhs, link, acc, x0_zero, x0_three, own, weights[0]],
    )

    at = jnp.arange(SLAB, dtype=jnp.int32)
    own_c, own_y, own_x = at // CELLS, at % CELLS // 6, at % 6
    own_cells = (row_id * 4 + own_y) * 48 + own_c * 6 + own_x
    hits = front_order[None, :] == own_cells[:, None]
    slots = jnp.sum(jnp.where(hits, jnp.arange(4 * BLOCK, dtype=jnp.int32)[None, :], 0), axis=1)
    (mine,) = call(
        cells_kernel,
        [SDS((8, ROWS, 128), f32)],
        jnp.concatenate([slots, place]),
        [x0_zero, x0_three, passing, passed, newest, own, both_zero, later, x3_one],
        scratch=[pltpu.VMEM((4 * BLOCK, 128), f32), pltpu.VMEM((128, 128), f32)],
    )
    (last,) = call(
        second_two_kernel,
        [SDS((8, ROWS, 256), f32)],
        place,
        [acc, mine, sent, *got, *weights[1:]],
    )
    arrived = lax.all_to_all(last, "col", 0, 0)
    return call(
        out_kernel,
        [SDS((2, 4, 6, 128), f32), SDS((2, SLAB, 128), f32)],
        place,
        [arrived],
    )


def solution(mesh):
    in_specs = (
        P(None, "row", "col", None),
        P(None, "row", "col", None),
        P(None, "row", "col"),
        P(None, "row", "col"),
        P(None, "row", "col"),
        P(None, None, "row"),
        P(),
    )
    out_specs = (P(None, "row", "col", None), P(None, "row", None))
    return jax.shard_map(
        on_device, mesh=mesh, in_specs=in_specs, out_specs=out_specs, check_vma=False
    )
```

```python
import functools

import jax
import jax.numpy as jnp
from jax import lax
from jax.experimental import pallas as pl
from jax.experimental.pallas import tpu as pltpu
from jax.sharding import PartitionSpec as P

GROUP = 4
CHUNK = 16
ROWS = 2 * CHUNK
SLAB = 192
BLOCK = 768
PIECE = 96
CELLS = 24
LATE = 2
VMEM = 16 * 1024 * 1024

SDS = jax.ShapeDtypeStruct
f32 = jnp.float32


def split(value):
    high = value.astype(jnp.bfloat16)
    return high, (value - high.astype(f32)).astype(jnp.bfloat16)


def complex_dot(vector, weight):
    weight_high, weight_low = split(weight)
    half = weight.shape[1] // 2
    high, low = split(vector)
    both = jnp.dot(
        jnp.concatenate([high, low], axis=0), weight_high, preferred_element_type=f32
    )
    total = both[:ROWS] + both[ROWS:] + jnp.dot(high, weight_low, preferred_element_type=f32)
    real = total[:CHUNK, :half] - total[CHUNK:, half:]
    imag = total[:CHUNK, half:] + total[CHUNK:, :half]
    return jnp.concatenate([real, imag], axis=0)


def slot_of(plane, block):
    return jnp.minimum(jnp.where(plane < block, block - 1, block), GROUP - 2)


def slab_weight(ref, source):
    at = pl.multiple_of(SLAB * source, SLAB)
    return ref[pl.ds(at, SLAB), :]


def slabs_dot(slabs, ref, q, keep=None):
    total = None
    for d, slab in enumerate(slabs):
        source = lax.rem(q - d + GROUP, GROUP)
        if keep is not None:
            keep[source] = slab
        part = complex_dot(slab, slab_weight(ref, source))
        total = part if total is None else total + part
    return total


def sent_dot(sent_ref, ref):
    total = None
    for s in range(GROUP):
        part = complex_dot(sent_ref[s], slab_weight(ref, s))
        total = part if total is None else total + part
    return total


def add_refs(refs):
    total = refs[0][...]
    for ref in refs[1:]:
        total = total + ref[...]
    return total


def call(body, out_shape, scalars, inputs, blocks=(), scratch=()):
    vmem = pl.BlockSpec(memory_space=pltpu.VMEM)
    specs = [vmem] * len(inputs)
    for _, shape, at in blocks:
        specs.append(pl.BlockSpec(shape, at, pipeline_mode=pl.Buffered(1)))
    near = [pltpu.with_memory_space_constraint(value, pltpu.VMEM) for value in inputs]
    far = [pltpu.with_memory_space_constraint(array, pltpu.HBM) for array, _, _ in blocks]
    return pl.pallas_call(
        body,
        grid_spec=pltpu.PrefetchScalarGridSpec(
            num_scalar_prefetch=1,
            grid=(1,),
            in_specs=specs,
            out_specs=(vmem,) * len(out_shape),
            scratch_shapes=scratch,
        ),
        out_shape=tuple(pltpu.VMEM(shape.shape, shape.dtype) for shape in out_shape),
        compiler_params=pltpu.CompilerParams(vmem_limit_bytes=VMEM),
    )(scalars, *near, *far)


def turn_first_kernel(place_ref, factor_ref, out_ref, turned_ref):
    rows = factor_ref[...].reshape(2 * SLAB, 4 * PIECE)
    for part in range(3):
        turned_ref[128 * part : 128 * part + 128, :] = rows[:, 128 * part : 128 * part + 128].T
    for slot in range(GROUP - 1):
        block = slot + jnp.where(place_ref[0] > slot, 0, 1)
        out_ref[PIECE * slot : PIECE * slot + PIECE, :] = turned_ref[pl.ds(block * PIECE, PIECE), :]


def pack_kernel(place_ref, first_ref, second_ref, link_ref, out_ref):
    lane = lax.broadcasted_iota(jnp.int32, (6, 128), 1)
    for at_row, ref in ((0, first_ref), (8, second_ref)):
        parts = [ref[part, y] for y in range(4) for part in range(2)]
        for c in range(8):
            row = jnp.zeros((6, 128), f32)
            for at, part in enumerate(parts):
                shift = (16 * at - 16 * c) % 128
                moved = pltpu.roll(part, shift, 1) if shift else part
                row = jnp.where((lane >= 16 * at) & (lane < 16 * at + 16), moved, row)
            out_ref[c, at_row : at_row + 6, :] = row
            out_ref[c, at_row + 6 : at_row + 8, :] = jnp.broadcast_to(link_ref[...], (2, 128))


def gather_rows(where_ref, first, cells_ref, rows_ref):
    def some(step, carry):
        for u in range(16):
            at = step * 16 + u
            rows_ref[pl.ds(at, 1), :] = cells_ref[pl.ds(where_ref[first + at], 1), :]
        return carry

    lax.fori_loop(0, 64, some, 0)


def turn_rows(rows_ref, mark_ref, rhs_ref):
    for part in range(8):
        at = slice(128 * part, 128 * part + 128)
        turned = rows_ref[at, :].T
        quarter = mark_ref[0:1, at]
        value = turned[0:32]
        for y in range(1, 4):
            value = jnp.where(quarter == y, turned[32 * y : 32 * y + 32], value)
        rhs_ref[:, at] = value


def first_front_kernel(where_ref, cells_ref, mark_ref, rhs_ref, rows_ref):
    gather_rows(where_ref, 0, cells_ref, rows_ref)
    turn_rows(rows_ref, mark_ref, rhs_ref)


def second_front_kernel(where_ref, mark_ref, late_ref, rhs_ref, link_ref, cells_ref, rows_ref):
    cells_ref[...] = late_ref[...].reshape(1024, 128)
    gather_rows(where_ref, 0, cells_ref, rows_ref)
    turn_rows(rows_ref, mark_ref, rhs_ref)
    gather_rows(where_ref, 1024, cells_ref, rows_ref)
    lane = lax.broadcasted_iota(jnp.int32, (32, 128), 0).astype(f32)
    for part in range(8):
        at = slice(128 * part, 128 * part + 128)
        turned = rows_ref[at, :].T
        own = mark_ref[1:2, at] == lane
        real = jnp.sum(jnp.where(own, turned[0:32], 0.0), axis=0, keepdims=True)
        imag = jnp.sum(jnp.where(own, turned[32:64], 0.0), axis=0, keepdims=True)
        link_ref[0:8, at] = jnp.broadcast_to(real, (8, 128))
        link_ref[8:16, at] = jnp.broadcast_to(imag, (8, 128))


def load_kernel(place_ref, *refs):
    count = len(refs) // 2
    for block_ref, out_ref in zip(refs[:count], refs[count:]):
        out_ref[...] = block_ref[:, 0].reshape(BLOCK, 2 * SLAB)


def start_kernel(place_ref, rhs_ref, weight_ref, acc_ref):
    product = complex_dot(rhs_ref[:, 0:BLOCK], weight_ref[:, 0].reshape(BLOCK, 2 * SLAB))
    slab = rhs_ref[:, BLOCK : BLOCK + SLAB]
    acc_ref[...] = jnp.where(place_ref[0] > 0, slab - product, slab)


def forward_one_kernel(place_ref, acc_ref, y0, y1, y2, y3, weight_ref, out_ref, keep_ref):
    slabs = [y0[...], y1[...], y2[...], y3[...]]
    out_ref[...] = acc_ref[...] - slabs_dot(slabs, weight_ref, place_ref[1], keep_ref)


def forward_two_kernel(
    place_ref, acc_ref, inverse_ref, sent_ref, y0, y1, y2, y3, weight1_ref, weight2_ref, out_ref, part_ref
):
    slabs = [y0[...], y1[...], y2[...], y3[...]]
    solved = (
        acc_ref[...]
        - sent_dot(sent_ref, weight1_ref)
        - slabs_dot(slabs, weight2_ref, place_ref[1])
    )
    out_ref[...] = solved
    part_ref[...] = complex_dot(solved, inverse_ref[...])


def back_three_kernel(
    place_ref,
    acc_ref,
    inverse_ref,
    p0,
    p1,
    p2,
    p3,
    weight_ref,
    x_ref,
    acc_out_ref,
    part_ref,
):
    x = add_refs([p0, p1, p2, p3])
    acc = acc_ref[...] - complex_dot(x, weight_ref[...])
    x_ref[...] = x
    acc_out_ref[...] = acc
    part_ref[...] = complex_dot(acc, inverse_ref[...])


def back_two_kernel(
    place_ref,
    acc_ref,
    inverse_ref,
    p0,
    p1,
    p2,
    p3,
    x3_ref,
    weight2_ref,
    weight3_ref,
    both_ref,
    acc_out_ref,
    part_ref,
):
    x = add_refs([p0, p1, p2, p3])
    acc = (
        acc_ref[...]
        - complex_dot(x3_ref[...], weight3_ref[...])
        - complex_dot(x, weight2_ref[...])
    )
    both_ref[0] = x
    both_ref[1] = x3_ref[...]
    acc_out_ref[...] = acc
    part_ref[...] = complex_dot(acc, inverse_ref[...])


def back_one_kernel(
    place_ref,
    acc_ref,
    inverse_ref,
    p0,
    p1,
    p2,
    p3,
    later_ref,
    x2_ref,
    x3_ref,
    weight1_ref,
    weight2_ref,
    weight3_ref,
    newest_ref,
    both_ref,
    part_ref,
):
    x = add_refs([p0, p1, p2, p3])
    acc = (
        acc_ref[...]
        - complex_dot(later_ref[1], weight3_ref[...])
        - complex_dot(later_ref[0], weight2_ref[...])
        - complex_dot(x, weight1_ref[...])
    )
    part_ref[...] = complex_dot(acc, inverse_ref[...])
    newest_ref[...] = x + x2_ref[0] + x3_ref[...]
    both_ref[0] = x
    both_ref[1] = later_ref[0]


def coupled(rhs, link_real, link_imag, x):
    real = rhs[:CHUNK] - (link_real * x[:CHUNK] - link_imag * x[CHUNK:])
    imag = rhs[CHUNK:] - (link_real * x[CHUNK:] + link_imag * x[:CHUNK])
    return jnp.concatenate([real, imag], axis=0)


def second_block(rhs_ref, link_ref, x):
    return coupled(
        rhs_ref[:, 0:BLOCK], link_ref[0:1, 0:BLOCK], link_ref[8:9, 0:BLOCK], x
    )


def second_slab(rhs_ref, link_ref, x, q):
    own = x[:, 0:SLAB]
    for s in range(1, GROUP):
        own = jnp.where(q == s, x[:, SLAB * s : SLAB * s + SLAB], own)
    end = BLOCK + SLAB
    return coupled(
        rhs_ref[:, BLOCK:end], link_ref[0:1, BLOCK:end], link_ref[8:9, BLOCK:end], own
    )


def couple_kernel(
    place_ref, rhs_ref, link_ref, p0, p1, p2, p3, own_ref, zero_ref, weight_ref, pass_ref, out_ref
):
    x0 = add_refs([p0, p1, p2, p3])
    slab = second_slab(rhs_ref, link_ref, own_ref[...], place_ref[1])
    out_ref[...] = slab - complex_dot(
        second_block(rhs_ref, link_ref, x0), weight_ref[...]
    )
    zero = place_ref[0] == 0
    pass_ref[0] = jnp.where(zero, zero_ref[0], x0)
    pass_ref[1] = jnp.where(zero, zero_ref[1], own_ref[...])


def second_one_kernel(
    place_ref,
    rhs_ref,
    link_ref,
    acc_ref,
    own_ref,
    sent_ref,
    got_ref,
    f0,
    f1,
    f2,
    f3,
    weight0_ref,
    weight1_ref,
    out_ref,
    keep_ref,
):
    plane, q = place_ref[0], place_ref[1]
    x0 = jnp.where(plane == 1, sent_ref[0], got_ref[0])
    for s in range(GROUP):
        keep_ref[GROUP + s] = x0[:, SLAB * s : SLAB * s + SLAB]
    slab = second_slab(rhs_ref, link_ref, own_ref[...], q)
    product = complex_dot(second_block(rhs_ref, link_ref, x0), weight0_ref[...])
    slabs = [f0[...], f1[...], f2[...], f3[...]]
    solved = slab - product - slabs_dot(slabs, weight1_ref, q, keep_ref)
    out_ref[...] = jnp.where(plane == 1, acc_ref[...], solved)


def joined(ref, first):
    return jnp.concatenate([ref[first + s] for s in range(GROUP)], axis=1)


def second_base_kernel(
    place_ref, rhs_ref, link_ref, acc_ref, got_ref, own_ref, weight_ref, out_ref
):
    plane, q = place_ref[0], place_ref[1]
    x0 = joined(got_ref, GROUP)
    own = jnp.where(plane == 0, x0, own_ref[...])
    slab = second_slab(rhs_ref, link_ref, own, q)
    product = complex_dot(second_block(rhs_ref, link_ref, x0), weight_ref[...])
    out_ref[...] = jnp.where(
        plane == 0, slab, jnp.where(plane == 3, slab - product, acc_ref[...])
    )


def cells_kernel(
    where_ref, got_ref, pass_ref, passed_ref, newest_ref, own_ref, both_zero, later_ref, x3_one, out_ref, front_ref, rows_ref
):
    plane = where_ref[SLAB]

    def pick(*by_plane):
        value = by_plane[0]
        for at in range(1, GROUP):
            value = jnp.where(plane == at, by_plane[at], value)
        return value

    last = joined(got_ref, GROUP)
    blocks = (
        pick(last, pass_ref[0], passed_ref[0], last),
        pick(newest_ref[...], own_ref[...], passed_ref[1], passed_ref[0]),
        pick(both_zero[1], newest_ref[...], own_ref[...], passed_ref[1]),
        pick(later_ref[1], x3_one[...], newest_ref[...], own_ref[...]),
    )
    for k, x in enumerate(blocks):
        for part in range(6):
            at = BLOCK * k + 128 * part
            piece = x[:, 128 * part : 128 * part + 128]
            wide = jnp.concatenate([piece, jnp.zeros((128 - ROWS, 128), f32)], axis=0)
            front_ref[at : at + 128, :] = wide.T
    rows_ref[...] = jnp.zeros_like(rows_ref)
    for c in range(8):
        for u in range(CELLS):
            rows_ref[64 + u : 65 + u, :] = front_ref[pl.ds(where_ref[CELLS * c + u], 1), :]
        out_ref[c] = rows_ref[...].T[:ROWS]


def second_two_kernel(
    place_ref, acc_ref, cells_ref, sent_ref, f0, f1, f2, f3, weight1_ref, weight2_ref, out_ref
):
    slabs = [f0[...], f1[...], f2[...], f3[...]]
    solved = (
        acc_ref[...]
        - sent_dot(sent_ref, weight1_ref)
        - slabs_dot(slabs, weight2_ref, place_ref[1])
    )
    lane = lax.broadcasted_iota(jnp.int32, (ROWS, 128), 1)
    tail = jnp.concatenate([solved[:, 128:], jnp.zeros((ROWS, 64), f32)], axis=1)
    for c in range(8):
        out_ref[c, :, 0:128] = solved[:, 0:128]
        out_ref[c, :, 128:256] = jnp.where(lane < 64, tail, cells_ref[c])


def out_kernel(place_ref, got_ref, solution_ref, forward_ref):
    for part in range(2):
        wide = got_ref[:, CHUNK * part : CHUNK * part + CHUNK, :].reshape(128, 256)
        forward_ref[part, 0:128, :] = wide[:, 0:128].T
        turned = wide[:, 128:256].T
        forward_ref[part, 128:SLAB, :] = turned[0:64]
        for y in range(4):
            solution_ref[part, y] = turned[64 + 6 * y : 70 + 6 * y]


def plane_send(value, *moves, turn=0):
    pairs = [
        (GROUP * source + q, GROUP * target + (q + turn) % GROUP)
        for source, target in moves
        for q in range(GROUP)
    ]
    return lax.ppermute(value, "row", pairs)


def plane_spread(value, source, target):
    return [plane_send(value, (source, target), turn=d) for d in range(GROUP)]


def after(value, arrived):
    return lax.optimization_barrier((value, arrived))[0]


def on_device(source1, source2, coupling, factor1, factor2, diag_inv, front_order):
    row_id = lax.axis_index("row")
    col_id = lax.axis_index("col")
    place = jnp.stack([row_id // GROUP, row_id % GROUP]).astype(jnp.int32)

    def gather_blocks(turned):
        return lax.all_gather(turned, "col").reshape(8, GROUP - 1, PIECE, 2 * SLAB)

    (turned1,) = call(
        turn_first_kernel,
        [SDS((3 * PIECE, 2 * SLAB), f32)],
        place,
        [],
        [(factor1, factor1.shape, lambda i, place: (0, 0, 0))],
        [pltpu.VMEM((4 * PIECE, 2 * SLAB), f32)],
    )
    matrix1 = gather_blocks(turned1)

    links = jnp.pad(coupling.reshape(2, CELLS), ((0, 0), (0, 32 - CELLS))).reshape(1, 64)
    links = jnp.pad(links, ((0, 0), (0, 64)))
    (packed,) = call(
        pack_kernel, [SDS((8, 16, 128), f32)], place, [source1, source2, links]
    )
    factor2 = after(factor2, packed)
    turned2 = factor2[:, :, : 3 * PIECE].reshape(2 * SLAB, 3 * PIECE).T
    packed = lax.all_to_all(packed, "col", 0, 0)
    early = jnp.broadcast_to(packed[:, :8].reshape(1, 64, 128), (16, 64, 128))
    early = lax.all_to_all(early, "row", 0, 0).reshape(1024, 128)
    late = packed[:, 8:].reshape(64, 128)
    late = jnp.broadcast_to(late[:, None], (64, LATE, 128)).reshape(64, LATE * 128)

    cell_y = front_order // 48
    cell_x = front_order % 48
    group_of = (cell_y // 4) * 64 + (cell_x // 6) * 8
    quarter = cell_y % 4
    inner = quarter * 6 + cell_x % 6
    every = jnp.stack([group_of + cell_x % 6, group_of + 6, quarter, inner])
    own = lax.dynamic_slice_in_dim(every, row_id * SLAB, SLAB, 1)
    every = jnp.concatenate([every[:, :BLOCK], own, jnp.zeros((4, 64), jnp.int32)], axis=1)
    where, mark = every[:2].reshape(2048), every[2:].astype(f32)
    rows_shape = SDS((ROWS, 1024), f32)
    rows_scratch = [pltpu.VMEM((1024, 128), f32)]
    (rhs,) = call(first_front_kernel, [rows_shape], where, [early, mark], scratch=rows_scratch)

    slab_shape = SDS((ROWS, SLAB), f32)
    block_shape = SDS((ROWS, BLOCK), f32)
    pair_shape = SDS((2, ROWS, BLOCK), f32)
    sent_shape = SDS((GROUP, ROWS, SLAB), f32)

    def load(matrix, numbers, arrived, second=False):
        matrix = after(matrix, arrived)
        blocks = [
            (
                matrix,
                (8, 1, PIECE, 2 * SLAB),
                (lambda i, place, n=number: (0, n, 0, 0))
                if second
                else (lambda i, place, n=number: (0, slot_of(place[0], n), 0, 0)),
            )
            for number in numbers
        ]
        shapes = [SDS((BLOCK, 2 * SLAB), f32)] * len(numbers)
        return call(load_kernel, shapes, place, [], blocks)

    first = [
        (matrix1, (8, 1, PIECE, 2 * SLAB), lambda i, place: (0, slot_of(place[0], 0), 0, 0))
    ]
    (acc,) = call(start_kernel, [slab_shape], place, [rhs], first)
    got = plane_spread(acc, 1, 2)
    late, turned2, diag_inv = after((late, turned2, diag_inv), acc)
    late = lax.all_gather(late, "row")
    matrix2 = gather_blocks(turned2)
    weights = load(matrix1, [1], acc)
    inverse = diag_inv.reshape(2 * BLOCK, SLAB).T
    acc, kept = call(
        forward_one_kernel, [slab_shape, sent_shape], place, [acc, *got, *weights]
    )
    sent = plane_send(kept, (2, 3))
    got = plane_spread(acc, 2, 3)
    weights = [*weights, *load(matrix1, [2], acc)]
    acc, part = call(
        forward_two_kernel,
        [slab_shape, block_shape],
        place,
        [acc, inverse, sent, *got, *weights],
    )
    got = plane_spread(part, 3, 2)
    block2 = weights[1]
    weights = load(matrix1, [3], part)
    x3_two, acc, part = call(
        back_three_kernel,
        [block_shape, slab_shape, block_shape],
        place,
        [acc, inverse, *got, *weights],
    )
    x3_one = plane_send(x3_two, (2, 1))
    got = plane_spread(part, 2, 1)
    weights = [block2, *weights]
    both_one, acc, part = call(
        back_two_kernel,
        [pair_shape, slab_shape, block_shape],
        place,
        [acc, inverse, *got, x3_one, *weights],
    )
    later = plane_send(both_one, (1, 0))
    got = plane_spread(part, 1, 0)
    weights = [*load(matrix1, [1], part), *weights]
    newest, both_zero, part = call(
        back_one_kernel,
        [block_shape, pair_shape, block_shape],
        place,
        [acc, inverse, *got, later, both_one, x3_two, *weights],
    )
    own = plane_send(newest, (0, 1), (1, 2), (2, 3))
    got = plane_spread(part, 0, 1)
    late = after(late, part)
    rhs, link = call(
        second_front_kernel,
        [rows_shape, SDS((16, 1024), f32)],
        where,
        [mark],
        [(late, (16, 64, 128), lambda i, place: (0, 0, 0))],
        scratch=rows_scratch * 2,
    )
    weights = load(matrix2, [0], part, True)
    passing, acc = call(
        couple_kernel,
        [pair_shape, slab_shape],
        place,
        [rhs, link, *got, own, both_zero, *weights],
    )
    passed = plane_send(passing, (1, 2), (0, 3))
    got = plane_spread(acc, 1, 2)
    weights = [*weights, *load(matrix2, [1], acc, True)]
    acc, kept = call(
        second_one_kernel,
        [slab_shape, SDS((2 * GROUP, ROWS, SLAB), f32)],
        place,
        [rhs, link, acc, own, passing, passed, *got, *weights],
    )
    sent = plane_send(kept, (2, 3), (1, 0))
    got = plane_spread(acc, 2, 3)
    weights = [*weights, *load(matrix2, [2], acc, True)]
    (acc,) = call(
        second_base_kernel,
        [slab_shape],
        place,
        [rhs, link, acc, sent, own, weights[0]],
    )

    at = jnp.arange(SLAB, dtype=jnp.int32)
    own_c, own_y, own_x = at // CELLS, at % CELLS // 6, at % 6
    own_cells = (row_id * 4 + own_y) * 48 + own_c * 6 + own_x
    hits = front_order[None, :] == own_cells[:, None]
    slots = jnp.sum(jnp.where(hits, jnp.arange(4 * BLOCK, dtype=jnp.int32)[None, :], 0), axis=1)
    (mine,) = call(
        cells_kernel,
        [SDS((8, ROWS, 128), f32)],
        jnp.concatenate([slots, place]),
        [sent, passing, passed, newest, own, both_zero, later, x3_one],
        scratch=[pltpu.VMEM((4 * BLOCK, 128), f32), pltpu.VMEM((128, 128), f32)],
    )
    (last,) = call(
        second_two_kernel,
        [SDS((8, ROWS, 256), f32)],
        place,
        [acc, mine, sent, *got, *weights[1:]],
    )
    arrived = lax.all_to_all(last, "col", 0, 0)
    return call(
        out_kernel,
        [SDS((2, 4, 6, 128), f32), SDS((2, SLAB, 128), f32)],
        place,
        [arrived],
    )


def solution(mesh):
    in_specs = (
        P(None, "row", "col", None),
        P(None, "row", "col", None),
        P(None, "row", "col"),
        P(None, "row", "col"),
        P(None, "row", "col"),
        P(None, None, "row"),
        P(),
    )
    out_specs = (P(None, "row", "col", None), P(None, "row", None))
    return jax.shard_map(
        on_device, mesh=mesh, in_specs=in_specs, out_specs=out_specs, check_vma=False
    )
```

```python
import functools

import jax
import jax.numpy as jnp
from jax import lax
from jax.experimental import pallas as pl
from jax.experimental.pallas import tpu as pltpu
from jax.sharding import PartitionSpec as P

GROUP = 4
CHUNK = 16
ROWS = 2 * CHUNK
SLAB = 192
BLOCK = 768
PIECE = 96
CELLS = 24
LATE = 2
VMEM = 16 * 1024 * 1024

SDS = jax.ShapeDtypeStruct
f32 = jnp.float32


def split(value):
    high = value.astype(jnp.bfloat16)
    return high, (value - high.astype(f32)).astype(jnp.bfloat16)


def complex_dot(vector, weight):
    weight_high, weight_low = split(weight)
    half = weight.shape[1] // 2
    high, low = split(vector)
    both = jnp.dot(
        jnp.concatenate([high, low], axis=0), weight_high, preferred_element_type=f32
    )
    total = both[:ROWS] + both[ROWS:] + jnp.dot(high, weight_low, preferred_element_type=f32)
    real = total[:CHUNK, :half] - total[CHUNK:, half:]
    imag = total[:CHUNK, half:] + total[CHUNK:, :half]
    return jnp.concatenate([real, imag], axis=0)


def slot_of(plane, block):
    return jnp.minimum(jnp.where(plane < block, block - 1, block), GROUP - 2)


def slab_weight(ref, source):
    at = pl.multiple_of(SLAB * source, SLAB)
    return ref[pl.ds(at, SLAB), :]


def slabs_dot(slabs, ref, q, keep=None):
    total = None
    for d, slab in enumerate(slabs):
        source = lax.rem(q - d + GROUP, GROUP)
        if keep is not None:
            keep[source] = slab
        part = complex_dot(slab, slab_weight(ref, source))
        total = part if total is None else total + part
    return total


def sent_dot(sent_ref, ref):
    total = None
    for s in range(GROUP):
        part = complex_dot(sent_ref[s], slab_weight(ref, s))
        total = part if total is None else total + part
    return total


def add_refs(refs):
    total = refs[0][...]
    for ref in refs[1:]:
        total = total + ref[...]
    return total


def call(body, out_shape, scalars, inputs, blocks=(), scratch=(), last=False):
    vmem = pl.BlockSpec(memory_space=pltpu.VMEM)
    specs = [vmem] * len(inputs)
    for _, shape, at in blocks:
        specs.append(pl.BlockSpec(shape, at, pipeline_mode=pl.Buffered(1)))
    near = [pltpu.with_memory_space_constraint(value, pltpu.VMEM) for value in inputs]
    far = [pltpu.with_memory_space_constraint(array, pltpu.HBM) for array, _, _ in blocks]
    outs = (vmem,) * len(out_shape)
    shapes = tuple(pltpu.VMEM(shape.shape, shape.dtype) for shape in out_shape)
    if last:
        outs = tuple(
            pl.BlockSpec(shape.shape, lambda i, place, n=len(shape.shape): (0,) * n)
            for shape in out_shape
        )
        shapes = tuple(pltpu.HBM(shape.shape, shape.dtype) for shape in out_shape)
    return pl.pallas_call(
        body,
        grid_spec=pltpu.PrefetchScalarGridSpec(
            num_scalar_prefetch=1,
            grid=(1,),
            in_specs=specs,
            out_specs=outs,
            scratch_shapes=scratch,
        ),
        out_shape=shapes,
        compiler_params=pltpu.CompilerParams(vmem_limit_bytes=VMEM),
    )(scalars, *near, *far)


def turn_first_kernel(place_ref, factor_ref, out_ref, turned_ref):
    rows = factor_ref[...].reshape(2 * SLAB, 4 * PIECE)
    for part in range(3):
        turned_ref[128 * part : 128 * part + 128, :] = rows[:, 128 * part : 128 * part + 128].T
    for slot in range(GROUP - 1):
        block = slot + jnp.where(place_ref[0] > slot, 0, 1)
        out_ref[PIECE * slot : PIECE * slot + PIECE, :] = turned_ref[pl.ds(block * PIECE, PIECE), :]


def pack_kernel(place_ref, first_ref, second_ref, link_ref, out_ref):
    lane = lax.broadcasted_iota(jnp.int32, (6, 128), 1)
    for at_row, ref in ((0, first_ref), (8, second_ref)):
        parts = [ref[part, y] for y in range(4) for part in range(2)]
        for c in range(8):
            row = jnp.zeros((6, 128), f32)
            for at, part in enumerate(parts):
                shift = (16 * at - 16 * c) % 128
                moved = pltpu.roll(part, shift, 1) if shift else part
                row = jnp.where((lane >= 16 * at) & (lane < 16 * at + 16), moved, row)
            out_ref[c, at_row : at_row + 6, :] = row
            out_ref[c, at_row + 6 : at_row + 8, :] = jnp.broadcast_to(link_ref[...], (2, 128))


def gather_rows(where_ref, first, cells_ref, rows_ref):
    def some(step, carry):
        for u in range(16):
            at = step * 16 + u
            rows_ref[pl.ds(at, 1), :] = cells_ref[pl.ds(where_ref[first + at], 1), :]
        return carry

    lax.fori_loop(0, 64, some, 0)


def turn_rows(rows_ref, mark_ref, rhs_ref):
    for part in range(8):
        at = slice(128 * part, 128 * part + 128)
        turned = rows_ref[at, :].T
        quarter = mark_ref[0:1, at]
        value = turned[0:32]
        for y in range(1, 4):
            value = jnp.where(quarter == y, turned[32 * y : 32 * y + 32], value)
        rhs_ref[:, at] = value


def first_front_kernel(where_ref, cells_ref, mark_ref, rhs_ref, rows_ref):
    gather_rows(where_ref, 0, cells_ref, rows_ref)
    turn_rows(rows_ref, mark_ref, rhs_ref)


def second_front_kernel(where_ref, mark_ref, late_ref, rhs_ref, link_ref, cells_ref, rows_ref):
    cells_ref[...] = late_ref[...].reshape(1024, 128)
    gather_rows(where_ref, 0, cells_ref, rows_ref)
    turn_rows(rows_ref, mark_ref, rhs_ref)
    gather_rows(where_ref, 1024, cells_ref, rows_ref)
    lane = lax.broadcasted_iota(jnp.int32, (32, 128), 0).astype(f32)
    for part in range(8):
        at = slice(128 * part, 128 * part + 128)
        turned = rows_ref[at, :].T
        own = mark_ref[1:2, at] == lane
        real = jnp.sum(jnp.where(own, turned[0:32], 0.0), axis=0, keepdims=True)
        imag = jnp.sum(jnp.where(own, turned[32:64], 0.0), axis=0, keepdims=True)
        link_ref[0:8, at] = jnp.broadcast_to(real, (8, 128))
        link_ref[8:16, at] = jnp.broadcast_to(imag, (8, 128))


def load_kernel(place_ref, *refs):
    count = len(refs) // 2
    for block_ref, out_ref in zip(refs[:count], refs[count:]):
        out_ref[...] = block_ref[:, 0].reshape(BLOCK, 2 * SLAB)


def start_kernel(place_ref, rhs_ref, weight_ref, acc_ref):
    product = complex_dot(rhs_ref[:, 0:BLOCK], weight_ref[:, 0].reshape(BLOCK, 2 * SLAB))
    slab = rhs_ref[:, BLOCK : BLOCK + SLAB]
    acc_ref[...] = jnp.where(place_ref[0] > 0, slab - product, slab)


def forward_one_kernel(place_ref, acc_ref, y0, y1, y2, y3, weight_ref, out_ref, keep_ref):
    slabs = [y0[...], y1[...], y2[...], y3[...]]
    out_ref[...] = acc_ref[...] - slabs_dot(slabs, weight_ref, place_ref[1], keep_ref)


def forward_two_kernel(
    place_ref, acc_ref, inverse_ref, sent_ref, y0, y1, y2, y3, weight1_ref, weight2_ref, out_ref, part_ref
):
    slabs = [y0[...], y1[...], y2[...], y3[...]]
    solved = (
        acc_ref[...]
        - sent_dot(sent_ref, weight1_ref)
        - slabs_dot(slabs, weight2_ref, place_ref[1])
    )
    out_ref[...] = solved
    part_ref[...] = complex_dot(solved, inverse_ref[...])


def back_three_kernel(
    place_ref,
    acc_ref,
    inverse_ref,
    p0,
    p1,
    p2,
    p3,
    weight_ref,
    x_ref,
    acc_out_ref,
    part_ref,
):
    x = add_refs([p0, p1, p2, p3])
    acc = acc_ref[...] - complex_dot(x, weight_ref[...])
    x_ref[...] = x
    acc_out_ref[...] = acc
    part_ref[...] = complex_dot(acc, inverse_ref[...])


def back_two_kernel(
    place_ref,
    acc_ref,
    inverse_ref,
    p0,
    p1,
    p2,
    p3,
    x3_ref,
    weight2_ref,
    weight3_ref,
    both_ref,
    acc_out_ref,
    part_ref,
):
    x = add_refs([p0, p1, p2, p3])
    acc = (
        acc_ref[...]
        - complex_dot(x3_ref[...], weight3_ref[...])
        - complex_dot(x, weight2_ref[...])
    )
    both_ref[0] = x
    both_ref[1] = x3_ref[...]
    acc_out_ref[...] = acc
    part_ref[...] = complex_dot(acc, inverse_ref[...])


def back_one_kernel(
    place_ref,
    acc_ref,
    inverse_ref,
    p0,
    p1,
    p2,
    p3,
    later_ref,
    x2_ref,
    x3_ref,
    weight1_ref,
    weight2_ref,
    weight3_ref,
    newest_ref,
    both_ref,
    part_ref,
):
    x = add_refs([p0, p1, p2, p3])
    acc = (
        acc_ref[...]
        - complex_dot(later_ref[1], weight3_ref[...])
        - complex_dot(later_ref[0], weight2_ref[...])
        - complex_dot(x, weight1_ref[...])
    )
    part_ref[...] = complex_dot(acc, inverse_ref[...])
    newest_ref[...] = x + x2_ref[0] + x3_ref[...]
    both_ref[0] = x
    both_ref[1] = later_ref[0]


def coupled(rhs, link_real, link_imag, x):
    real = rhs[:CHUNK] - (link_real * x[:CHUNK] - link_imag * x[CHUNK:])
    imag = rhs[CHUNK:] - (link_real * x[CHUNK:] + link_imag * x[:CHUNK])
    return jnp.concatenate([real, imag], axis=0)


def second_block(rhs_ref, link_ref, x):
    return coupled(
        rhs_ref[:, 0:BLOCK], link_ref[0:1, 0:BLOCK], link_ref[8:9, 0:BLOCK], x
    )


def second_slab(rhs_ref, link_ref, x, q):
    own = x[:, 0:SLAB]
    for s in range(1, GROUP):
        own = jnp.where(q == s, x[:, SLAB * s : SLAB * s + SLAB], own)
    end = BLOCK + SLAB
    return coupled(
        rhs_ref[:, BLOCK:end], link_ref[0:1, BLOCK:end], link_ref[8:9, BLOCK:end], own
    )


def couple_kernel(
    place_ref, rhs_ref, link_ref, p0, p1, p2, p3, own_ref, zero_ref, weight_ref, pass_ref, out_ref
):
    x0 = add_refs([p0, p1, p2, p3])
    slab = second_slab(rhs_ref, link_ref, own_ref[...], place_ref[1])
    out_ref[...] = slab - complex_dot(
        second_block(rhs_ref, link_ref, x0), weight_ref[...]
    )
    zero = place_ref[0] == 0
    pass_ref[0] = jnp.where(zero, zero_ref[0], x0)
    pass_ref[1] = jnp.where(zero, zero_ref[1], own_ref[...])


def second_one_kernel(
    place_ref,
    rhs_ref,
    link_ref,
    acc_ref,
    own_ref,
    sent_ref,
    got_ref,
    f0,
    f1,
    f2,
    f3,
    weight0_ref,
    weight1_ref,
    out_ref,
    keep_ref,
):
    plane, q = place_ref[0], place_ref[1]
    x0 = jnp.where(plane == 1, sent_ref[0], got_ref[0])
    for s in range(GROUP):
        keep_ref[GROUP + s] = x0[:, SLAB * s : SLAB * s + SLAB]
    slab = second_slab(rhs_ref, link_ref, own_ref[...], q)
    product = complex_dot(second_block(rhs_ref, link_ref, x0), weight0_ref[...])
    slabs = [f0[...], f1[...], f2[...], f3[...]]
    solved = slab - product - slabs_dot(slabs, weight1_ref, q, keep_ref)
    out_ref[...] = jnp.where(plane == 1, acc_ref[...], solved)


def joined(ref, first):
    return jnp.concatenate([ref[first + s] for s in range(GROUP)], axis=1)


def second_base_kernel(
    place_ref, rhs_ref, link_ref, acc_ref, got_ref, own_ref, weight_ref, out_ref
):
    plane, q = place_ref[0], place_ref[1]
    x0 = joined(got_ref, GROUP)
    own = jnp.where(plane == 0, x0, own_ref[...])
    slab = second_slab(rhs_ref, link_ref, own, q)
    product = complex_dot(second_block(rhs_ref, link_ref, x0), weight_ref[...])
    out_ref[...] = jnp.where(
        plane == 0, slab, jnp.where(plane == 3, slab - product, acc_ref[...])
    )


def cells_kernel(
    where_ref, got_ref, pass_ref, passed_ref, newest_ref, own_ref, both_zero, later_ref, x3_one, out_ref, front_ref, rows_ref
):
    plane = where_ref[SLAB]

    def pick(*by_plane):
        value = by_plane[0]
        for at in range(1, GROUP):
            value = jnp.where(plane == at, by_plane[at], value)
        return value

    last = joined(got_ref, GROUP)
    blocks = (
        pick(last, pass_ref[0], passed_ref[0], last),
        pick(newest_ref[...], own_ref[...], passed_ref[1], passed_ref[0]),
        pick(both_zero[1], newest_ref[...], own_ref[...], passed_ref[1]),
        pick(later_ref[1], x3_one[...], newest_ref[...], own_ref[...]),
    )
    for k, x in enumerate(blocks):
        for part in range(6):
            at = BLOCK * k + 128 * part
            piece = x[:, 128 * part : 128 * part + 128]
            wide = jnp.concatenate([piece, jnp.zeros((128 - ROWS, 128), f32)], axis=0)
            front_ref[at : at + 128, :] = wide.T
    rows_ref[...] = jnp.zeros_like(rows_ref)
    for c in range(8):
        for u in range(CELLS):
            rows_ref[64 + u : 65 + u, :] = front_ref[pl.ds(where_ref[CELLS * c + u], 1), :]
        out_ref[c] = rows_ref[...].T[:ROWS]


def second_two_kernel(
    place_ref, acc_ref, cells_ref, sent_ref, f0, f1, f2, f3, weight1_ref, weight2_ref, out_ref
):
    slabs = [f0[...], f1[...], f2[...], f3[...]]
    solved = (
        acc_ref[...]
        - sent_dot(sent_ref, weight1_ref)
        - slabs_dot(slabs, weight2_ref, place_ref[1])
    )
    lane = lax.broadcasted_iota(jnp.int32, (ROWS, 128), 1)
    tail = jnp.concatenate([solved[:, 128:], jnp.zeros((ROWS, 64), f32)], axis=1)
    for c in range(8):
        out_ref[c, :, 0:128] = solved[:, 0:128]
        out_ref[c, :, 128:256] = jnp.where(lane < 64, tail, cells_ref[c])


def out_kernel(place_ref, got_ref, solution_ref, forward_ref):
    for part in range(2):
        wide = got_ref[:, CHUNK * part : CHUNK * part + CHUNK, :].reshape(128, 256)
        forward_ref[part, 0:128, :] = wide[:, 0:128].T
        turned = wide[:, 128:256].T
        forward_ref[part, 128:SLAB, :] = turned[0:64]
        for y in range(4):
            solution_ref[part, y] = turned[64 + 6 * y : 70 + 6 * y]


def plane_send(value, *moves, turn=0):
    pairs = [
        (GROUP * source + q, GROUP * target + (q + turn) % GROUP)
        for source, target in moves
        for q in range(GROUP)
    ]
    return lax.ppermute(value, "row", pairs)


def plane_spread(value, source, target):
    return [plane_send(value, (source, target), turn=d) for d in range(GROUP)]


def after(value, arrived):
    return lax.optimization_barrier((value, arrived))[0]


def on_device(source1, source2, coupling, factor1, factor2, diag_inv, front_order):
    row_id = lax.axis_index("row")
    col_id = lax.axis_index("col")
    place = jnp.stack([row_id // GROUP, row_id % GROUP]).astype(jnp.int32)

    def gather_blocks(turned):
        return lax.all_gather(turned, "col").reshape(8, GROUP - 1, PIECE, 2 * SLAB)

    (turned1,) = call(
        turn_first_kernel,
        [SDS((3 * PIECE, 2 * SLAB), f32)],
        place,
        [],
        [(factor1, factor1.shape, lambda i, place: (0, 0, 0))],
        [pltpu.VMEM((4 * PIECE, 2 * SLAB), f32)],
    )
    matrix1 = gather_blocks(turned1)

    links = jnp.pad(coupling.reshape(2, CELLS), ((0, 0), (0, 32 - CELLS))).reshape(1, 64)
    links = jnp.pad(links, ((0, 0), (0, 64)))
    (packed,) = call(
        pack_kernel, [SDS((8, 16, 128), f32)], place, [source1, source2, links]
    )
    factor2 = after(factor2, packed)
    turned2 = factor2[:, :, : 3 * PIECE].reshape(2 * SLAB, 3 * PIECE).T
    packed = lax.all_to_all(packed, "col", 0, 0)
    early = jnp.broadcast_to(packed[:, :8].reshape(1, 64, 128), (16, 64, 128))
    early = lax.all_to_all(early, "row", 0, 0).reshape(1024, 128)
    late = packed[:, 8:].reshape(64, 128)
    late = jnp.broadcast_to(late[:, None], (64, LATE, 128)).reshape(64, LATE * 128)

    cell_y = front_order // 48
    cell_x = front_order % 48
    group_of = (cell_y // 4) * 64 + (cell_x // 6) * 8
    quarter = cell_y % 4
    inner = quarter * 6 + cell_x % 6
    every = jnp.stack([group_of + cell_x % 6, group_of + 6, quarter, inner])
    own = lax.dynamic_slice_in_dim(every, row_id * SLAB, SLAB, 1)
    every = jnp.concatenate([every[:, :BLOCK], own, jnp.zeros((4, 64), jnp.int32)], axis=1)
    where, mark = every[:2].reshape(2048), every[2:].astype(f32)
    rows_shape = SDS((ROWS, 1024), f32)
    rows_scratch = [pltpu.VMEM((1024, 128), f32)]
    (rhs,) = call(first_front_kernel, [rows_shape], where, [early, mark], scratch=rows_scratch)

    slab_shape = SDS((ROWS, SLAB), f32)
    block_shape = SDS((ROWS, BLOCK), f32)
    pair_shape = SDS((2, ROWS, BLOCK), f32)
    sent_shape = SDS((GROUP, ROWS, SLAB), f32)

    def load(matrix, numbers, arrived, second=False):
        matrix = after(matrix, arrived)
        blocks = [
            (
                matrix,
                (8, 1, PIECE, 2 * SLAB),
                (lambda i, place, n=number: (0, n, 0, 0))
                if second
                else (lambda i, place, n=number: (0, slot_of(place[0], n), 0, 0)),
            )
            for number in numbers
        ]
        shapes = [SDS((BLOCK, 2 * SLAB), f32)] * len(numbers)
        return call(load_kernel, shapes, place, [], blocks)

    first = [
        (matrix1, (8, 1, PIECE, 2 * SLAB), lambda i, place: (0, slot_of(place[0], 0), 0, 0))
    ]
    (acc,) = call(start_kernel, [slab_shape], place, [rhs], first)
    got = plane_spread(acc, 1, 2)
    late, turned2, diag_inv = after((late, turned2, diag_inv), acc)
    late = lax.all_gather(late, "row")
    matrix2 = gather_blocks(turned2)
    weights = load(matrix1, [1], acc)
    inverse = diag_inv.reshape(2 * BLOCK, SLAB).T
    acc, kept = call(
        forward_one_kernel, [slab_shape, sent_shape], place, [acc, *got, *weights]
    )
    sent = plane_send(kept, (2, 3))
    got = plane_spread(acc, 2, 3)
    weights = [*weights, *load(matrix1, [2], acc)]
    acc, part = call(
        forward_two_kernel,
        [slab_shape, block_shape],
        place,
        [acc, inverse, sent, *got, *weights],
    )
    got = plane_spread(part, 3, 2)
    block2 = weights[1]
    weights = load(matrix1, [3], part)
    x3_two, acc, part = call(
        back_three_kernel,
        [block_shape, slab_shape, block_shape],
        place,
        [acc, inverse, *got, *weights],
    )
    x3_one = plane_send(x3_two, (2, 1))
    got = plane_spread(part, 2, 1)
    weights = [block2, *weights]
    both_one, acc, part = call(
        back_two_kernel,
        [pair_shape, slab_shape, block_shape],
        place,
        [acc, inverse, *got, x3_one, *weights],
    )
    later = plane_send(both_one, (1, 0))
    got = plane_spread(part, 1, 0)
    weights = [*load(matrix1, [1], part), *weights]
    newest, both_zero, part = call(
        back_one_kernel,
        [block_shape, pair_shape, block_shape],
        place,
        [acc, inverse, *got, later, both_one, x3_two, *weights],
    )
    own = plane_send(newest, (0, 1), (1, 2), (2, 3))
    got = plane_spread(part, 0, 1)
    late = after(late, part)
    rhs, link = call(
        second_front_kernel,
        [rows_shape, SDS((16, 1024), f32)],
        where,
        [mark],
        [(late, (16, 64, 128), lambda i, place: (0, 0, 0))],
        scratch=rows_scratch * 2,
    )
    weights = load(matrix2, [0], part, True)
    passing, acc = call(
        couple_kernel,
        [pair_shape, slab_shape],
        place,
        [rhs, link, *got, own, both_zero, *weights],
    )
    passed = plane_send(passing, (1, 2), (0, 3))
    got = plane_spread(acc, 1, 2)
    weights = [*weights, *load(matrix2, [1, 2], acc, True)]
    acc, kept = call(
        second_one_kernel,
        [slab_shape, SDS((2 * GROUP, ROWS, SLAB), f32)],
        place,
        [rhs, link, acc, own, passing, passed, *got, *weights[:2]],
    )
    sent = plane_send(kept, (2, 3), (1, 0))
    got = plane_spread(acc, 2, 3)
    (acc,) = call(
        second_base_kernel,
        [slab_shape],
        place,
        [rhs, link, acc, sent, own, weights[0]],
    )

    at = jnp.arange(SLAB, dtype=jnp.int32)
    own_c, own_y, own_x = at // CELLS, at % CELLS // 6, at % 6
    own_cells = (row_id * 4 + own_y) * 48 + own_c * 6 + own_x
    hits = front_order[None, :] == own_cells[:, None]
    slots = jnp.sum(jnp.where(hits, jnp.arange(4 * BLOCK, dtype=jnp.int32)[None, :], 0), axis=1)
    (mine,) = call(
        cells_kernel,
        [SDS((8, ROWS, 128), f32)],
        jnp.concatenate([slots, place]),
        [sent, passing, passed, newest, own, both_zero, later, x3_one],
        scratch=[pltpu.VMEM((4 * BLOCK, 128), f32), pltpu.VMEM((128, 128), f32)],
    )
    (last,) = call(
        second_two_kernel,
        [SDS((8, ROWS, 256), f32)],
        place,
        [acc, mine, sent, *got, *weights[1:]],
    )
    arrived = lax.all_to_all(last, "col", 0, 0)
    return call(
        out_kernel,
        [SDS((2, 4, 6, 128), f32), SDS((2, SLAB, 128), f32)],
        place,
        [arrived],
        last=True,
    )


def solution(mesh):
    in_specs = (
        P(None, "row", "col", None),
        P(None, "row", "col", None),
        P(None, "row", "col"),
        P(None, "row", "col"),
        P(None, "row", "col"),
        P(None, None, "row"),
        P(),
    )
    out_specs = (P(None, "row", "col", None), P(None, "row", None))
    return jax.shard_map(
        on_device, mesh=mesh, in_specs=in_specs, out_specs=out_specs, check_vma=False
    )
```

```python
import functools

import jax
import jax.numpy as jnp
from jax import lax
from jax.experimental import pallas as pl
from jax.experimental.pallas import tpu as pltpu
from jax.sharding import PartitionSpec as P

GROUP = 4
CHUNK = 16
ROWS = 2 * CHUNK
SLAB = 192
BLOCK = 768
PIECE = 96
CELLS = 24
LATE = 2
VMEM = 16 * 1024 * 1024

SDS = jax.ShapeDtypeStruct
f32 = jnp.float32


def split(value):
    high = value.astype(jnp.bfloat16)
    return high, (value - high.astype(f32)).astype(jnp.bfloat16)


def complex_dot(vector, weight):
    weight_high, weight_low = split(weight)
    half = weight.shape[1] // 2
    high, low = split(vector)
    both = jnp.dot(
        jnp.concatenate([high, low], axis=0), weight_high, preferred_element_type=f32
    )
    total = both[:ROWS] + both[ROWS:] + jnp.dot(high, weight_low, preferred_element_type=f32)
    real = total[:CHUNK, :half] - total[CHUNK:, half:]
    imag = total[:CHUNK, half:] + total[CHUNK:, :half]
    return jnp.concatenate([real, imag], axis=0)


def slot_of(plane, block):
    return jnp.minimum(jnp.where(plane < block, block - 1, block), GROUP - 2)


def slab_weight(ref, source):
    at = pl.multiple_of(SLAB * source, SLAB)
    return ref[pl.ds(at, SLAB), :]


def slabs_dot(slabs, ref, q, keep=None):
    total = None
    for d, slab in enumerate(slabs):
        source = lax.rem(q - d + GROUP, GROUP)
        if keep is not None:
            keep[source] = slab
        part = complex_dot(slab, slab_weight(ref, source))
        total = part if total is None else total + part
    return total


def sent_dot(sent_ref, ref):
    total = None
    for s in range(GROUP):
        part = complex_dot(sent_ref[s], slab_weight(ref, s))
        total = part if total is None else total + part
    return total


def add_refs(refs):
    total = refs[0][...]
    for ref in refs[1:]:
        total = total + ref[...]
    return total


def call(body, out_shape, scalars, inputs, blocks=(), scratch=(), last=False):
    vmem = pl.BlockSpec(memory_space=pltpu.VMEM)
    specs = [vmem] * len(inputs)
    for _, shape, at in blocks:
        specs.append(pl.BlockSpec(shape, at, pipeline_mode=pl.Buffered(1)))
    near = [pltpu.with_memory_space_constraint(value, pltpu.VMEM) for value in inputs]
    far = [pltpu.with_memory_space_constraint(array, pltpu.HBM) for array, _, _ in blocks]
    outs = (vmem,) * len(out_shape)
    shapes = tuple(pltpu.VMEM(shape.shape, shape.dtype) for shape in out_shape)
    if last:
        outs = tuple(
            pl.BlockSpec(shape.shape, lambda i, place, n=len(shape.shape): (0,) * n)
            for shape in out_shape
        )
        shapes = tuple(pltpu.HBM(shape.shape, shape.dtype) for shape in out_shape)
    return pl.pallas_call(
        body,
        grid_spec=pltpu.PrefetchScalarGridSpec(
            num_scalar_prefetch=1,
            grid=(1,),
            in_specs=specs,
            out_specs=outs,
            scratch_shapes=scratch,
        ),
        out_shape=shapes,
        compiler_params=pltpu.CompilerParams(vmem_limit_bytes=VMEM),
    )(scalars, *near, *far)


def turn_first_kernel(place_ref, factor_ref, out_ref, turned_ref):
    rows = factor_ref[...].reshape(2 * SLAB, 4 * PIECE)
    for part in range(3):
        turned_ref[128 * part : 128 * part + 128, :] = rows[:, 128 * part : 128 * part + 128].T
    for slot in range(GROUP - 1):
        block = slot + jnp.where(place_ref[0] > slot, 0, 1)
        out_ref[PIECE * slot : PIECE * slot + PIECE, :] = turned_ref[pl.ds(block * PIECE, PIECE), :]


def pack_kernel(place_ref, first_ref, second_ref, link_ref, out_ref):
    lane = lax.broadcasted_iota(jnp.int32, (6, 128), 1)
    for at_row, ref in ((0, first_ref), (8, second_ref)):
        parts = [ref[part, y] for y in range(4) for part in range(2)]
        for c in range(8):
            row = jnp.zeros((6, 128), f32)
            for at, part in enumerate(parts):
                shift = (16 * at - 16 * c) % 128
                moved = pltpu.roll(part, shift, 1) if shift else part
                row = jnp.where((lane >= 16 * at) & (lane < 16 * at + 16), moved, row)
            out_ref[c, at_row : at_row + 6, :] = row
            out_ref[c, at_row + 6 : at_row + 8, :] = jnp.broadcast_to(link_ref[...], (2, 128))


def gather_rows(where_ref, first, cells_ref, rows_ref):
    def some(step, carry):
        for u in range(16):
            at = step * 16 + u
            rows_ref[pl.ds(at, 1), :] = cells_ref[pl.ds(where_ref[first + at], 1), :]
        return carry

    lax.fori_loop(0, 64, some, 0)


def turn_rows(rows_ref, mark_ref, rhs_ref):
    for part in range(8):
        at = slice(128 * part, 128 * part + 128)
        turned = rows_ref[at, :].T
        quarter = mark_ref[0:1, at]
        value = turned[0:32]
        for y in range(1, 4):
            value = jnp.where(quarter == y, turned[32 * y : 32 * y + 32], value)
        rhs_ref[:, at] = value


def first_front_kernel(where_ref, cells_ref, mark_ref, rhs_ref, rows_ref):
    gather_rows(where_ref, 0, cells_ref, rows_ref)
    turn_rows(rows_ref, mark_ref, rhs_ref)


def second_front_kernel(where_ref, mark_ref, late_ref, rhs_ref, link_ref, cells_ref, rows_ref):
    cells_ref[...] = late_ref[...].reshape(1024, 128)
    gather_rows(where_ref, 0, cells_ref, rows_ref)
    turn_rows(rows_ref, mark_ref, rhs_ref)
    gather_rows(where_ref, 1024, cells_ref, rows_ref)
    lane = lax.broadcasted_iota(jnp.int32, (32, 128), 0).astype(f32)
    for part in range(8):
        at = slice(128 * part, 128 * part + 128)
        turned = rows_ref[at, :].T
        own = mark_ref[1:2, at] == lane
        real = jnp.sum(jnp.where(own, turned[0:32], 0.0), axis=0, keepdims=True)
        imag = jnp.sum(jnp.where(own, turned[32:64], 0.0), axis=0, keepdims=True)
        link_ref[0:8, at] = jnp.broadcast_to(real, (8, 128))
        link_ref[8:16, at] = jnp.broadcast_to(imag, (8, 128))


def load_kernel(place_ref, *refs):
    count = len(refs) // 2
    for block_ref, out_ref in zip(refs[:count], refs[count:]):
        out_ref[...] = block_ref[:, 0].reshape(BLOCK, 2 * SLAB)


def start_kernel(place_ref, rhs_ref, weight_ref, acc_ref):
    product = complex_dot(rhs_ref[:, 0:BLOCK], weight_ref[:, 0].reshape(BLOCK, 2 * SLAB))
    slab = rhs_ref[:, BLOCK : BLOCK + SLAB]
    acc_ref[...] = jnp.where(place_ref[0] > 0, slab - product, slab)


def forward_one_kernel(place_ref, acc_ref, y0, y1, y2, y3, weight_ref, out_ref, keep_ref):
    slabs = [y0[...], y1[...], y2[...], y3[...]]
    out_ref[...] = acc_ref[...] - slabs_dot(slabs, weight_ref, place_ref[1], keep_ref)


def forward_two_kernel(
    place_ref, acc_ref, inverse_ref, sent_ref, y0, y1, y2, y3, weight1_ref, weight2_ref, out_ref, part_ref
):
    slabs = [y0[...], y1[...], y2[...], y3[...]]
    solved = (
        acc_ref[...]
        - sent_dot(sent_ref, weight1_ref)
        - slabs_dot(slabs, weight2_ref, place_ref[1])
    )
    out_ref[...] = solved
    part_ref[...] = complex_dot(solved, inverse_ref[...])


def back_three_kernel(
    place_ref,
    acc_ref,
    inverse_ref,
    p0,
    p1,
    p2,
    p3,
    weight_ref,
    x_ref,
    acc_out_ref,
    part_ref,
):
    x = add_refs([p0, p1, p2, p3])
    acc = acc_ref[...] - complex_dot(x, weight_ref[...])
    x_ref[...] = x
    acc_out_ref[...] = acc
    part_ref[...] = complex_dot(acc, inverse_ref[...])


def back_two_kernel(
    place_ref,
    acc_ref,
    inverse_ref,
    p0,
    p1,
    p2,
    p3,
    x3_ref,
    weight2_ref,
    weight3_ref,
    both_ref,
    acc_out_ref,
    part_ref,
):
    x = add_refs([p0, p1, p2, p3])
    acc = (
        acc_ref[...]
        - complex_dot(x3_ref[...], weight3_ref[...])
        - complex_dot(x, weight2_ref[...])
    )
    both_ref[0] = x
    both_ref[1] = x3_ref[...]
    acc_out_ref[...] = acc
    part_ref[...] = complex_dot(acc, inverse_ref[...])


def back_one_kernel(
    place_ref,
    acc_ref,
    inverse_ref,
    p0,
    p1,
    p2,
    p3,
    later_ref,
    x2_ref,
    x3_ref,
    weight1_ref,
    weight2_ref,
    weight3_ref,
    newest_ref,
    both_ref,
    part_ref,
):
    x = add_refs([p0, p1, p2, p3])
    acc = (
        acc_ref[...]
        - complex_dot(later_ref[1], weight3_ref[...])
        - complex_dot(later_ref[0], weight2_ref[...])
        - complex_dot(x, weight1_ref[...])
    )
    part_ref[...] = complex_dot(acc, inverse_ref[...])
    newest_ref[...] = x + x2_ref[0] + x3_ref[...]
    both_ref[0] = x
    both_ref[1] = later_ref[0]


def coupled(rhs, link_real, link_imag, x):
    real = rhs[:CHUNK] - (link_real * x[:CHUNK] - link_imag * x[CHUNK:])
    imag = rhs[CHUNK:] - (link_real * x[CHUNK:] + link_imag * x[:CHUNK])
    return jnp.concatenate([real, imag], axis=0)


def second_block(rhs_ref, link_ref, x):
    return coupled(
        rhs_ref[:, 0:BLOCK], link_ref[0:1, 0:BLOCK], link_ref[8:9, 0:BLOCK], x
    )


def second_slab(rhs_ref, link_ref, x, q):
    own = x[:, 0:SLAB]
    for s in range(1, GROUP):
        own = jnp.where(q == s, x[:, SLAB * s : SLAB * s + SLAB], own)
    end = BLOCK + SLAB
    return coupled(
        rhs_ref[:, BLOCK:end], link_ref[0:1, BLOCK:end], link_ref[8:9, BLOCK:end], own
    )


def couple_kernel(
    place_ref, rhs_ref, link_ref, p0, p1, p2, p3, own_ref, zero_ref, weight_ref, pass_ref, out_ref
):
    x0 = add_refs([p0, p1, p2, p3])
    slab = second_slab(rhs_ref, link_ref, own_ref[...], place_ref[1])
    out_ref[...] = slab - complex_dot(
        second_block(rhs_ref, link_ref, x0), weight_ref[...]
    )
    zero = place_ref[0] == 0
    pass_ref[0] = jnp.where(zero, zero_ref[0], x0)
    pass_ref[1] = jnp.where(zero, zero_ref[1], own_ref[...])


def second_one_kernel(
    place_ref,
    rhs_ref,
    link_ref,
    acc_ref,
    own_ref,
    sent_ref,
    got_ref,
    f0,
    f1,
    f2,
    f3,
    weight0_ref,
    weight1_ref,
    out_ref,
    keep_ref,
):
    plane, q = place_ref[0], place_ref[1]
    x0 = jnp.where(plane == 1, sent_ref[0], got_ref[0])
    for s in range(GROUP):
        keep_ref[GROUP + s] = x0[:, SLAB * s : SLAB * s + SLAB]
    slab = second_slab(rhs_ref, link_ref, own_ref[...], q)
    product = complex_dot(second_block(rhs_ref, link_ref, x0), weight0_ref[...])
    slabs = [f0[...], f1[...], f2[...], f3[...]]
    solved = slab - product - slabs_dot(slabs, weight1_ref, q, keep_ref)
    out_ref[...] = jnp.where(plane == 1, acc_ref[...], solved)


def joined(ref, first):
    return jnp.concatenate([ref[first + s] for s in range(GROUP)], axis=1)


def second_base_kernel(
    place_ref, rhs_ref, link_ref, acc_ref, got_ref, own_ref, weight_ref, out_ref
):
    plane, q = place_ref[0], place_ref[1]
    x0 = joined(got_ref, GROUP)
    own = jnp.where(plane == 0, x0, own_ref[...])
    slab = second_slab(rhs_ref, link_ref, own, q)
    product = complex_dot(second_block(rhs_ref, link_ref, x0), weight_ref[...])
    out_ref[...] = jnp.where(
        plane == 0, slab, jnp.where(plane == 3, slab - product, acc_ref[...])
    )


def cells_kernel(
    where_ref, got_ref, pass_ref, passed_ref, newest_ref, own_ref, both_zero, later_ref, x3_one, out_ref, front_ref, rows_ref
):
    plane = where_ref[SLAB]

    def pick(*by_plane):
        value = by_plane[0]
        for at in range(1, GROUP):
            value = jnp.where(plane == at, by_plane[at], value)
        return value

    last = joined(got_ref, GROUP)
    blocks = (
        pick(last, pass_ref[0], passed_ref[0], last),
        pick(newest_ref[...], own_ref[...], passed_ref[1], passed_ref[0]),
        pick(both_zero[1], newest_ref[...], own_ref[...], passed_ref[1]),
        pick(later_ref[1], x3_one[...], newest_ref[...], own_ref[...]),
    )
    for k, x in enumerate(blocks):
        for part in range(6):
            at = BLOCK * k + 128 * part
            piece = x[:, 128 * part : 128 * part + 128]
            wide = jnp.concatenate([piece, jnp.zeros((128 - ROWS, 128), f32)], axis=0)
            front_ref[at : at + 128, :] = wide.T
    rows_ref[...] = jnp.zeros_like(rows_ref)
    for c in range(8):
        for u in range(CELLS):
            rows_ref[64 + u : 65 + u, :] = front_ref[pl.ds(where_ref[CELLS * c + u], 1), :]
        out_ref[c] = rows_ref[...].T[:ROWS]


def second_two_kernel(
    place_ref, acc_ref, cells_ref, sent_ref, f0, f1, f2, f3, weight1_ref, weight2_ref, out_ref
):
    slabs = [f0[...], f1[...], f2[...], f3[...]]
    solved = (
        acc_ref[...]
        - sent_dot(sent_ref, weight1_ref)
        - slabs_dot(slabs, weight2_ref, place_ref[1])
    )
    lane = lax.broadcasted_iota(jnp.int32, (ROWS, 128), 1)
    tail = jnp.concatenate([solved[:, 128:], jnp.zeros((ROWS, 64), f32)], axis=1)
    for c in range(8):
        out_ref[c, :, 0:128] = solved[:, 0:128]
        out_ref[c, :, 128:256] = jnp.where(lane < 64, tail, cells_ref[c])


def out_kernel(place_ref, got_ref, solution_ref, forward_ref):
    for part in range(2):
        wide = got_ref[:, CHUNK * part : CHUNK * part + CHUNK, :].reshape(128, 256)
        forward_ref[part, 0:128, :] = wide[:, 0:128].T
        turned = wide[:, 128:256].T
        forward_ref[part, 128:SLAB, :] = turned[0:64]
        for y in range(4):
            solution_ref[part, y] = turned[64 + 6 * y : 70 + 6 * y]


def plane_send(value, *moves, turn=0):
    pairs = [
        (GROUP * source + q, GROUP * target + (q + turn) % GROUP)
        for source, target in moves
        for q in range(GROUP)
    ]
    return lax.ppermute(value, "row", pairs)


def plane_spread(value, source, target):
    sent = {d: plane_send(value, (source, target), turn=d) for d in (2, 1, 3, 0)}
    return [sent[d] for d in range(GROUP)]


def after(value, arrived):
    return lax.optimization_barrier((value, arrived))[0]


def on_device(source1, source2, coupling, factor1, factor2, diag_inv, front_order):
    row_id = lax.axis_index("row")
    col_id = lax.axis_index("col")
    place = jnp.stack([row_id // GROUP, row_id % GROUP]).astype(jnp.int32)

    def gather_blocks(turned):
        return lax.all_gather(turned, "col").reshape(8, GROUP - 1, PIECE, 2 * SLAB)

    (turned1,) = call(
        turn_first_kernel,
        [SDS((3 * PIECE, 2 * SLAB), f32)],
        place,
        [],
        [(factor1, factor1.shape, lambda i, place: (0, 0, 0))],
        [pltpu.VMEM((4 * PIECE, 2 * SLAB), f32)],
    )
    matrix1 = gather_blocks(turned1)

    links = jnp.pad(coupling.reshape(2, CELLS), ((0, 0), (0, 32 - CELLS))).reshape(1, 64)
    links = jnp.pad(links, ((0, 0), (0, 64)))
    (packed,) = call(
        pack_kernel, [SDS((8, 16, 128), f32)], place, [source1, source2, links]
    )
    factor2 = after(factor2, packed)
    turned2 = factor2[:, :, : 3 * PIECE].reshape(2 * SLAB, 3 * PIECE).T
    packed = lax.all_to_all(packed, "col", 0, 0)
    early = jnp.broadcast_to(packed[:, :8].reshape(1, 64, 128), (16, 64, 128))
    early = lax.all_to_all(early, "row", 0, 0).reshape(1024, 128)
    late = packed[:, 8:].reshape(64, 128)
    late = jnp.broadcast_to(late[:, None], (64, LATE, 128)).reshape(64, LATE * 128)

    cell_y = front_order // 48
    cell_x = front_order % 48
    group_of = (cell_y // 4) * 64 + (cell_x // 6) * 8
    quarter = cell_y % 4
    inner = quarter * 6 + cell_x % 6
    every = jnp.stack([group_of + cell_x % 6, group_of + 6, quarter, inner])
    own = lax.dynamic_slice_in_dim(every, row_id * SLAB, SLAB, 1)
    every = jnp.concatenate([every[:, :BLOCK], own, jnp.zeros((4, 64), jnp.int32)], axis=1)
    where, mark = every[:2].reshape(2048), every[2:].astype(f32)
    rows_shape = SDS((ROWS, 1024), f32)
    rows_scratch = [pltpu.VMEM((1024, 128), f32)]
    (rhs,) = call(first_front_kernel, [rows_shape], where, [early, mark], scratch=rows_scratch)

    slab_shape = SDS((ROWS, SLAB), f32)
    block_shape = SDS((ROWS, BLOCK), f32)
    pair_shape = SDS((2, ROWS, BLOCK), f32)
    sent_shape = SDS((GROUP, ROWS, SLAB), f32)

    def load(matrix, numbers, arrived, second=False):
        matrix = after(matrix, arrived)
        blocks = [
            (
                matrix,
                (8, 1, PIECE, 2 * SLAB),
                (lambda i, place, n=number: (0, n, 0, 0))
                if second
                else (lambda i, place, n=number: (0, slot_of(place[0], n), 0, 0)),
            )
            for number in numbers
        ]
        shapes = [SDS((BLOCK, 2 * SLAB), f32)] * len(numbers)
        return call(load_kernel, shapes, place, [], blocks)

    first = [
        (matrix1, (8, 1, PIECE, 2 * SLAB), lambda i, place: (0, slot_of(place[0], 0), 0, 0))
    ]
    (acc,) = call(start_kernel, [slab_shape], place, [rhs], first)
    got = plane_spread(acc, 1, 2)
    late, turned2, diag_inv = after((late, turned2, diag_inv), acc)
    late = lax.all_gather(late, "row")
    matrix2 = gather_blocks(turned2)
    weights = load(matrix1, [1], acc)
    inverse = diag_inv.reshape(2 * BLOCK, SLAB).T
    acc, kept = call(
        forward_one_kernel, [slab_shape, sent_shape], place, [acc, *got, *weights]
    )
    sent = plane_send(kept, (2, 3))
    got = plane_spread(acc, 2, 3)
    weights = [*weights, *load(matrix1, [2], acc)]
    acc, part = call(
        forward_two_kernel,
        [slab_shape, block_shape],
        place,
        [acc, inverse, sent, *got, *weights],
    )
    got = plane_spread(part, 3, 2)
    block2 = weights[1]
    weights = load(matrix1, [3], part)
    x3_two, acc, part = call(
        back_three_kernel,
        [block_shape, slab_shape, block_shape],
        place,
        [acc, inverse, *got, *weights],
    )
    x3_one = plane_send(x3_two, (2, 1))
    got = plane_spread(part, 2, 1)
    weights = [block2, *weights]
    both_one, acc, part = call(
        back_two_kernel,
        [pair_shape, slab_shape, block_shape],
        place,
        [acc, inverse, *got, x3_one, *weights],
    )
    later = plane_send(both_one, (1, 0))
    got = plane_spread(part, 1, 0)
    weights = [*load(matrix1, [1], part), *weights]
    newest, both_zero, part = call(
        back_one_kernel,
        [block_shape, pair_shape, block_shape],
        place,
        [acc, inverse, *got, later, both_one, x3_two, *weights],
    )
    own = plane_send(newest, (0, 1), (1, 2), (2, 3))
    got = plane_spread(part, 0, 1)
    late = after(late, part)
    rhs, link = call(
        second_front_kernel,
        [rows_shape, SDS((16, 1024), f32)],
        where,
        [mark],
        [(late, (16, 64, 128), lambda i, place: (0, 0, 0))],
        scratch=rows_scratch * 2,
    )
    weights = load(matrix2, [0], part, True)
    passing, acc = call(
        couple_kernel,
        [pair_shape, slab_shape],
        place,
        [rhs, link, *got, own, both_zero, *weights],
    )
    passed = plane_send(passing, (1, 2), (0, 3))
    got = plane_spread(acc, 1, 2)
    weights = [*weights, *load(matrix2, [1, 2], acc, True)]
    acc, kept = call(
        second_one_kernel,
        [slab_shape, SDS((2 * GROUP, ROWS, SLAB), f32)],
        place,
        [rhs, link, acc, own, passing, passed, *got, *weights[:2]],
    )
    sent = plane_send(kept, (2, 3), (1, 0))
    got = plane_spread(acc, 2, 3)
    (acc,) = call(
        second_base_kernel,
        [slab_shape],
        place,
        [rhs, link, acc, sent, own, weights[0]],
    )

    at = jnp.arange(SLAB, dtype=jnp.int32)
    own_c, own_y, own_x = at // CELLS, at % CELLS // 6, at % 6
    own_cells = (row_id * 4 + own_y) * 48 + own_c * 6 + own_x
    hits = front_order[None, :] == own_cells[:, None]
    slots = jnp.sum(jnp.where(hits, jnp.arange(4 * BLOCK, dtype=jnp.int32)[None, :], 0), axis=1)
    (mine,) = call(
        cells_kernel,
        [SDS((8, ROWS, 128), f32)],
        jnp.concatenate([slots, place]),
        [sent, passing, passed, newest, own, both_zero, later, x3_one],
        scratch=[pltpu.VMEM((4 * BLOCK, 128), f32), pltpu.VMEM((128, 128), f32)],
    )
    (last,) = call(
        second_two_kernel,
        [SDS((8, ROWS, 256), f32)],
        place,
        [acc, mine, sent, *got, *weights[1:]],
    )
    arrived = lax.all_to_all(last, "col", 0, 0)
    return call(
        out_kernel,
        [SDS((2, 4, 6, 128), f32), SDS((2, SLAB, 128), f32)],
        place,
        [arrived],
        last=True,
    )


def solution(mesh):
    in_specs = (
        P(None, "row", "col", None),
        P(None, "row", "col", None),
        P(None, "row", "col"),
        P(None, "row", "col"),
        P(None, "row", "col"),
        P(None, None, "row"),
        P(),
    )
    out_specs = (P(None, "row", "col", None), P(None, "row", None))
    return jax.shard_map(
        on_device, mesh=mesh, in_specs=in_specs, out_specs=out_specs, check_vma=False
    )
```
